128 devices in a mesh: dp: 32 (over y, x, core), seq: 4 (over z).
Axes of the slice: x: 4, y: 4, z: 4, core: 2. Of those that a mesh axis runs over, the one named last changes fastest.
Arguments:
- enc_patches: bfloat16 [64, 1024, 512], P('dp', 'seq'), may hold values from -6 to 6
- enc_latents: bfloat16 [64, 128, 512], P('dp'), may hold values from -6 to 6
- resolution: int32 [64], P('dp'), may hold values from 128 to 512, as said below
- lengths: int32 [64], P('dp'), may hold values from 32 to 1024, as said below
- codes: int32 [64, 128], P('dp'), may hold values from 0 to 4095
- enc_qkv: bfloat16 [512, 1536], replicated, may hold values from -0.25 to 0.25
- enc_out: bfloat16 [512, 512], replicated, may hold values from -1 to 1
- enc_mlp_in: bfloat16 [512, 2048], replicated, may hold values from -0.25 to 0.25
- enc_mlp_out: bfloat16 [2048, 512], replicated, may hold values from -0.125 to 0.125
- enc_gains: bfloat16 [3, 512], replicated, may hold values from 0.5 to 1.5
- enc_biases: bfloat16 [6, 512], replicated, may hold values from -1.5 to 1.5
- enc_query_bias: bfloat16 [512], replicated, may hold values from -1.5 to 1.5
- enc_hidden_bias: bfloat16 [2048], replicated, may hold values from -1.5 to 1.5
- latent_proj: bfloat16 [12, 512], replicated, may hold values from -0.25 to 0.25
- latent_bias: bfloat16 [12], replicated, may hold values from -2 to 2
- codebook: bfloat16 [12, 4096], replicated, may hold values from -5 to 5
- latent_embed: bfloat16 [12, 512], replicated, may hold values from -1.75 to 1.75
- pos_table: bfloat16 [1024, 512], replicated, may hold values from -5 to 5
- dec_qkv: bfloat16 [512, 1536], replicated, may hold values from -0.25 to 0.25
- dec_out: bfloat16 [512, 512], replicated, may hold values from -1 to 1
- dec_mlp_in: bfloat16 [512, 2048], replicated, may hold values from -0.25 to 0.25
- dec_mlp_out: bfloat16 [2048, 512], replicated, may hold values from -0.125 to 0.125
- dec_gains: bfloat16 [2, 512], replicated, may hold values from 0.5 to 1.5
- dec_biases: bfloat16 [8, 512], replicated, may hold values from -1.5 to 1.5
- dec_hidden_bias: bfloat16 [2048], replicated, may hold values from -1.5 to 1.5
- out_cot: bfloat16 [64, 1024, 512], P('dp', 'seq'), may hold values from -6 to 6
Outputs:
- dec_result: bfloat16 [64, 1024, 512], P('dp', 'seq')
- grad_patches: float32 [64, 1024, 512], P('dp', 'seq')
- grad_latents: float32 [64, 128, 512], P('dp')
- quant_loss: float32 [], replicated
- grad_enc_qkv: float32 [512, 1536], replicated
- grad_enc_out: float32 [512, 512], replicated
- grad_enc_mlp_in: float32 [512, 2048], replicated
- grad_enc_mlp_out: float32 [2048, 512], replicated
- grad_enc_gains: float32 [3, 512], replicated
- grad_enc_biases: float32 [6, 512], replicated
- grad_enc_query_bias: float32 [512], replicated
- grad_enc_hidden_bias: float32 [2048], replicated
- grad_latent_proj: float32 [12, 512], replicated
- grad_latent_bias: float32 [12], replicated
- grad_codebook: float32 [12, 4096], replicated
- grad_latent_embed: float32 [12, 512], replicated
- grad_pos_table: float32 [1024, 512], replicated
- grad_dec_qkv: float32 [512, 1536], replicated
- grad_dec_out: float32 [512, 512], replicated
- grad_dec_mlp_in: float32 [512, 2048], replicated
- grad_dec_mlp_out: float32 [2048, 512], replicated
- grad_dec_gains: float32 [2, 512], replicated
- grad_dec_biases: float32 [8, 512], replicated
- grad_dec_hidden_bias: float32 [2048], replicated
The draws below stay inside these ranges and needn't reach their ends.
Inputs may be any that keep to these rules, and one draw needn't show every extreme that they name: `resolution`: Each value is 128, 256 or 512; among the 2 images of each index of dp at least one has resolution 512. `lengths`: A whole number of patch rows: a multiple of resolution // 16, at least half and at most all of the patches of its image; in each index of dp one image of resolution 512 has more than 7 / 8 of its slots valid, and some image has all its slots valid.
All inputs are finite; a program needn't handle non-finite values.
Results may differ from the reference program's by a relative error of at most 0.02.
Values may be sent and summed in bfloat16 or wider, within the bound.
No kernel may reach another device: no remote copies, remote signals or barrier semaphores. Data moves between devices by JAX's collectives and lax.ppermute only.
A program may use at most 256 MiB of HBM per device.

```python
import jax
import jax.numpy as jnp
from jax import lax

D = 512
HEADS = 8
HD = 64
FF = 2048
LATD = 12
CODES = 4096
LAT = 128
GRID = 32
IMGS = 2
IMAGES = 64
MAXP = 1024


def image_plan(key):
    groups = IMAGES // IMGS
    picked = jax.random.randint(jax.random.fold_in(key, 11), (IMAGES,), 0, 3)
    anchor = jax.random.randint(jax.random.fold_in(key, 12), (groups,), 0, IMGS)
    slot_index = jnp.arange(IMAGES, dtype=jnp.int32)
    is_anchor = slot_index % IMGS == jnp.repeat(anchor, IMGS)
    picked = jnp.where(is_anchor, 2, picked)
    image_res = jnp.where(picked == 0, 128, jnp.where(picked == 1, 256, 512)).astype(jnp.int32)
    grid_side = image_res // (512 // GRID)
    least_rows = jnp.where(is_anchor, grid_side - grid_side // 8 + 1, grid_side // 2)
    least_rows = jnp.minimum(least_rows, grid_side)
    extra_rows = jax.random.randint(jax.random.fold_in(key, 13), (IMAGES,), 0, grid_side - least_rows + 1)
    row_count = least_rows + extra_rows
    row_count = jnp.where(slot_index == anchor[0], grid_side, row_count)
    return (image_res, (grid_side * row_count).astype(jnp.int32))


def draw_resolution(key, part):
    return image_plan(key)[0]


def draw_lengths(key, part):
    return image_plan(key)[1]


def touch_ends(entries, rng, least, largest):
    index_at = [jax.random.randint(jax.random.fold_in(rng, axis), (), 0, length) for axis, length in enumerate(entries.shape)]
    main_axis = entries.shape.index(max(entries.shape))
    neighbour = index_at[:main_axis] + [(index_at[main_axis] + 1) % entries.shape[main_axis]] + index_at[main_axis + 1:]
    return entries.at[tuple(index_at)].set(least).at[tuple(neighbour)].set(largest)


def steps_of(own_key, dims, pieces, least, high):
    def one(position, blocks):
        heights = jax.random.uniform(jax.random.fold_in(jax.random.fold_in(own_key, 6), position), (blocks,), jnp.float32, least / len(pieces), high / len(pieces))
        return jnp.repeat(jnp.exp(heights), dims[position] // blocks).reshape((-1,) + (1,) * (len(dims) - position - 1))

    gain = one(*pieces[0])
    for cut in pieces[1:]:
        gain = gain * one(*cut)
    return gain


def normal_values(own_key, dims, deviation, bound, shards=(), kind=jnp.bfloat16):
    array = deviation * jax.random.normal(own_key, dims, jnp.float32)
    if shards:
        array = array * steps_of(own_key, dims, shards, -0.22, 0.18)
    return jnp.clip(array, -bound, bound).astype(kind)


def setup_inputs(seed: int = 0) -> dict:
    arg_keys = jax.random.split(jax.random.key(seed), 27)
    return {
        "enc_patches": normal_values(arg_keys[0], (IMAGES, MAXP, D), 1.0, 6.0, ((0, 32), (1, 4))),
        "enc_latents": normal_values(arg_keys[1], (IMAGES, LAT, D), 1.0, 6.0, ((0, 32),)),
        "resolution": draw_resolution(jax.random.fold_in(arg_keys[26], 71), 0),
        "lengths": draw_lengths(jax.random.fold_in(arg_keys[26], 71), 0),
        "codes": touch_ends(jax.random.randint(arg_keys[4], (IMAGES, LAT), 0, CODES), jax.random.fold_in(arg_keys[4], 1), 0, CODES - 1).astype(jnp.int32),
        "enc_qkv": normal_values(arg_keys[5], (D, 3 * D), D ** -0.5, 0.25),
        "enc_out": normal_values(arg_keys[6], (D, D), (D // 16) ** -0.5, 1.0),
        "enc_mlp_in": normal_values(arg_keys[7], (D, FF), D ** -0.5, 0.25),
        "enc_mlp_out": normal_values(arg_keys[8], (FF, D), FF ** -0.5, 0.125),
        "enc_gains": jnp.clip(1.0 + 0.1 * jax.random.normal(arg_keys[9], (3, D), jnp.float32), 0.5, 1.5).astype(jnp.bfloat16),
        "enc_biases": normal_values(arg_keys[10], (6, D), 0.3, 1.5),
        "enc_query_bias": normal_values(arg_keys[11], (D,), 0.3, 1.5),
        "enc_hidden_bias": normal_values(arg_keys[12], (FF,), 0.3, 1.5),
        "latent_proj": normal_values(arg_keys[13], (LATD, D), D ** -0.5, 0.25),
        "latent_bias": normal_values(arg_keys[14], (LATD,), 0.5, 2.0),
        "codebook": normal_values(arg_keys[15], (LATD, CODES), 1.0, 5.0),
        "latent_embed": normal_values(arg_keys[16], (LATD, D), LATD ** -0.5, 1.75),
        "pos_table": normal_values(arg_keys[17], (MAXP, D), 1.0, 5.0),
        "dec_qkv": normal_values(arg_keys[18], (D, 3 * D), D ** -0.5, 0.25),
        "dec_out": normal_values(arg_keys[19], (D, D), (D // 16) ** -0.5, 1.0),
        "dec_mlp_in": normal_values(arg_keys[20], (D, FF), D ** -0.5, 0.25),
        "dec_mlp_out": normal_values(arg_keys[21], (FF, D), FF ** -0.5, 0.125),
        "dec_gains": jnp.clip(1.0 + 0.1 * jax.random.normal(arg_keys[22], (2, D), jnp.float32), 0.5, 1.5).astype(jnp.bfloat16),
        "dec_biases": normal_values(arg_keys[23], (8, D), 0.3, 1.5),
        "dec_hidden_bias": normal_values(arg_keys[24], (FF,), 0.3, 1.5),
        "out_cot": normal_values(arg_keys[25], (IMAGES, MAXP, D), 1.0, 6.0, ((0, 32), (1, 4))),
    }


@jax.custom_vjp
def low(v):
    return lax.optimization_barrier(v.astype(jnp.bfloat16)).astype(jnp.float32)

@jax.custom_vjp
def low_back(v):
    return v

def low_keep(v):
    return (low(v), None)

def low_pass(kept, grad):
    return (grad,)

def back_keep(v):
    return (v, None)

def back_low(kept, grad):
    return (low(grad),)
low.defvjp(low_keep, low_pass)
low_back.defvjp(back_keep, back_low)
eps_norm = 1e-06
beta_commit = 0.25

def matmul(left, right):
    return jnp.matmul(left, right, precision=lax.Precision.HIGHEST)

def layer_norm(values, norm_gain, norm_offset):
    centre = values - lax.optimization_barrier(jnp.mean(values, -1, keepdims=True))
    spread = lax.optimization_barrier(jnp.mean(centre * centre, -1, keepdims=True))
    return centre * lax.rsqrt(spread + eps_norm) * norm_gain + norm_offset

def rounded(values):
    return low(low_back(values))

def attend(queries, key_rows, value_rows, key_valid):
    query_count = queries.shape[0]
    key_count = key_rows.shape[0]
    query_heads = queries.reshape(query_count, HEADS, HD)
    key_heads = key_rows.reshape(key_count, HEADS, HD)
    value_heads = value_rows.reshape(key_count, HEADS, HD)
    scores = jnp.einsum('qhd,khd->hqk', query_heads, key_heads, precision=lax.Precision.HIGHEST) * HD ** (-0.5)
    scores = jnp.where(key_valid[None, None, :], scores, -1e+30)
    scores = low_back(scores)
    shifted = scores - lax.optimization_barrier(jnp.max(scores, -1, keepdims=True))
    expo = jnp.exp(shifted)
    probs = low(expo / lax.optimization_barrier(jnp.sum(expo, -1, keepdims=True)))
    mixed = jnp.einsum('hqk,khd->qhd', probs, value_heads, precision=lax.Precision.HIGHEST)
    return rounded(mixed.reshape(query_count, HEADS * HD))

def feed_forward(resid, norm_gain, norm_offset, weight_in, bias_in, weight_out, bias_out):
    normed = low(layer_norm(resid, norm_gain, norm_offset))
    pre_act = low_back(matmul(normed, weight_in) + bias_in)
    activ = low(jax.nn.gelu(pre_act, approximate=False))
    return resid + low_back(matmul(activ, weight_out) + bias_out)

def image_forward(params, patch_rows, latent_rows, frozen_latent, patch_valid, code_row, pos_index, frozen_code):
    enc_qkv, enc_out, enc_mlp_in, enc_mlp_out, enc_gains, enc_biases, enc_query_bias, enc_hidden_bias, latent_proj, latent_bias, codebook, latent_embed, pos_table, dec_qkv, dec_out, dec_mlp_in, dec_mlp_out, dec_gains, dec_biases, dec_hidden_bias = params
    zero_row = jnp.zeros((D,), patch_rows.dtype)
    key_valid = jnp.concatenate([patch_valid, jnp.ones((LAT,), jnp.bool_)])
    norm_patch = low(layer_norm(patch_rows, enc_gains[0], enc_biases[0]))
    norm_latent = low(layer_norm(latent_rows, enc_gains[0], enc_biases[0]))
    patch_kv = matmul(norm_patch, enc_qkv[:, D:]) + jnp.concatenate([zero_row, enc_biases[1]])
    latent_qkv = matmul(norm_latent, enc_qkv) + jnp.concatenate([enc_query_bias, zero_row, enc_biases[1]])
    all_kv = rounded(jnp.concatenate([patch_kv, latent_qkv[:, D:]], 0))
    latent_query = rounded(latent_qkv[:, :D])
    enc_attn = attend(latent_query, all_kv[:, :D], all_kv[:, D:], key_valid)
    enc_mid = latent_rows + low_back(matmul(enc_attn, enc_out) + enc_biases[2])
    enc_final = feed_forward(enc_mid, enc_gains[1], enc_biases[3], enc_mlp_in, enc_hidden_bias, enc_mlp_out, enc_biases[4])
    post_norm = low(layer_norm(enc_final, enc_gains[2], enc_biases[5]))
    latent_code = low_back(matmul(post_norm, latent_proj.T) + latent_bias)
    quant = codebook[:, code_row].T
    passed = frozen_code + latent_code - frozen_latent
    code_gap = frozen_latent - quant
    commit_gap = latent_code - frozen_code
    vq_term = jnp.sum(code_gap * code_gap) + beta_commit * jnp.sum(commit_gap * commit_gap)
    embed_in = low_back(matmul(low(passed), latent_embed) + dec_biases[6])
    dec_in = dec_biases[7] + pos_table[pos_index]
    dec_norm_patch = low(layer_norm(dec_in, dec_gains[0], dec_biases[0]))
    dec_norm_latent = low(layer_norm(embed_in, dec_gains[0], dec_biases[0]))
    patch_qkv = rounded(matmul(dec_norm_patch, dec_qkv) + jnp.concatenate([dec_biases[1], zero_row, dec_biases[2]]))
    latent_kv = rounded(matmul(dec_norm_latent, dec_qkv[:, D:]) + jnp.concatenate([zero_row, dec_biases[2]]))
    dec_keys = jnp.concatenate([patch_qkv[:, D:], latent_kv], 0)
    dec_attn = attend(patch_qkv[:, :D], dec_keys[:, :D], dec_keys[:, D:], key_valid)
    dec_mid = dec_in + low_back(matmul(dec_attn, dec_out) + dec_biases[3])
    dec_final = feed_forward(dec_mid, dec_gains[1], dec_biases[4], dec_mlp_in, dec_hidden_bias, dec_mlp_out, dec_biases[5])
    return (dec_final * patch_valid[:, None], vq_term, latent_code)

def reference(enc_patches, enc_latents, resolution, lengths, codes, enc_qkv, enc_out, enc_mlp_in, enc_mlp_out, enc_gains, enc_biases, enc_query_bias, enc_hidden_bias, latent_proj, latent_bias, codebook, latent_embed, pos_table, dec_qkv, dec_out, dec_mlp_in, dec_mlp_out, dec_gains, dec_biases, dec_hidden_bias, out_cot):
    params = tuple((weight.astype(jnp.float32) for weight in (enc_qkv, enc_out, enc_mlp_in, enc_mlp_out, enc_gains, enc_biases, enc_query_bias, enc_hidden_bias, latent_proj, latent_bias, codebook, latent_embed, pos_table, dec_qkv, dec_out, dec_mlp_in, dec_mlp_out, dec_gains, dec_biases, dec_hidden_bias)))
    slot_index = jnp.arange(GRID * GRID, dtype=jnp.int32)

    def one_image(carry, item):
        grad_total, loss_total = carry
        patch_rows, latent_rows, image_res, image_len, code_row, cotangent = item
        grid_side = image_res // (512 // GRID)
        row_index = jnp.minimum(slot_index // grid_side, grid_side - 1)
        col_index = slot_index % grid_side
        pos_index = (row_index * GRID // grid_side * GRID + col_index * GRID // grid_side).astype(jnp.int32)
        patch_valid = slot_index < image_len
        frozen_code = params[10][:, code_row].T
        zero_code = jnp.zeros((LAT, LATD), jnp.float32)

        def forward(weights, patch_in, latent_in, frozen_latent):
            dec_rows, vq_term, latent_code = image_forward(weights, patch_in, latent_in, frozen_latent, patch_valid, code_row, pos_index, frozen_code)
            return ((dec_rows, vq_term), latent_code)
        latent_value = forward(params, patch_rows, latent_rows, zero_code)[1]
        primal, pullback, unused_aux = jax.vjp(lambda weights, patch_in, latent_in: forward(weights, patch_in, latent_in, latent_value), params, patch_rows, latent_rows, has_aux=True)
        grad_params, grad_patch, grad_latent = pullback((cotangent, jnp.ones((), jnp.float32)))
        grad_total = jax.tree.map(lambda left, right: left + right, grad_total, grad_params)
        return ((grad_total, loss_total + primal[1]), (primal[0].astype(jnp.bfloat16), grad_patch, grad_latent))
    start_grads = jax.tree.map(jnp.zeros_like, params)
    items = (enc_patches.astype(jnp.float32), enc_latents.astype(jnp.float32), resolution, lengths, codes, out_cot.astype(jnp.float32))
    final_carry, stacked = lax.scan(one_image, (start_grads, jnp.zeros((), jnp.float32)), items)
    grad_total, loss_total = final_carry
    dec_result, grad_patches, grad_latents = stacked
    quant_loss = loss_total / (IMAGES * LAT * LATD)
    return (dec_result, grad_patches, grad_latents, quant_loss) + tuple(grad_total)
```

```python
import functools

import jax
import jax.numpy as jnp
from jax import lax
from jax.experimental import pallas as pl
from jax.experimental.pallas import tpu as pltpu
from jax.sharding import Mesh
from jax.sharding import PartitionSpec as P

F32 = jnp.float32
BF16 = jnp.bfloat16
EPS = 1e-06
COMMIT = 0.25
NEG = -1e30
D = 512
HEADS = 8
HD = 64
FF = 2048
GROUP = 4
GW = GROUP * HD
LAT = 128
IMGS = 2
SLOTS = 256
ROWS = IMGS * SLOTS
LROWS = IMGS * LAT
TABLE = 1024
KEYS = TABLE + LAT
OWN_KEYS = SLOTS + LAT
PIECES = 128
SHARE = 0.25
SMALL = 192
CODE_ROW = 64

NN = (((1,), (0,)), ((), ()))
NT = (((1,), (1,)), ((), ()))
TN = (((0,), (0,)), ((), ()))
VMEM_LIMIT = 60 * 1024 * 1024


def dot(left, right, dims=NN):
    return lax.dot_general(left, right, dims, preferred_element_type=F32)


def row_of(ref, index):
    return ref[index : index + 1, :].astype(F32)


def norm_parts(values):
    centre = values - jnp.mean(values, -1, keepdims=True)
    scale = lax.rsqrt(jnp.mean(centre * centre, -1, keepdims=True) + EPS)
    return centre * scale, scale


def norm_rows(values, gain, offset):
    return norm_parts(values)[0] * gain + offset


def norm_back(values, gain, upstream):
    hat, scale = norm_parts(values)
    inner = upstream * gain
    low = jnp.mean(inner, -1, keepdims=True)
    along = jnp.mean(inner * hat, -1, keepdims=True)
    return scale * (inner - low - hat * along), upstream * hat


def fold(values):
    return jnp.sum(values.reshape(values.shape[0] // 8, 8, values.shape[1]), 0)


def col_sum(values):
    return jnp.sum(values, 0, keepdims=True)


def gelu_parts(point):
    size = jnp.abs(point) * 0.7071067811865476
    t = 1.0 / (1.0 + 0.3275911 * size)
    bell = jnp.exp(-0.5 * point * point)
    poly = t * (
        0.254829592
        + t * (-0.284496736 + t * (1.421413741 + t * (-1.453152027 + t * 1.061405429)))
    )
    tail = 0.5 * poly * bell
    cdf = jnp.where(point >= 0, 1.0 - tail, tail)
    return point * cdf, cdf + point * bell * 0.3989422804014327


def loop(count, body):
    def step(index, carry):
        body(index)
        return carry

    lax.fori_loop(0, count, step, 0)


def chunk(index, size):
    return pl.ds(pl.multiple_of(index * size, size), size)


def head_stack(block, rows):
    lane = lax.broadcasted_iota(jnp.int32, (rows, GW), 1) // HD
    parts = [jnp.where(lane == h, block, jnp.zeros_like(block)) for h in range(GROUP)]
    return jnp.concatenate(parts, 0)


def coords(info):
    return info[4], info[5], info[6], info[7]


def rel_piece(info, z, q):
    c0, y0, x0, z0 = coords(info)
    c, y, x = q // 16, (q // 4) % 4, q % 4
    rel_c = (c + c0) & 1
    rel_y = (y - y0) & 3
    rel_x = (x - x0) & 3
    plane = rel_y * 4 + rel_x
    if z is None:
        return rel_c * 16 + plane
    return (rel_c * 4 + ((z - z0) & 3)) * 16 + plane


def put_pieces(info, out, offset, z, block, rows, cols):
    for q in range(32):
        row = (q % 8) * rows
        rel = rel_piece(info, z, q)
        for b in range(cols // 128):
            col = (q // 8) * cols + b * 128
            at = offset + b * rows
            out[rel, at : at + rows, :] = block[row : row + rows, col : col + 128].astype(BF16)


def own_positions(info, image, iota):
    shift = info[2 + image]
    side = lax.shift_left(1, shift)
    slot = info[7] * SLOTS + iota
    row = jnp.minimum(lax.shift_right_logical(slot, shift), side - 1)
    col = slot & (side - 1)
    up = lax.shift_right_logical(row * 32, shift)
    across = lax.shift_right_logical(col * 32, shift)
    return up * 32 + across


def shifted(info, image):
    return info[2 + image]


def table_bias(info, image, shape):
    shift = info[2 + image]
    place = lax.broadcasted_iota(jnp.int32, shape, 0)
    gap = 5 - shift
    mask = lax.shift_left(1, gap) - 1
    row = lax.shift_right_logical(place, 5)
    col = place & 31
    slot = lax.shift_left(lax.shift_right_logical(row, gap), shift) + lax.shift_right_logical(
        col, gap
    )
    keep = jnp.logical_and(((row | col) & mask) == 0, slot < info[image])
    return jnp.where(keep, 0.0, NEG)


def code_onehot(codes_ref, entries):
    ids = codes_ref[...]
    lane = lax.broadcasted_iota(jnp.int32, (LROWS, entries), 1)
    return jnp.where(ids == lane, 1.0, 0.0).astype(BF16)


def enc_front(
    info, patches, latents, wqkv, gains, biases, qbias, codes, codebook,
    np_out, nl_out, kv_out, lqkv_out, part_out, quant_out,
    bias_ref, k_ref, vt_ref,
):
    gain, offset = row_of(gains, 0), row_of(biases, 0)
    vbias = row_of(biases, 1)

    def norm_patch(r):
        at = chunk(r, 64)
        np_out[at, :] = norm_rows(patches[at, :].astype(F32), gain, offset).astype(BF16)

    loop(ROWS // 64, norm_patch)

    def norm_lat(r):
        at = chunk(r, 64)
        nl_out[at, :] = norm_rows(latents[at, :].astype(F32), gain, offset).astype(BF16)

    loop(LROWS // 64, norm_lat)
    kv_out[:, :D] = dot(np_out[...], wqkv[:, D : 2 * D]).astype(BF16)
    kv_out[:, D:] = (dot(np_out[...], wqkv[:, 2 * D :]) + vbias).astype(BF16)
    lqkv_out[:, :D] = (dot(nl_out[...], wqkv[:, :D]) + qbias[...].astype(F32)).astype(BF16)
    lqkv_out[:, D : 2 * D] = dot(nl_out[...], wqkv[:, D : 2 * D]).astype(BF16)
    lqkv_out[:, 2 * D :] = (dot(nl_out[...], wqkv[:, 2 * D :]) + vbias).astype(BF16)
    quant_out[...] = dot(codebook[...], code_onehot(codes, codebook.shape[1]), NT).astype(BF16)
    enc_bias(info, bias_ref)
    part_out[D:, :] = jnp.zeros((32, LROWS), BF16)
    for image in range(IMGS):
        lat_at = slice(image * LAT, (image + 1) * LAT)
        lane_at = slice(image * LAT, (image + 1) * LAT)
        for g in range(2):
            cols = slice(g * GW, (g + 1) * GW)
            enc_keys(kv_out, lqkv_out, image, g, k_ref, None, vt_ref, None)
            query = lqkv_out[lat_at, cols] * jnp.asarray(0.125, BF16)
            scores = dot(k_ref[...], head_stack(query, LAT), NT)
            bias = bias_ref[image]
            scores = scores + jnp.concatenate([bias] * GROUP, 1)
            top = jnp.max(scores, 0, keepdims=True)
            expo = jnp.exp(scores - top)
            total = col_sum(expo)
            low = expo.astype(BF16)
            log_total = top + jnp.log(total)
            inverse = 1.0 / total
            for h in range(GROUP):
                head = slice(h * LAT, (h + 1) * LAT)
                mixed = dot(vt_ref[h * HD : (h + 1) * HD, :], low[:, head])
                at = g * GW + h * HD
                part_out[at : at + HD, lane_at] = (mixed * inverse[:, head]).astype(BF16)
            rows = jnp.concatenate(
                [log_total[:, h * LAT : (h + 1) * LAT] for h in range(GROUP)], 0
            )
            high = rows.astype(BF16)
            rest = rows - high.astype(F32)
            mid = rest.astype(BF16)
            last = (rest - mid.astype(F32)).astype(BF16)
            for n, piece in enumerate((high, mid, last)):
                at = D + 8 * n + 4 * g
                part_out[at : at + 4, lane_at] = piece


def enc_bias(info, bias_ref):
    place = lax.broadcasted_iota(jnp.int32, (SLOTS, LAT), 0) + info[7] * SLOTS
    token = lax.broadcasted_iota(jnp.int32, (LAT, LAT), 0) // 32
    lat = jnp.where(token == info[7], 0.0, NEG)
    for image in range(IMGS):
        bias_ref[image, :SLOTS, :] = jnp.where(place < info[image], 0.0, NEG)
        bias_ref[image, SLOTS:, :] = lat


def enc_keys(kv, lqkv, image, g, k_ref, v_ref, vt_ref, kt_ref):
    rows = slice(image * SLOTS, (image + 1) * SLOTS)
    lat_at = slice(image * LAT, (image + 1) * LAT)
    k_ref[:SLOTS, :] = kv[rows, g * GW : (g + 1) * GW]
    k_ref[SLOTS:, :] = lqkv[lat_at, D + g * GW : D + (g + 1) * GW]
    value = jnp.concatenate(
        [kv[rows, D + g * GW : D + (g + 1) * GW], lqkv[lat_at, 2 * D + g * GW : 2 * D + (g + 1) * GW]],
        0,
    )
    if v_ref is not None:
        v_ref[...] = value
    if vt_ref is not None:
        vt_ref[...] = value.T
    if kt_ref is not None:
        kt_ref[...] = k_ref[...].T


def dec_front(
    info, pos, quant, lemb, wqkv, wo, win, wout, gains, biases, hbias, cot,
    res_out, f_out, dmid_out, attn_out, e_out, inv_out, q_out, k_out, v_out, tn_out, xn_out,
    ln_out, x_out, sm_out,
    bias_ref, vt_ref, ot_ref, mid_ref, hn_ref, dy_ref, acc_ref, dhn_ref, act_ref, dpre_ref,
):
    gain0, off0 = row_of(gains, 0), row_of(biases, 0)
    gain1, off1 = row_of(gains, 1), row_of(biases, 4)
    qbias, vbias = row_of(biases, 1), row_of(biases, 2)
    token = row_of(biases, 7)

    def table_norm(r):
        at = chunk(r, 64)
        values = token + pos[at, :].astype(F32)
        tn_out[at, :] = norm_rows(values, gain0, off0).astype(BF16)

    loop(TABLE // 64, table_norm)

    def table_keys(r):
        at = chunk(r, 256)
        key = dot(tn_out[at, :], wqkv[:, D : 2 * D]).astype(BF16)
        value = (dot(tn_out[at, :], wqkv[:, 2 * D :]) + vbias).astype(BF16)
        for image in range(IMGS):
            k_out[image, at, :] = key
            v_out[image, at, :] = value

    loop(TABLE // 256, table_keys)
    embed = dot(quant[...], lemb[...], TN) + row_of(biases, 6)
    ln_out[...] = norm_rows(embed, gain0, off0).astype(BF16)
    lat_k = dot(ln_out[...], wqkv[:, D : 2 * D]).astype(BF16)
    lat_v = (dot(ln_out[...], wqkv[:, 2 * D :]) + vbias).astype(BF16)
    for image in range(IMGS):
        at = slice(image * LAT, (image + 1) * LAT)
        k_out[image, TABLE:, :] = lat_k[at, :]
        v_out[image, TABLE:, :] = lat_v[at, :]
        bias_ref[image, :TABLE, :] = table_bias(info, image, (TABLE, LAT))
        bias_ref[image, TABLE:, :] = jnp.zeros((LAT, LAT), F32)
        place = own_positions(info, image, lax.broadcasted_iota(jnp.int32, (SLOTS, 1), 0))
        lane = lax.broadcasted_iota(jnp.int32, (SLOTS, TABLE), 1)
        hot = jnp.where(place == lane, 1.0, 0.0).astype(BF16)
        x_out[image * SLOTS : (image + 1) * SLOTS, :] = dot(hot, pos[...]).astype(BF16)
        for b in range(D // 128):
            cols = slice(b * 128, (b + 1) * 128)
            vt_ref[image, cols, :] = v_out[image, :, cols].T

    def own_norm(r):
        at = chunk(r, 64)
        values = token + x_out[at, :].astype(F32)
        xn_out[at, :] = norm_rows(values, gain0, off0).astype(BF16)
        slot = lax.broadcasted_iota(jnp.int32, (64, 1), 0) + (r % 4) * 64 + info[7] * SLOTS
        valid = slot < info[r // 4]
        dy_ref[at, :] = jnp.where(valid, cot[at, :], jnp.zeros((64, D), BF16))

    loop(ROWS // 64, own_norm)
    q_out[...] = (dot(xn_out[...], wqkv[:, :D]) + qbias).astype(BF16)

    def attend(t):
        image, g = t // 2, t % 2
        cols = chunk(g, GW)
        keys = k_out[image, :, cols]
        query = q_out[chunk(image, SLOTS), cols] * jnp.asarray(0.125, BF16)
        bias = bias_ref[image]
        bias = jnp.concatenate([bias, bias], 1)
        lane = lax.broadcasted_iota(jnp.int32, (SLOTS, GW), 1) // HD
        for h in range(GROUP):
            scores = dot(keys, jnp.where(lane == h, query, jnp.zeros_like(query)), NT) + bias
            top = jnp.max(scores, 0, keepdims=True)
            expo = jnp.exp(scores - top)
            total = col_sum(expo)
            low = expo.astype(BF16)
            e_out[t, :, h * SLOTS : (h + 1) * SLOTS] = low
            at = pl.ds(pl.multiple_of(g * GW + h * HD, HD), HD)
            inverse = 1.0 / total
            ot_ref[image, at, :] = dot(vt_ref[image, at, :], low) * inverse
            inv_out[t, h : h + 1, :] = inverse

    loop(4, attend)
    for image in range(IMGS):
        for b in range(D // 128):
            cols = slice(b * 128, (b + 1) * 128)
            attn_out[image * SLOTS : (image + 1) * SLOTS, cols] = (
                ot_ref[image, cols, :].T.astype(BF16)
            )
    out_bias = row_of(biases, 3)
    mid_ref[...] = dot(attn_out[...], wo[...]) + out_bias

    def mid_norm(r):
        at = chunk(r, 64)
        values = mid_ref[at, :] + (token + x_out[at, :].astype(F32))
        mid_ref[at, :] = values
        hn_ref[at, :] = norm_rows(values, gain1, off1).astype(BF16)

    loop(ROWS // 64, mid_norm)

    def feed(j):
        cols = chunk(j, D)
        at = chunk(j, D)
        act_grad = dot(dy_ref[...], wout[at, :], NT)
        pre = dot(hn_ref[...], win[:, cols]) + hbias[0:1, cols].astype(F32)
        act, slope = gelu_parts(pre)
        act_ref[...] = act.astype(BF16)
        pre_grad = (act_grad * slope).astype(BF16)
        dpre_ref[...] = pre_grad
        sm_out[pl.ds(4 + j, 1), :] = col_sum(pre_grad.astype(F32))
        more = dot(act_ref[...], wout[at, :])
        back = dot(dpre_ref[...], win[:, cols], NT)

        @pl.when(j == 0)
        def _():
            acc_ref[...] = more
            dhn_ref[...] = back

        @pl.when(j > 0)
        def _():
            acc_ref[...] += more
            dhn_ref[...] += back

        put_pieces(info, f_out, 0, j, dot(hn_ref[...], dpre_ref[...], TN), 64, 128)
        put_pieces(info, f_out, 64, j, dot(act_ref[...], dy_ref[...], TN), 64, 128)

    loop(FF // D, feed)
    last_bias = row_of(biases, 5)

    def finish(r, carry):
        gain_sum, off_sum, out_sum = carry
        at = chunk(r, 64)
        values = mid_ref[at, :]
        final = values + acc_ref[at, :] + last_bias
        slot = lax.broadcasted_iota(jnp.int32, (64, 1), 0) + (r % 4) * 64 + info[7] * SLOTS
        valid = slot < info[r // 4]
        res_out[at, :] = jnp.where(valid, final, 0.0).astype(BF16)
        upstream = dhn_ref[at, :]
        down, along = norm_back(values, gain1, upstream)
        top = dy_ref[at, :].astype(F32)
        dmid_out[at, :] = top + down
        return gain_sum + fold(along), off_sum + fold(upstream), out_sum + fold(top)

    zero = jnp.zeros((8, D), F32)
    gain_sum, off_sum, out_sum = lax.fori_loop(0, ROWS // 64, finish, (zero, zero, zero))
    sm_out[0:1, :] = col_sum(gain_sum)
    sm_out[1:2, :] = col_sum(off_sum)
    sm_out[2:3, :] = col_sum(out_sum)
    sm_out[3:4, :] = jnp.zeros((1, D), F32)


def dec_back(
    info, dmid, attn, e_in, inv, q_in, k_in, v_in, tn, xn, ln, x_in, pos, quant, lemb, wqkv, wo,
    gains, biases,
    f_out, code_out, sm_out,
    da_ref, dqt_ref, dk_ref, dv_ref, dkl_ref, dvl_ref, kt_ref, ds_ref, dq_ref, dkv_ref, dkvl_ref,
    w_ref, dn_ref, din_ref, tab_ref, dbr_ref,
):
    gain0, off0 = row_of(gains, 0), row_of(biases, 0)
    token = row_of(biases, 7)

    def branch(r, carry):
        at = chunk(r, 64)
        low = dmid[at, :].astype(BF16)
        dbr_ref[at, :] = low
        return carry + fold(low.astype(F32))

    zero = jnp.zeros((8, D), F32)
    sm_out[3:4, :] = col_sum(lax.fori_loop(0, ROWS // 64, branch, zero))
    da_ref[...] = dot(dbr_ref[...], wo[...], NT).astype(BF16)
    w_ref[:, :D] = dot(attn[...], dbr_ref[...], TN)
    for z in range(4):
        put_pieces(info, f_out, 0, z, w_ref[z * 128 : (z + 1) * 128, :D], 16, 128)
    for image in range(IMGS):
        for b in range(D // 128):
            cols = slice(b * 128, (b + 1) * 128)
            kt_ref[image, cols, :] = k_in[image, :, cols].T
    dk_ref[...] = jnp.zeros_like(dk_ref)
    dv_ref[...] = jnp.zeros_like(dv_ref)

    def attend(t):
        image, g = t // 2, t % 2
        cols = chunk(g, GW)
        rows = chunk(image, SLOTS)
        lat_rows = chunk(image, LAT)
        out_grad_t = da_ref[rows, cols].astype(F32).T
        out_t = attn[rows, cols].astype(F32).T
        scaled, inner = [], []
        for h in range(GROUP):
            at = slice(h * HD, (h + 1) * HD)
            inverse = inv[t, h : h + 1, :]
            scaled.append(out_grad_t[at, :] * inverse)
            inner.append(col_sum(out_grad_t[at, :] * out_t[at, :]) * inverse)
        out_grad = jnp.concatenate(scaled, 0).T.astype(BF16)
        out_stack = head_stack(out_grad, SLOTS)
        query = q_in[rows, cols] * jnp.asarray(0.125, BF16)
        values = v_in[image, :, cols]
        for h in range(GROUP):
            lanes = slice(h * SLOTS, (h + 1) * SLOTS)
            prob_grad = dot(values, out_stack[lanes, :], NT)
            low = (e_in[t, :, lanes].astype(F32) * (prob_grad - inner[h])).astype(BF16)
            ds_ref[:, lanes] = low
            at = pl.ds(pl.multiple_of(g * GW + h * HD, HD), HD)
            dqt_ref[image, at, :] = dot(kt_ref[image, at, :], low)
        value_grad = dot(e_in[t], out_stack)
        dv_ref[:, cols] += value_grad[:TABLE, :]
        dvl_ref[lat_rows, cols] = value_grad[TABLE:, :]
        key_grad = dot(ds_ref[...], head_stack(query, SLOTS))
        dk_ref[:, cols] += key_grad[:TABLE, :]
        dkl_ref[lat_rows, cols] = key_grad[TABLE:, :]

    loop(4, attend)
    for image in range(IMGS):
        for b in range(D // 128):
            cols = slice(b * 128, (b + 1) * 128)
            dq_ref[image * SLOTS : (image + 1) * SLOTS, cols] = (
                (dqt_ref[image, cols, :] * 0.125).T.astype(BF16)
            )
    dkv_ref[:, :D] = dk_ref[...].astype(BF16)
    dkv_ref[:, D:] = dv_ref[...].astype(BF16)
    dkvl_ref[:, :D] = dkl_ref[...].astype(BF16)
    dkvl_ref[:, D:] = dvl_ref[...].astype(BF16)
    sm_out[4:5, :] = col_sum(fold(dq_ref[...].astype(F32)))
    sm_out[5:6, :] = col_sum(fold(dv_ref[...]) + fold(dvl_ref[...]))
    w_ref[:, :D] = dot(xn[...], dq_ref[...], TN)
    w_ref[:, D:] = dot(tn[...], dkv_ref[...], TN) + dot(ln[...], dkvl_ref[...], TN)
    for z in range(4):
        put_pieces(info, f_out, 16, z, w_ref[z * 128 : (z + 1) * 128, :], 16, 384)
    dn_ref[:ROWS, :] = dot(dq_ref[...], wqkv[:, :D], NT)

    def own(r, carry):
        gain_sum, off_sum = carry
        at = chunk(r, 64)
        upstream = dn_ref[at, :]
        down, along = norm_back(token + x_in[at, :].astype(F32), gain0, upstream)
        din_ref[at, :] = (dmid[at, :] + down).astype(BF16)
        return gain_sum + fold(along), off_sum + fold(upstream)

    sums = lax.fori_loop(0, ROWS // 64, own, (zero, zero))
    for r in range(4):
        at = slice(r * 256, (r + 1) * 256)
        dn_ref[at, :] = dot(dkv_ref[at, :], wqkv[:, D:], NT)
    lane = lax.broadcasted_iota(jnp.int32, (1, SLOTS), 1)
    place = [own_positions(info, image, lane) for image in range(IMGS)]

    def scatter(r):
        at = chunk(r, 256)
        index = lax.broadcasted_iota(jnp.int32, (256, SLOTS), 0) + r * 256
        total = jnp.zeros((256, D), F32)
        for image in range(IMGS):
            hot = jnp.where(place[image] == index, 1.0, 0.0).astype(BF16)
            total = total + dot(hot, din_ref[image * SLOTS : (image + 1) * SLOTS, :])
        tab_ref[at, :] = total

    loop(4, scatter)

    def table(r, carry):
        gain_sum, off_sum, mask_sum = carry
        at = chunk(r, 64)
        upstream = dn_ref[at, :]
        down, along = norm_back(token + pos[at, :].astype(F32), gain0, upstream)
        rows = tab_ref[at, :] + down
        tab_ref[at, :] = rows
        return gain_sum + fold(along), off_sum + fold(upstream), mask_sum + fold(rows)

    gain_sum, off_sum, mask_sum = lax.fori_loop(0, TABLE // 64, table, sums + (zero,))
    for z in range(4):
        put_pieces(info, f_out, 64, z, tab_ref[z * 256 : (z + 1) * 256, :], 32, 128)
    dn_ref[:LROWS, :] = dot(dkvl_ref[...], wqkv[:, D:], NT)
    tab_ref[:LROWS, :] = dot(quant[...], lemb[...], TN) + row_of(biases, 6)

    def latent(r, carry):
        gain_sum, off_sum, embed_sum = carry
        at = chunk(r, 64)
        upstream = dn_ref[at, :]
        down, along = norm_back(tab_ref[at, :], gain0, upstream)
        low = down.astype(BF16)
        din_ref[at, :] = low
        return gain_sum + fold(along), off_sum + fold(upstream), embed_sum + fold(low.astype(F32))

    gain_sum, off_sum, embed_sum = lax.fori_loop(
        0, LROWS // 64, latent, (gain_sum, off_sum, zero)
    )
    embed_grad = din_ref[:LROWS, :]
    code_out[...] = dot(lemb[...], embed_grad, NT)
    sm_out[0:1, :] = col_sum(gain_sum)
    sm_out[1:2, :] = col_sum(off_sum)
    sm_out[2:3, :] = col_sum(mask_sum)
    sm_out[6:7, :] = col_sum(embed_sum)
    sm_out[7:8, :] = jnp.zeros((1, D), F32)
    sm_out[8:20, :] = dot(quant[...], embed_grad)
    sm_out[20:, :] = jnp.zeros((4, D), F32)


def enc_mid(
    info, parts0, parts1, parts2, parts3, latents, wo, win, wout, gains, biases, hbias, proj, pbias, quant,
    attn_out, mid_out, hn_out, act_out, slope_out, final_out, post_out, diff_out, lse_out,
    ot_ref, acc_ref,
):
    logs = []
    for part in (parts0, parts1, parts2, parts3):
        logs.append(
            part[D : D + 8, :].astype(F32)
            + part[D + 8 : D + 16, :].astype(F32)
            + part[D + 16 : D + 24, :].astype(F32)
        )
    top = functools.reduce(jnp.maximum, logs)
    log_total = top + jnp.log(sum(jnp.exp(rows - top) for rows in logs))
    lse_out[...] = log_total
    weights = [jnp.exp(rows - log_total) for rows in logs]
    for h in range(HEADS):
        at = slice(h * HD, (h + 1) * HD)
        ot_ref[at, :] = sum(
            part[at, :].astype(F32) * weight[h : h + 1, :]
            for part, weight in zip((parts0, parts1, parts2, parts3), weights)
        )
    for b in range(D // 128):
        cols = slice(b * 128, (b + 1) * 128)
        attn_out[:, cols] = ot_ref[cols, :].T.astype(BF16)
    acc_ref[...] = dot(attn_out[...], wo[...]) + row_of(biases, 2)
    gain1, off1 = row_of(gains, 1), row_of(biases, 3)
    gain2, off2 = row_of(gains, 2), row_of(biases, 5)

    def mid_norm(r):
        at = chunk(r, 64)
        values = acc_ref[at, :] + latents[at, :].astype(F32)
        mid_out[at, :] = values
        hn_out[at, :] = norm_rows(values, gain1, off1).astype(BF16)
        acc_ref[at, :] = values + row_of(biases, 4)

    loop(LROWS // 64, mid_norm)

    def feed(j):
        cols = chunk(j, D)
        pre = dot(hn_out[...], win[:, cols]) + hbias[0:1, cols].astype(F32)
        act, slope = gelu_parts(pre)
        low = act.astype(BF16)
        act_out[:, cols] = low
        slope_out[:, cols] = slope
        acc_ref[...] += dot(low, wout[cols, :])

    loop(FF // D, feed)

    def post_norm(r):
        at = chunk(r, 64)
        values = acc_ref[at, :]
        final_out[at, :] = values
        post_out[at, :] = norm_rows(values, gain2, off2).astype(BF16)

    loop(LROWS // 64, post_norm)
    code = dot(proj[...], post_out[...], NT) + pbias[...].astype(F32)
    diff_out[...] = code - quant[...].astype(F32)


def enc_mlp_back(
    info, code0, code1, code2, code3, diff, post, final, mid, hn, act, slope, attn, wo, win, wout, gains, proj,
    f_out, da_out, dmid_out, sm_out,
    dy_ref, dn_ref, dfin_ref, dpre_ref, dbr_ref,
):
    zero = jnp.zeros((8, D), F32)
    gain1, gain2 = row_of(gains, 1), row_of(gains, 2)
    code_grad = code0[...] + code1[...] + code2[...] + code3[...] + 2.0 * COMMIT * diff[...]
    low = code_grad.astype(BF16)
    sm_out[16:28, :] = dot(low, post[...]) * SHARE
    sm_out[28:40, :] = jnp.broadcast_to(
        jnp.sum(low.astype(F32), -1, keepdims=True) * SHARE, (12, D)
    )
    loss = (1.0 + COMMIT) * jnp.sum(diff[...] * diff[...]) * SHARE
    sm_out[40:48, :] = jnp.full((8, D), loss, F32)
    dn_ref[...] = dot(low, proj[...], TN)

    def post_back(r, carry):
        gain_sum, off_sum, out_sum = carry
        at = chunk(r, 64)
        upstream = dn_ref[at, :]
        down, along = norm_back(final[at, :], gain2, upstream)
        dfin_ref[at, :] = down
        branch = down.astype(BF16)
        dy_ref[at, :] = branch
        return gain_sum + fold(along), off_sum + fold(upstream), out_sum + fold(branch.astype(F32))

    sums = lax.fori_loop(0, LROWS // 64, post_back, (zero, zero, zero))
    for n in range(3):
        sm_out[n : n + 1, :] = col_sum(sums[n]) * SHARE
    dn_ref[...] = jnp.zeros_like(dn_ref)

    def feed(j):
        cols = chunk(j, D)
        act_grad = dot(dy_ref[...], wout[cols, :], NT)
        pre_grad = (act_grad * slope[:, cols]).astype(BF16)
        dpre_ref[:, cols] = pre_grad
        sm_out[pl.ds(8 + j, 1), :] = col_sum(pre_grad.astype(F32)) * SHARE
        dn_ref[...] += dot(pre_grad, win[:, cols], NT)

    loop(FF // D, feed)
    mine = chunk(info[7], D)
    put_pieces(info, f_out, 0, None, dot(hn[...], dpre_ref[:, mine], TN), 64, 128)
    put_pieces(info, f_out, 64, None, dot(act[:, mine], dy_ref[...], TN), 64, 128)

    def mid_back(r, carry):
        gain_sum, off_sum, out_sum = carry
        at = chunk(r, 64)
        upstream = dn_ref[at, :]
        down, along = norm_back(mid[at, :], gain1, upstream)
        total = dfin_ref[at, :] + down
        dmid_out[at, :] = total
        branch = total.astype(BF16)
        dbr_ref[at, :] = branch
        return gain_sum + fold(along), off_sum + fold(upstream), out_sum + fold(branch.astype(F32))

    sums = lax.fori_loop(0, LROWS // 64, mid_back, (zero, zero, zero))
    for n in range(3):
        sm_out[3 + n : 4 + n, :] = col_sum(sums[n]) * SHARE
    sm_out[6:8, :] = jnp.zeros((2, D), F32)
    sm_out[12:16, :] = jnp.zeros((4, D), F32)
    da_out[...] = dot(dbr_ref[...], wo[...], NT).astype(BF16)
    own = attn[:, chunk(info[7], 128)]
    put_pieces(info, f_out, 128, None, dot(own, dbr_ref[...], TN), 16, 128)


def enc_back(
    info, da, attn, lse, kv, lqkv, np_in, nl, patches, latents, wqkv, gains, codes, diff,
    sm_mlp, sm_front, sm_dec,
    f_out, patch_out, lat_out,
    bias_ref, k_ref, v_ref, kt_ref, dqt_ref, dkv_ref, dlat_ref, w_ref, dn_ref, sm_ref,
):
    zero = jnp.zeros((8, D), F32)
    gain0 = row_of(gains, 0)
    enc_bias(info, bias_ref)
    for image in range(IMGS):
        rows = slice(image * SLOTS, (image + 1) * SLOTS)
        lat_at = slice(image * LAT, (image + 1) * LAT)
        for g in range(2):
            cols = slice(g * GW, (g + 1) * GW)
            enc_keys(kv, lqkv, image, g, k_ref, v_ref, None, kt_ref)
            query_stack = head_stack(lqkv[lat_at, cols] * jnp.asarray(0.125, BF16), LAT)
            out_grad = da[lat_at, cols]
            out_stack = head_stack(out_grad, LAT)
            grad_t = out_grad.astype(F32).T
            out_t = attn[lat_at, cols].astype(F32).T
            inner = jnp.concatenate(
                [
                    col_sum(grad_t[h * HD : (h + 1) * HD, :] * out_t[h * HD : (h + 1) * HD, :])
                    for h in range(GROUP)
                ],
                1,
            )
            log_total = jnp.concatenate(
                [lse[g * GROUP + h : g * GROUP + h + 1, lat_at] for h in range(GROUP)], 1
            )
            scores = dot(k_ref[...], query_stack, NT)
            bias = jnp.concatenate([bias_ref[image]] * GROUP, 1)
            probs = jnp.exp(scores + bias - log_total)
            prob_grad = dot(v_ref[...], out_stack, NT)
            low = (probs * (prob_grad - inner)).astype(BF16)
            value_grad = dot(probs.astype(BF16), out_stack).astype(BF16)
            key_grad = dot(low, query_stack).astype(BF16)
            dkv_ref[rows, cols] = key_grad[:SLOTS, :]
            dkv_ref[rows, D + g * GW : D + (g + 1) * GW] = value_grad[:SLOTS, :]
            dlat_ref[lat_at, D + g * GW : D + (g + 1) * GW] = key_grad[SLOTS:, :]
            dlat_ref[lat_at, 2 * D + g * GW : 2 * D + (g + 1) * GW] = value_grad[SLOTS:, :]
            for h in range(GROUP):
                part = dot(kt_ref[h * HD : (h + 1) * HD, :], low[:, h * LAT : (h + 1) * LAT])
                at = g * GW + h * HD
                dqt_ref[at : at + HD, lat_at] = part * 0.125
    for b in range(D // 128):
        cols = slice(b * 128, (b + 1) * 128)
        dlat_ref[:, cols] = dqt_ref[cols, :].T.astype(BF16)
    dn_ref[...] = dot(dkv_ref[...], wqkv[:, D:], NT)

    def patch_back(r, carry):
        gain_sum, off_sum = carry
        at = chunk(r, 64)
        upstream = dn_ref[at, :]
        down, along = norm_back(patches[at, :].astype(F32), gain0, upstream)
        patch_out[at, :] = down
        return gain_sum + fold(along), off_sum + fold(upstream)

    sums = lax.fori_loop(0, ROWS // 64, patch_back, (zero, zero))
    dn_ref[:LROWS, :] = dot(dlat_ref[...], wqkv[...], NT)

    def lat_back(r, carry):
        gain_sum, off_sum = carry
        at = chunk(r, 64)
        upstream = dn_ref[at, :]
        down, along = norm_back(latents[at, :].astype(F32), gain0, upstream)
        lat_out[at, :] = down.astype(BF16)
        return gain_sum + fold(along), off_sum + fold(upstream)

    sums = lax.fori_loop(0, LROWS // 64, lat_back, sums)
    w_ref[:, :D] = dot(nl[...], dlat_ref[:, :D], TN)
    w_ref[:, D:] = dot(nl[...], dlat_ref[:, D:], TN) + dot(np_in[...], dkv_ref[...], TN)
    for z in range(4):
        put_pieces(info, f_out, 0, z, w_ref[z * 128 : (z + 1) * 128, :], 16, 384)
    sm_ref[0:1, :] = col_sum(sums[0])
    sm_ref[1:2, :] = sm_mlp[3:4, :]
    sm_ref[2:3, :] = sm_mlp[0:1, :]
    sm_ref[3:4, :] = col_sum(sums[1])
    sm_ref[4:5, :] = col_sum(
        fold(dkv_ref[:, D:].astype(F32)) + fold(dlat_ref[:, 2 * D :].astype(F32))
    )
    sm_ref[5:6, :] = sm_mlp[5:6, :]
    sm_ref[6:7, :] = sm_mlp[4:5, :]
    sm_ref[7:8, :] = sm_mlp[2:3, :]
    sm_ref[8:9, :] = sm_mlp[1:2, :]
    sm_ref[9:10, :] = col_sum(fold(dlat_ref[:, :D].astype(F32)))
    sm_ref[10:14, :] = sm_mlp[8:12, :]
    sm_ref[14:26, :] = sm_mlp[16:28, :]
    pick = lax.broadcasted_iota(jnp.int32, (12, D), 0) == lax.broadcasted_iota(
        jnp.int32, (12, D), 1
    )
    sm_ref[26:27, :] = col_sum(jnp.where(pick, sm_mlp[28:40, :], 0.0))
    sm_ref[27:28, :] = sm_mlp[40:41, :]
    sm_ref[28:40, :] = sm_dec[8:20, :]
    sm_ref[40:41, :] = sm_dec[0:1, :]
    sm_ref[41:42, :] = sm_front[0:1, :]
    sm_ref[42:43, :] = sm_dec[1:2, :]
    sm_ref[43:44, :] = sm_dec[4:5, :]
    sm_ref[44:45, :] = sm_dec[5:6, :]
    sm_ref[45:46, :] = sm_dec[3:4, :]
    sm_ref[46:47, :] = sm_front[1:2, :]
    sm_ref[47:48, :] = sm_front[2:3, :]
    sm_ref[48:49, :] = sm_dec[6:7, :]
    sm_ref[49:50, :] = sm_dec[2:3, :]
    sm_ref[50:54, :] = sm_front[4:8, :]
    sm_ref[54:, :] = jnp.zeros((SMALL - 54, D), F32)
    token = lax.broadcasted_iota(jnp.int32, (12, LROWS), 1) % LAT
    mine = jnp.where(token // 32 == info[7], -2.0 * diff[...], 0.0).astype(BF16)
    book = dot(mine, code_onehot(codes, 8 * D))
    for n in range(8):
        at = CODE_ROW + 16 * n
        sm_ref[at : at + 12, :] = book[:, n * D : (n + 1) * D]
    for p in range(PIECES):
        rel = rel_piece(info, p // 32, p % 32)
        if p < SMALL // 4:
            row, col = (p // 4) * 16, (p % 4) * 128
            f_out[rel, 48:64, :] = sm_ref[row : row + 16, col : col + 128].astype(BF16)
        else:
            f_out[rel, 48:64, :] = jnp.zeros((16, 128), BF16)


def take_pieces(info, src, offset, dst, place, rows, cols):
    for z in range(4):
        for q in range(32):
            rel = rel_piece(info, z, q)
            row, col = place(z, q)
            for b in range(cols // 128):
                at = offset + b * rows
                dst[row : row + rows, col + b * 128 : col + (b + 1) * 128] = src[
                    rel, at : at + rows, :
                ].astype(F32)


def in_place(z, q):
    return (q % 8) * 64, z * D + (q // 8) * 128


def rows_place(rows, cols):
    return lambda z, q: ((z * 8 + q % 8) * rows, (q // 8) * cols)


def unpack_dec(info, src, in_out, wout_out, out_out, qkv_out, pos_out):
    take_pieces(info, src, 0, in_out, in_place, 64, 128)
    take_pieces(info, src, 64, wout_out, rows_place(64, 128), 64, 128)
    take_pieces(info, src, 128, out_out, rows_place(16, 128), 16, 128)
    take_pieces(info, src, 144, qkv_out, rows_place(16, 384), 16, 384)
    take_pieces(info, src, 192, pos_out, rows_place(32, 128), 32, 128)


def unpack_enc(
    info, src, in_out, wout_out, out_out, qkv_out,
    gains_out, biases_out, query_out, hidden_out, proj_out, pbias_out, loss_out, embed_out,
    dgains_out, dbiases_out, dhidden_out, book_out,
    sm_ref,
):
    take_pieces(info, src, 0, in_out, in_place, 64, 128)
    take_pieces(info, src, 64, wout_out, rows_place(64, 128), 64, 128)
    take_pieces(info, src, 128, out_out, rows_place(16, 128), 16, 128)
    take_pieces(info, src, 144, qkv_out, rows_place(16, 384), 16, 384)
    for p in range(SMALL // 4):
        rel = rel_piece(info, p // 32, p % 32)
        row, col = (p // 4) * 16, (p % 4) * 128
        sm_ref[row : row + 16, col : col + 128] = src[rel, 192:208, :].astype(F32)
    gains_out[...] = sm_ref[0:3, :]
    biases_out[...] = sm_ref[3:9, :]
    query_out[...] = sm_ref[9:10, :]
    for n in range(4):
        hidden_out[:, n * D : (n + 1) * D] = sm_ref[10 + n : 11 + n, :]
        dhidden_out[:, n * D : (n + 1) * D] = sm_ref[50 + n : 51 + n, :]
    proj_out[...] = sm_ref[14:26, :]
    pbias_out[...] = sm_ref[26:27, :128]
    loss_out[...] = sm_ref[27:28, :128]
    embed_out[...] = sm_ref[28:40, :]
    dgains_out[...] = sm_ref[40:42, :]
    dbiases_out[...] = sm_ref[42:50, :]
    for n in range(8):
        at = CODE_ROW + 16 * n
        book_out[:, n * D : (n + 1) * D] = sm_ref[at : at + 12, :]


def call(kernel, name, outs, scratch, info, *args, flops=0):
    out_shape = [jax.ShapeDtypeStruct(shape, kind) for shape, kind in outs]
    moved = sum(a.size * a.dtype.itemsize for a in args) + sum(
        o.size * o.dtype.itemsize for o in out_shape
    )
    vmem = pl.BlockSpec(memory_space=pltpu.VMEM)
    return pl.pallas_call(
        kernel,
        out_shape=out_shape,
        in_specs=[pl.BlockSpec(memory_space=pltpu.SMEM)] + [vmem] * len(args),
        out_specs=[vmem] * len(outs),
        scratch_shapes=[pltpu.VMEM(shape, kind) for shape, kind in scratch],
        compiler_params=pltpu.CompilerParams(vmem_limit_bytes=VMEM_LIMIT),
        cost_estimate=pl.CostEstimate(flops=flops, bytes_accessed=moved, transcendentals=0),
        name=name,
    )(info, *args)


def shift(value, axis, by):
    return lax.ppermute(value, axis, [(i, (i + by) % 4) for i in range(4)])


def swap(value):
    return lax.ppermute(value, "core", [(0, 1), (1, 0)])


def sum_core(value):
    half = value.shape[0] // 2
    other = swap(value[half:])
    return (value[:half].astype(F32) + other.astype(F32)).astype(BF16)


def sum_axis(value, axis):
    total = value[0].astype(F32)
    for by in (1, 3, 2):
        total = total + shift(value[by], axis, by).astype(F32)
    return total.astype(BF16)


def gather_axis(value, axis):
    return jnp.stack([value] + [shift(value, axis, -by) for by in (1, 2, 3)])


def gather_all(value):
    for axis in ("x", "y", "z"):
        value = gather_axis(value, axis)
    both = jnp.stack([value, swap(value)])
    return both.reshape((PIECES,) + both.shape[-2:])


def per_device(
    enc_patches, enc_latents, resolution, lengths, codes, enc_qkv, enc_out, enc_mlp_in, enc_mlp_out,
    enc_gains, enc_biases, enc_query_bias, enc_hidden_bias, latent_proj, latent_bias, codebook,
    latent_embed, pos_table, dec_qkv, dec_out, dec_mlp_in, dec_mlp_out, dec_gains, dec_biases,
    dec_hidden_bias, out_cot,
):
    place = [lax.axis_index(axis).astype(jnp.int32) for axis in ("core", "y", "x", "z")]
    side = 3 + (resolution >= 256).astype(jnp.int32) + (resolution >= 512).astype(jnp.int32)
    info = jnp.concatenate([lengths, side, jnp.stack(place)])
    patches = enc_patches.reshape(ROWS, D)
    latents = enc_latents.reshape(LROWS, D)
    cot = out_cot.reshape(ROWS, D)
    code_col = codes.reshape(LROWS, 1)
    entries = codebook.shape[1]

    enc_norm, lat_norm, kv, lqkv, part, quant = call(
        enc_front, "enc_front",
        [((ROWS, D), BF16), ((LROWS, D), BF16), ((ROWS, 2 * D), BF16), ((LROWS, 3 * D), BF16),
         ((D + 32, LROWS), BF16), ((12, LROWS), BF16)],
        [((IMGS, OWN_KEYS, LAT), F32), ((OWN_KEYS, GW), BF16), ((GW, OWN_KEYS), BF16)],
        info, patches, latents, enc_qkv, enc_gains, enc_biases, enc_query_bias.reshape(1, D),
        code_col, codebook, flops=2_000_000_000,
    )
    parts = [part] + [shift(part, "z", -by) for by in (1, 2, 3)]

    (result, f_mlp, dmid, attn, expo, inverse, query, keys, values, tab_norm, own_norm, emb_norm,
     own_pos, sm_front) = call(
        dec_front, "dec_front",
        [((ROWS, D), BF16), ((PIECES, 128, 128), BF16), ((ROWS, D), F32), ((ROWS, D), BF16),
         ((4, KEYS, GROUP * SLOTS), BF16), ((4, GROUP, SLOTS), F32), ((ROWS, D), BF16),
         ((IMGS, KEYS, D), BF16), ((IMGS, KEYS, D), BF16), ((TABLE, D), BF16), ((ROWS, D), BF16),
         ((LROWS, D), BF16), ((ROWS, D), BF16), ((8, D), F32)],
        [((IMGS, KEYS, LAT), F32), ((IMGS, D, KEYS), BF16), ((IMGS, D, SLOTS), F32),
         ((ROWS, D), F32), ((ROWS, D), BF16), ((ROWS, D), BF16), ((ROWS, D), F32), ((ROWS, D), F32),
         ((ROWS, D), BF16), ((ROWS, D), BF16)],
        info, pos_table, quant, latent_embed, dec_qkv, dec_out, dec_mlp_in, dec_mlp_out, dec_gains,
        dec_biases, dec_hidden_bias.reshape(1, FF), cot, flops=12_000_000_000,
    )
    f_rest, code_part, sm_dec = call(
        dec_back, "dec_back",
        [((PIECES, 96, 128), BF16), ((12, LROWS), F32), ((24, D), F32)],
        [((ROWS, D), BF16), ((IMGS, D, SLOTS), F32), ((TABLE, D), F32), ((TABLE, D), F32),
         ((LROWS, D), F32), ((LROWS, D), F32), ((IMGS, D, KEYS), BF16),
         ((KEYS, GROUP * SLOTS), BF16), ((ROWS, D), BF16), ((TABLE, 2 * D), BF16),
         ((LROWS, 2 * D), BF16), ((D, 3 * D), F32), ((TABLE, D), F32), ((ROWS, D), BF16),
         ((TABLE, D), F32), ((ROWS, D), BF16)],
        info, dmid, attn, expo, inverse, query, keys, values, tab_norm, own_norm, emb_norm, own_pos,
        pos_table, quant, latent_embed, dec_qkv, dec_out, dec_gains, dec_biases,
        flops=10_000_000_000,
    )
    code_parts = [code_part] + [shift(code_part, "z", -by) for by in (1, 2, 3)]

    enc_attn, mid, hidden_norm, act, slope, final, post, diff, lse = call(
        enc_mid, "enc_mid",
        [((LROWS, D), BF16), ((LROWS, D), F32), ((LROWS, D), BF16), ((LROWS, FF), BF16),
         ((LROWS, FF), F32), ((LROWS, D), F32), ((LROWS, D), BF16), ((12, LROWS), F32),
         ((HEADS, LROWS), F32)],
        [((D, LROWS), F32), ((LROWS, D), F32)],
        info, *parts, latents, enc_out, enc_mlp_in, enc_mlp_out, enc_gains, enc_biases,
        enc_hidden_bias.reshape(1, FF), latent_proj, latent_bias.reshape(12, 1), quant,
        flops=1_500_000_000,
    )
    f_zmlp, enc_da, enc_dmid, sm_mlp = call(
        enc_mlp_back, "enc_mlp_back",
        [((32, 144, 128), BF16), ((LROWS, D), BF16), ((LROWS, D), F32), ((48, D), F32)],
        [((LROWS, D), BF16), ((LROWS, D), F32), ((LROWS, D), F32), ((LROWS, FF), BF16),
         ((LROWS, D), BF16)],
        info, *code_parts, diff, post, final, mid, hidden_norm, act, slope, enc_attn, enc_out,
        enc_mlp_in, enc_mlp_out, enc_gains, latent_proj, flops=2_500_000_000,
    )
    f_qkv, grad_patches, lat_part = call(
        enc_back, "enc_back",
        [((PIECES, 64, 128), BF16), ((ROWS, D), F32), ((LROWS, D), BF16)],
        [((IMGS, OWN_KEYS, LAT), F32), ((OWN_KEYS, GW), BF16), ((OWN_KEYS, GW), BF16),
         ((GW, OWN_KEYS), BF16), ((D, LROWS), F32), ((ROWS, 2 * D), BF16), ((LROWS, 3 * D), BF16),
         ((D, 3 * D), F32), ((ROWS, D), F32), ((SMALL, D), F32)],
        info, enc_da, enc_attn, lse, kv, lqkv, enc_norm, lat_norm, patches, latents, enc_qkv,
        enc_gains, code_col, diff, sm_mlp, sm_front, sm_dec, flops=3_000_000_000,
    )

    dec_mlp = sum_axis(sum_core(f_mlp).reshape(4, 4, 4, 128, 128), "z")
    dec_rest = sum_axis(sum_core(f_rest).reshape(4, 4, 4, 96, 128), "z")
    dec_sum = jnp.concatenate([dec_mlp, dec_rest], 2)
    dec_sum = sum_axis(sum_axis(dec_sum, "y"), "x")
    dec_all = gather_all(dec_sum)
    enc_rest = sum_axis(sum_core(f_qkv).reshape(4, 4, 4, 64, 128), "z")
    enc_sum = jnp.concatenate([sum_core(f_zmlp).reshape(4, 4, 144, 128), enc_rest], 2)
    enc_sum = sum_axis(sum_axis(enc_sum, "y"), "x")
    enc_all = gather_all(enc_sum)

    lat_total = lat_part.astype(F32)
    for by in (1, 2, 3):
        lat_total = lat_total + shift(lat_part, "z", by).astype(F32)
    grad_latents = (enc_dmid + lat_total).reshape(IMGS, LAT, D)

    dec_in_grad, dec_wout_grad, dec_out_grad, dec_qkv_grad, pos_grad = call(
        unpack_dec, "unpack_dec",
        [((D, FF), F32), ((FF, D), F32), ((D, D), F32), ((D, 3 * D), F32), ((TABLE, D), F32)],
        [], info, dec_all,
    )
    (enc_in_grad, enc_wout_grad, enc_out_grad, enc_qkv_grad, gains_grad, biases_grad, query_grad,
     hidden_grad, proj_grad, pbias_grad, loss, embed_grad, dec_gains_grad, dec_biases_grad,
     dec_hidden_grad, book_grad) = call(
        unpack_enc, "unpack_enc",
        [((D, FF), F32), ((FF, D), F32), ((D, D), F32), ((D, 3 * D), F32), ((3, D), F32),
         ((6, D), F32), ((1, D), F32), ((1, FF), F32), ((12, D), F32), ((1, 128), F32),
         ((1, 128), F32), ((12, D), F32), ((2, D), F32), ((8, D), F32), ((1, FF), F32),
         ((12, entries), F32)],
        [((SMALL, D), F32)], info, enc_all,
    )
    images = IMGS * lax.axis_size(("y", "x", "core"))
    quant_loss = loss[0, 0] / (images * LAT * 12)
    return (
        result.reshape(IMGS, SLOTS, D),
        grad_patches.reshape(IMGS, SLOTS, D),
        grad_latents,
        quant_loss,
        enc_qkv_grad,
        enc_out_grad,
        enc_in_grad,
        enc_wout_grad,
        gains_grad,
        biases_grad,
        query_grad.reshape(D),
        hidden_grad.reshape(FF),
        proj_grad,
        pbias_grad[0, :12],
        book_grad,
        embed_grad,
        pos_grad,
        dec_qkv_grad,
        dec_out_grad,
        dec_in_grad,
        dec_wout_grad,
        dec_gains_grad,
        dec_biases_grad,
        dec_hidden_grad.reshape(FF),
    )


def solution(mesh):
    devices = mesh.devices.reshape(4, 4, 2, 4)
    fine = Mesh(devices, ("y", "x", "core", "z"))
    dp = ("y", "x", "core")
    whole = P()
    images = P(dp, "z", None)
    placed = (images, P(dp, None, None), P(dp), P(dp), P(dp, None)) + (whole,) * 20 + (images,)
    return jax.shard_map(
        per_device,
        mesh=fine,
        in_specs=placed,
        out_specs=(images, images, P(dp, None, None)) + (whole,) * 21,
        check_vma=False,
    )
```

```python
import functools

import jax
import jax.numpy as jnp
from jax import lax
from jax.experimental import pallas as pl
from jax.experimental.pallas import tpu as pltpu
from jax.sharding import Mesh
from jax.sharding import PartitionSpec as P

F32 = jnp.float32
BF16 = jnp.bfloat16
EPS = 1e-06
COMMIT = 0.25
NEG = -1e30
D = 512
HEADS = 8
HD = 64
FF = 2048
GROUP = 4
GW = GROUP * HD
LAT = 128
IMGS = 2
SLOTS = 256
ROWS = IMGS * SLOTS
LROWS = IMGS * LAT
TABLE = 1024
KEYS = TABLE + LAT
OWN_KEYS = SLOTS + LAT
PIECES = 128
SHARE = 0.25
SMALL = 192
CODE_ROW = 64

NN = (((1,), (0,)), ((), ()))
NT = (((1,), (1,)), ((), ()))
TN = (((0,), (0,)), ((), ()))
VMEM_LIMIT = 60 * 1024 * 1024


def dot(left, right, dims=NN):
    return lax.dot_general(left, right, dims, preferred_element_type=F32)


def row_of(ref, index):
    return ref[index : index + 1, :].astype(F32)


def norm_parts(values):
    centre = values - jnp.mean(values, -1, keepdims=True)
    scale = lax.rsqrt(jnp.mean(centre * centre, -1, keepdims=True) + EPS)
    return centre * scale, scale


def norm_rows(values, gain, offset):
    return norm_parts(values)[0] * gain + offset


def norm_back(values, gain, upstream):
    hat, scale = norm_parts(values)
    inner = upstream * gain
    low = jnp.mean(inner, -1, keepdims=True)
    along = jnp.mean(inner * hat, -1, keepdims=True)
    return scale * (inner - low - hat * along), upstream * hat


def fold(values):
    return jnp.sum(values.reshape(values.shape[0] // 8, 8, values.shape[1]), 0)


def col_sum(values):
    return jnp.sum(values, 0, keepdims=True)


def gelu_parts(point):
    size = jnp.abs(point) * 0.7071067811865476
    t = 1.0 / (1.0 + 0.3275911 * size)
    bell = jnp.exp(-0.5 * point * point)
    poly = t * (
        0.254829592
        + t * (-0.284496736 + t * (1.421413741 + t * (-1.453152027 + t * 1.061405429)))
    )
    tail = 0.5 * poly * bell
    cdf = jnp.where(point >= 0, 1.0 - tail, tail)
    return point * cdf, cdf + point * bell * 0.3989422804014327


def loop(count, body):
    def step(index, carry):
        body(index)
        return carry

    lax.fori_loop(0, count, step, 0)


def chunk(index, size):
    return pl.ds(pl.multiple_of(index * size, size), size)


def head_stack(block, rows):
    lane = lax.broadcasted_iota(jnp.int32, (rows, GW), 1) // HD
    parts = [jnp.where(lane == h, block, jnp.zeros_like(block)) for h in range(GROUP)]
    return jnp.concatenate(parts, 0)


class Info:
    def __init__(self, lengths, resolution):
        self.lengths, self.resolution = lengths, resolution

    def __getitem__(self, index):
        if isinstance(index, int) and index >= 4:
            return lax.axis_index(("core", "y", "x", "z")[index - 4])
        return self.lengths[index]

    def side(self, image):
        size = self.resolution[image]
        return 3 + jnp.where(size >= 256, 1, 0) + jnp.where(size >= 512, 1, 0)


def coords(info):
    return info[4], info[5], info[6], info[7]


def turn(at, own):
    return (at - own) & 3


def plane_index(info, core, y, x):
    first = turn(y, info[5]) * 4 + x
    second = turn(x, info[6]) * 4 + y
    return jnp.where(core == 0, first, second)


def put_pieces(info, keep, send, offset, z, block, rows, cols):
    mine_first = info[4] == 0
    base = 0 if z is None else turn(z, info[7]) * 16
    for q in range(16):
        y, x = q // 4, q % 4
        own = base + plane_index(info, info[4], y, x)
        away = base + plane_index(info, 1 - info[4], y, x)
        row = (q % 8) * rows
        for b in range(cols // 128):
            col = (q // 8) * cols + b * 128
            at = offset + b * rows
            mine = block[row : row + rows, col : col + 128].astype(BF16)
            col = col + 2 * cols
            other = block[row : row + rows, col : col + 128].astype(BF16)
            keep[own, at : at + rows, :] = jnp.where(mine_first, mine, other)
            send[away, at : at + rows, :] = jnp.where(mine_first, other, mine)


def own_positions(info, image, iota):
    shift = info.side(image)
    side = lax.shift_left(1, shift)
    slot = info[7] * SLOTS + iota
    row = jnp.minimum(lax.shift_right_logical(slot, shift), side - 1)
    col = slot & (side - 1)
    up = lax.shift_right_logical(row * 32, shift)
    across = lax.shift_right_logical(col * 32, shift)
    return up * 32 + across


def table_bias(info, image, shape):
    shift = info.side(image)
    place = lax.broadcasted_iota(jnp.int32, shape, 0)
    gap = 5 - shift
    mask = lax.shift_left(1, gap) - 1
    row = lax.shift_right_logical(place, 5)
    col = place & 31
    slot = lax.shift_left(lax.shift_right_logical(row, gap), shift) + lax.shift_right_logical(
        col, gap
    )
    keep = jnp.logical_and(((row | col) & mask) == 0, slot < info[image])
    return jnp.where(keep, 0.0, NEG)


def code_onehot(codes_ref, entries):
    ids = jnp.concatenate([codes_ref[image : image + 1, :] for image in range(IMGS)], 1)
    entry = lax.broadcasted_iota(jnp.int32, (entries, LROWS), 0)
    return jnp.where(ids == entry, 1.0, 0.0).astype(BF16)


def enc_front(
    info, patches, latents, wqkv, gains, biases, qbias, codes, codebook,
    np_out, nl_out, kv_out, lqkv_out, part_out, quant_out,
    bias_ref, k_ref, vt_ref,
):
    gain, offset = row_of(gains, 0), row_of(biases, 0)
    vbias = row_of(biases, 1)

    def norm_patch(r):
        at = chunk(r, 64)
        np_out[at, :] = norm_rows(patches[at, :].astype(F32), gain, offset).astype(BF16)

    loop(ROWS // 64, norm_patch)

    def norm_lat(r):
        at = chunk(r, 64)
        nl_out[at, :] = norm_rows(latents[at, :].astype(F32), gain, offset).astype(BF16)

    loop(LROWS // 64, norm_lat)
    kv_out[:, :D] = dot(np_out[...], wqkv[:, D : 2 * D]).astype(BF16)
    kv_out[:, D:] = (dot(np_out[...], wqkv[:, 2 * D :]) + vbias).astype(BF16)
    lqkv_out[:, :D] = (dot(nl_out[...], wqkv[:, :D]) + qbias[...].astype(F32).reshape(1, D)).astype(BF16)
    lqkv_out[:, D : 2 * D] = dot(nl_out[...], wqkv[:, D : 2 * D]).astype(BF16)
    lqkv_out[:, 2 * D :] = (dot(nl_out[...], wqkv[:, 2 * D :]) + vbias).astype(BF16)
    quant_out[...] = dot(codebook[...], code_onehot(codes, codebook.shape[1])).astype(BF16)
    enc_bias(info, bias_ref)
    part_out[D:, :] = jnp.zeros((32, LROWS), BF16)
    for image in range(IMGS):
        lat_at = slice(image * LAT, (image + 1) * LAT)
        lane_at = slice(image * LAT, (image + 1) * LAT)
        for g in range(2):
            cols = slice(g * GW, (g + 1) * GW)
            enc_keys(kv_out, lqkv_out, image, g, k_ref, None, vt_ref, None)
            query = lqkv_out[lat_at, cols] * jnp.asarray(0.125, BF16)
            scores = dot(k_ref[...], head_stack(query, LAT), NT)
            bias = bias_ref[image]
            scores = scores + jnp.concatenate([bias] * GROUP, 1)
            top = jnp.max(scores, 0, keepdims=True)
            expo = jnp.exp(scores - top)
            total = col_sum(expo)
            low = expo.astype(BF16)
            log_total = top + jnp.log(total)
            inverse = 1.0 / total
            for h in range(GROUP):
                head = slice(h * LAT, (h + 1) * LAT)
                mixed = dot(vt_ref[h * HD : (h + 1) * HD, :], low[:, head])
                at = g * GW + h * HD
                part_out[at : at + HD, lane_at] = (mixed * inverse[:, head]).astype(BF16)
            rows = jnp.concatenate(
                [log_total[:, h * LAT : (h + 1) * LAT] for h in range(GROUP)], 0
            )
            high = rows.astype(BF16)
            rest = rows - high.astype(F32)
            mid = rest.astype(BF16)
            last = (rest - mid.astype(F32)).astype(BF16)
            for n, piece in enumerate((high, mid, last)):
                at = D + 8 * n + 4 * g
                part_out[at : at + 4, lane_at] = piece


def enc_bias(info, bias_ref):
    place = lax.broadcasted_iota(jnp.int32, (SLOTS, LAT), 0) + info[7] * SLOTS
    token = lax.broadcasted_iota(jnp.int32, (LAT, LAT), 0) // 32
    lat = jnp.where(token == info[7], 0.0, NEG)
    for image in range(IMGS):
        bias_ref[image, :SLOTS, :] = jnp.where(place < info[image], 0.0, NEG)
        bias_ref[image, SLOTS:, :] = lat


def enc_keys(kv, lqkv, image, g, k_ref, v_ref, vt_ref, kt_ref):
    rows = slice(image * SLOTS, (image + 1) * SLOTS)
    lat_at = slice(image * LAT, (image + 1) * LAT)
    k_ref[:SLOTS, :] = kv[rows, g * GW : (g + 1) * GW]
    k_ref[SLOTS:, :] = lqkv[lat_at, D + g * GW : D + (g + 1) * GW]
    value = jnp.concatenate(
        [kv[rows, D + g * GW : D + (g + 1) * GW], lqkv[lat_at, 2 * D + g * GW : 2 * D + (g + 1) * GW]],
        0,
    )
    if v_ref is not None:
        v_ref[...] = value
    if vt_ref is not None:
        vt_ref[...] = value.T
    if kt_ref is not None:
        kt_ref[...] = k_ref[...].T


def dec_front(
    info, pos, quant, lemb, wqkv, wo, win, wout, gains, biases, hbias, cot,
    res_out, keep_out, send_out, dmid_out, attn_out, tn_out, xn_out, ln_out, x_out, sm_out,
    dq_ref, dkv_ref, dkvl_ref, dbr_ref, code_out, sm_back,
    e_out, inv_out, q_out, k_out, v_out,
    bias_ref, vt_ref, ot_ref, mid_ref, hn_ref, dy_ref, acc_ref, dhn_ref, act_ref, dpre_ref,
    da_ref, dqt_ref, dk_ref, dv_ref, dkl_ref, dvl_ref, kt_ref, ds_ref, dn_ref, emb_ref, din_ref,
):
    gain0, off0 = row_of(gains, 0), row_of(biases, 0)
    gain1, off1 = row_of(gains, 1), row_of(biases, 4)
    qbias, vbias = row_of(biases, 1), row_of(biases, 2)
    token = row_of(biases, 7)

    def table_norm(r):
        at = chunk(r, 64)
        values = token + pos[at, :].astype(F32)
        tn_out[at, :] = norm_rows(values, gain0, off0).astype(BF16)

    loop(TABLE // 64, table_norm)

    def table_keys(r):
        at = chunk(r, 256)
        key = dot(tn_out[at, :], wqkv[:, D : 2 * D]).astype(BF16)
        value = (dot(tn_out[at, :], wqkv[:, 2 * D :]) + vbias).astype(BF16)
        for image in range(IMGS):
            k_out[image, at, :] = key
            v_out[image, at, :] = value

    loop(TABLE // 256, table_keys)
    embed = dot(quant[...], lemb[...], TN) + row_of(biases, 6)
    ln_out[...] = norm_rows(embed, gain0, off0).astype(BF16)
    lat_k = dot(ln_out[...], wqkv[:, D : 2 * D]).astype(BF16)
    lat_v = (dot(ln_out[...], wqkv[:, 2 * D :]) + vbias).astype(BF16)
    for image in range(IMGS):
        at = slice(image * LAT, (image + 1) * LAT)
        k_out[image, TABLE:, :] = lat_k[at, :]
        v_out[image, TABLE:, :] = lat_v[at, :]
        bias_ref[image, :TABLE, :] = table_bias(info, image, (TABLE, LAT))
        bias_ref[image, TABLE:, :] = jnp.zeros((LAT, LAT), F32)
        place = own_positions(info, image, lax.broadcasted_iota(jnp.int32, (SLOTS, 1), 0))
        lane = lax.broadcasted_iota(jnp.int32, (SLOTS, TABLE), 1)
        hot = jnp.where(place == lane, 1.0, 0.0).astype(BF16)
        x_out[image * SLOTS : (image + 1) * SLOTS, :] = dot(hot, pos[...]).astype(BF16)
        for b in range(D // 128):
            cols = slice(b * 128, (b + 1) * 128)
            vt_ref[image, cols, :] = v_out[image, :, cols].T

    def own_norm(r):
        at = chunk(r, 64)
        values = token + x_out[at, :].astype(F32)
        xn_out[at, :] = norm_rows(values, gain0, off0).astype(BF16)
        slot = lax.broadcasted_iota(jnp.int32, (64, 1), 0) + (r % 4) * 64 + info[7] * SLOTS
        valid = slot < info[r // 4]
        dy_ref[at, :] = jnp.where(valid, cot[at, :], jnp.zeros((64, D), BF16))

    loop(ROWS // 64, own_norm)
    q_out[...] = (dot(xn_out[...], wqkv[:, :D]) + qbias).astype(BF16)

    def attend(t):
        image, g = t // 2, t % 2
        cols = chunk(g, GW)
        keys = k_out[image, :, cols]
        query = q_out[chunk(image, SLOTS), cols] * jnp.asarray(0.125, BF16)
        bias = bias_ref[image]
        bias = jnp.concatenate([bias, bias], 1)
        lane = lax.broadcasted_iota(jnp.int32, (SLOTS, GW), 1) // HD
        for h in range(GROUP):
            scores = dot(keys, jnp.where(lane == h, query, jnp.zeros_like(query)), NT) + bias
            top = jnp.max(scores, 0, keepdims=True)
            expo = jnp.exp(scores - top)
            total = col_sum(expo)
            low = expo.astype(BF16)
            e_out[t, :, h * SLOTS : (h + 1) * SLOTS] = low
            at = pl.ds(pl.multiple_of(g * GW + h * HD, HD), HD)
            inverse = 1.0 / total
            ot_ref[image, at, :] = dot(vt_ref[image, at, :], low) * inverse
            inv_out[t, h : h + 1, :] = inverse

    loop(4, attend)
    for image in range(IMGS):
        for b in range(D // 128):
            cols = slice(b * 128, (b + 1) * 128)
            attn_out[image * SLOTS : (image + 1) * SLOTS, cols] = (
                ot_ref[image, cols, :].T.astype(BF16)
            )
    out_bias = row_of(biases, 3)
    mid_ref[...] = dot(attn_out[...], wo[...]) + out_bias

    def mid_norm(r):
        at = chunk(r, 64)
        values = mid_ref[at, :] + (token + x_out[at, :].astype(F32))
        mid_ref[at, :] = values
        hn_ref[at, :] = norm_rows(values, gain1, off1).astype(BF16)

    loop(ROWS // 64, mid_norm)

    def feed(j):
        cols = chunk(j, D)
        at = chunk(j, D)
        act_grad = dot(dy_ref[...], wout[at, :], NT)
        pre = dot(hn_ref[...], win[:, cols]) + hbias[cols].astype(F32).reshape(1, D)
        act, slope = gelu_parts(pre)
        act_ref[...] = act.astype(BF16)
        pre_grad = (act_grad * slope).astype(BF16)
        dpre_ref[...] = pre_grad
        sm_out[pl.ds(4 + j, 1), :] = col_sum(pre_grad.astype(F32))
        more = dot(act_ref[...], wout[at, :])
        back = dot(dpre_ref[...], win[:, cols], NT)

        @pl.when(j == 0)
        def _():
            acc_ref[...] = more
            dhn_ref[...] = back

        @pl.when(j > 0)
        def _():
            acc_ref[...] += more
            dhn_ref[...] += back

        put_pieces(info, keep_out, send_out, 0, j, dot(hn_ref[...], dpre_ref[...], TN), 64, 128)
        put_pieces(info, keep_out, send_out, 64, j, dot(act_ref[...], dy_ref[...], TN), 64, 128)

    loop(FF // D, feed)
    last_bias = row_of(biases, 5)

    def finish(r, carry):
        gain_sum, off_sum, out_sum = carry
        at = chunk(r, 64)
        values = mid_ref[at, :]
        final = values + acc_ref[at, :] + last_bias
        slot = lax.broadcasted_iota(jnp.int32, (64, 1), 0) + (r % 4) * 64 + info[7] * SLOTS
        valid = slot < info[r // 4]
        res_out[at, :] = jnp.where(valid, final, 0.0).astype(BF16)
        upstream = dhn_ref[at, :]
        down, along = norm_back(values, gain1, upstream)
        top = dy_ref[at, :].astype(F32)
        dmid_out[at, :] = top + down
        return gain_sum + fold(along), off_sum + fold(upstream), out_sum + fold(top)

    zero = jnp.zeros((8, D), F32)
    gain_sum, off_sum, out_sum = lax.fori_loop(0, ROWS // 64, finish, (zero, zero, zero))
    sm_out[0:1, :] = col_sum(gain_sum)
    sm_out[1:2, :] = col_sum(off_sum)
    sm_out[2:3, :] = col_sum(out_sum)
    sm_out[3:4, :] = jnp.zeros((1, D), F32)
    dec_back(
        dmid_out, attn_out, e_out, inv_out, q_out, k_out, v_out, quant, lemb, wqkv, wo, gains, biases,
        dq_ref, dkv_ref, dkvl_ref, dbr_ref, code_out, sm_back,
        da_ref, dqt_ref, dk_ref, dv_ref, dkl_ref, dvl_ref, kt_ref, ds_ref, dn_ref, emb_ref, din_ref,
    )


def dec_back(
    dmid, attn, e_in, inv, q_in, k_in, v_in, quant, lemb, wqkv, wo, gains, biases,
    dq_ref, dkv_ref, dkvl_ref, dbr_ref, code_out, sm_out,
    da_ref, dqt_ref, dk_ref, dv_ref, dkl_ref, dvl_ref, kt_ref, ds_ref, dn_ref, emb_ref, din_ref,
):
    gain0 = row_of(gains, 0)

    def branch(r, carry):
        at = chunk(r, 64)
        low = dmid[at, :].astype(BF16)
        dbr_ref[at, :] = low
        return carry + fold(low.astype(F32))

    zero = jnp.zeros((8, D), F32)
    sm_out[3:4, :] = col_sum(lax.fori_loop(0, ROWS // 64, branch, zero))
    da_ref[...] = dot(dbr_ref[...], wo[...], NT).astype(BF16)
    for image in range(IMGS):
        for b in range(D // 128):
            cols = slice(b * 128, (b + 1) * 128)
            kt_ref[image, cols, :] = k_in[image, :, cols].T
    dk_ref[...] = jnp.zeros_like(dk_ref)
    dv_ref[...] = jnp.zeros_like(dv_ref)

    def attend(t):
        image, g = t // 2, t % 2
        cols = chunk(g, GW)
        rows = chunk(image, SLOTS)
        lat_rows = chunk(image, LAT)
        out_grad_t = da_ref[rows, cols].astype(F32).T
        out_t = attn[rows, cols].astype(F32).T
        scaled, inner = [], []
        for h in range(GROUP):
            at = slice(h * HD, (h + 1) * HD)
            inverse = inv[t, h : h + 1, :]
            scaled.append(out_grad_t[at, :] * inverse)
            inner.append(col_sum(out_grad_t[at, :] * out_t[at, :]) * inverse)
        out_grad = jnp.concatenate(scaled, 0).T.astype(BF16)
        out_stack = head_stack(out_grad, SLOTS)
        query = q_in[rows, cols] * jnp.asarray(0.125, BF16)
        values = v_in[image, :, cols]
        for h in range(GROUP):
            lanes = slice(h * SLOTS, (h + 1) * SLOTS)
            prob_grad = dot(values, out_stack[lanes, :], NT)
            low = (e_in[t, :, lanes].astype(F32) * (prob_grad - inner[h])).astype(BF16)
            ds_ref[:, lanes] = low
            at = pl.ds(pl.multiple_of(g * GW + h * HD, HD), HD)
            dqt_ref[image, at, :] = dot(kt_ref[image, at, :], low)
        value_grad = dot(e_in[t], out_stack)
        dv_ref[:, cols] += value_grad[:TABLE, :]
        dvl_ref[lat_rows, cols] = value_grad[TABLE:, :]
        key_grad = dot(ds_ref[...], head_stack(query, SLOTS))
        dk_ref[:, cols] += key_grad[:TABLE, :]
        dkl_ref[lat_rows, cols] = key_grad[TABLE:, :]

    loop(4, attend)
    dkvl_ref[:, :D] = dkl_ref[...].astype(BF16)
    dkvl_ref[:, D:] = dvl_ref[...].astype(BF16)
    dn_ref[...] = dot(dkvl_ref[...], wqkv[:, D:], NT)
    emb_ref[...] = dot(quant[...], lemb[...], TN) + row_of(biases, 6)

    def latent(r, carry):
        gain_sum, off_sum, embed_sum = carry
        at = chunk(r, 64)
        upstream = dn_ref[at, :]
        down, along = norm_back(emb_ref[at, :], gain0, upstream)
        low = down.astype(BF16)
        din_ref[at, :] = low
        return gain_sum + fold(along), off_sum + fold(upstream), embed_sum + fold(low.astype(F32))

    sums = lax.fori_loop(0, LROWS // 64, latent, (zero, zero, zero))
    embed_grad = din_ref[...]
    code_out[...] = dot(lemb[...], embed_grad, NT)
    sm_out[0:1, :] = col_sum(sums[0])
    sm_out[1:2, :] = col_sum(sums[1])
    sm_out[2:3, :] = jnp.zeros((1, D), F32)
    sm_out[6:7, :] = col_sum(sums[2])
    sm_out[7:8, :] = jnp.zeros((1, D), F32)
    sm_out[8:20, :] = dot(quant[...], embed_grad)
    sm_out[20:, :] = jnp.zeros((4, D), F32)
    for image in range(IMGS):
        for b in range(D // 128):
            cols = slice(b * 128, (b + 1) * 128)
            dq_ref[image * SLOTS : (image + 1) * SLOTS, cols] = (
                (dqt_ref[image, cols, :] * 0.125).T.astype(BF16)
            )
    dkv_ref[:, :D] = dk_ref[...].astype(BF16)
    dkv_ref[:, D:] = dv_ref[...].astype(BF16)
    sm_out[4:5, :] = col_sum(fold(dq_ref[...].astype(F32)))
    sm_out[5:6, :] = col_sum(fold(dv_ref[...]) + fold(dvl_ref[...]))


def dec_weights(
    info, dq_ref, dkv_ref, dkvl_ref, dbr_ref, sm_in, dmid, attn, tn, xn, ln, x_in, pos, wqkv,
    gains, biases,
    keep_out, send_out, sm_out,
    w_ref, dn_ref, din_ref, tab_ref,
):
    gain0 = row_of(gains, 0)
    token = row_of(biases, 7)
    zero = jnp.zeros((8, D), F32)
    w_ref[:, :D] = dot(attn[...], dbr_ref[...], TN)
    for z in range(4):
        put_pieces(
            info, keep_out, send_out, 0, z, w_ref[z * 128 : (z + 1) * 128, :D], 16, 128
        )
    w_ref[:, :D] = dot(xn[...], dq_ref[...], TN)
    w_ref[:, D:] = dot(tn[...], dkv_ref[...], TN) + dot(ln[...], dkvl_ref[...], TN)
    for z in range(4):
        put_pieces(
            info, keep_out, send_out, 16, z, w_ref[z * 128 : (z + 1) * 128, :], 16, 384
        )
    dn_ref[:ROWS, :] = dot(dq_ref[...], wqkv[:, :D], NT)

    def own(r, carry):
        gain_sum, off_sum = carry
        at = chunk(r, 64)
        upstream = dn_ref[at, :]
        down, along = norm_back(token + x_in[at, :].astype(F32), gain0, upstream)
        din_ref[at, :] = (dmid[at, :] + down).astype(BF16)
        return gain_sum + fold(along), off_sum + fold(upstream)

    sums = lax.fori_loop(0, ROWS // 64, own, (zero, zero))
    for r in range(4):
        at = slice(r * 256, (r + 1) * 256)
        dn_ref[at, :] = dot(dkv_ref[at, :], wqkv[:, D:], NT)
    lane = lax.broadcasted_iota(jnp.int32, (1, SLOTS), 1)
    place = [own_positions(info, image, lane) for image in range(IMGS)]

    def scatter(r):
        at = chunk(r, 256)
        index = lax.broadcasted_iota(jnp.int32, (256, SLOTS), 0) + r * 256
        total = jnp.zeros((256, D), F32)
        for image in range(IMGS):
            hot = jnp.where(place[image] == index, 1.0, 0.0).astype(BF16)
            total = total + dot(hot, din_ref[image * SLOTS : (image + 1) * SLOTS, :])
        tab_ref[at, :] = total

    loop(4, scatter)

    def table(r, carry):
        gain_sum, off_sum, mask_sum = carry
        at = chunk(r, 64)
        upstream = dn_ref[at, :]
        down, along = norm_back(token + pos[at, :].astype(F32), gain0, upstream)
        rows = tab_ref[at, :] + down
        tab_ref[at, :] = rows
        return gain_sum + fold(along), off_sum + fold(upstream), mask_sum + fold(rows)

    gain_sum, off_sum, mask_sum = lax.fori_loop(0, TABLE // 64, table, sums + (zero,))
    for z in range(4):
        put_pieces(
            info, keep_out, send_out, 64, z, tab_ref[z * 256 : (z + 1) * 256, :], 32, 128
        )
    sm_out[...] = sm_in[...]
    sm_out[0:1, :] = sm_in[0:1, :] + col_sum(gain_sum)
    sm_out[1:2, :] = sm_in[1:2, :] + col_sum(off_sum)
    sm_out[2:3, :] = col_sum(mask_sum)


def enc_mid(
    info, parts0, parts1, parts2, parts3, latents, wo, win, wout, gains, biases, hbias, proj, pbias, quant,
    attn_out, mid_out, hn_out, act_out, slope_out, final_out, post_out, diff_out, lse_out,
    ot_ref, acc_ref,
):
    logs = []
    for part in (parts0, parts1, parts2, parts3):
        logs.append(
            part[D : D + 8, :].astype(F32)
            + part[D + 8 : D + 16, :].astype(F32)
            + part[D + 16 : D + 24, :].astype(F32)
        )
    top = functools.reduce(jnp.maximum, logs)
    log_total = top + jnp.log(sum(jnp.exp(rows - top) for rows in logs))
    lse_out[...] = log_total
    weights = [jnp.exp(rows - log_total) for rows in logs]
    for h in range(HEADS):
        at = slice(h * HD, (h + 1) * HD)
        ot_ref[at, :] = sum(
            part[at, :].astype(F32) * weight[h : h + 1, :]
            for part, weight in zip((parts0, parts1, parts2, parts3), weights)
        )
    for b in range(D // 128):
        cols = slice(b * 128, (b + 1) * 128)
        attn_out[:, cols] = ot_ref[cols, :].T.astype(BF16)
    acc_ref[...] = dot(attn_out[...], wo[...]) + row_of(biases, 2)
    gain1, off1 = row_of(gains, 1), row_of(biases, 3)
    gain2, off2 = row_of(gains, 2), row_of(biases, 5)

    def mid_norm(r):
        at = chunk(r, 64)
        values = acc_ref[at, :] + latents[at, :].astype(F32)
        mid_out[at, :] = values
        hn_out[at, :] = norm_rows(values, gain1, off1).astype(BF16)
        acc_ref[at, :] = values + row_of(biases, 4)

    loop(LROWS // 64, mid_norm)

    def feed(j):
        cols = chunk(j, D)
        pre = dot(hn_out[...], win[:, cols]) + hbias[cols].astype(F32).reshape(1, D)
        act, slope = gelu_parts(pre)
        low = act.astype(BF16)
        act_out[:, cols] = low
        slope_out[:, cols] = slope
        acc_ref[...] += dot(low, wout[cols, :])

    loop(FF // D, feed)

    def post_norm(r):
        at = chunk(r, 64)
        values = acc_ref[at, :]
        final_out[at, :] = values
        post_out[at, :] = norm_rows(values, gain2, off2).astype(BF16)

    loop(LROWS // 64, post_norm)
    same = lax.broadcasted_iota(jnp.int32, (12, 12), 0) == lax.broadcasted_iota(
        jnp.int32, (12, 12), 1
    )
    shift_col = jnp.sum(jnp.where(same, pbias[...].astype(F32).reshape(1, 12), 0.0), -1, keepdims=True)
    code = dot(proj[...], post_out[...], NT) + shift_col
    diff_out[...] = code - quant[...].astype(F32)


def enc_mlp_back(
    info, code0, code1, code2, code3, diff, post, final, mid, hn, act, slope, attn, wo, win, wout, gains, proj,
    keep_out, send_out, da_out, dmid_out, sm_out,
    dy_ref, dn_ref, dfin_ref, dpre_ref, dbr_ref,
):
    zero = jnp.zeros((8, D), F32)
    gain1, gain2 = row_of(gains, 1), row_of(gains, 2)
    code_grad = code0[...] + code1[...] + code2[...] + code3[...] + 2.0 * COMMIT * diff[...]
    low = code_grad.astype(BF16)
    sm_out[16:28, :] = dot(low, post[...]) * SHARE
    sm_out[28:40, :] = jnp.broadcast_to(
        jnp.sum(low.astype(F32), -1, keepdims=True) * SHARE, (12, D)
    )
    loss = (1.0 + COMMIT) * jnp.sum(diff[...] * diff[...]) * SHARE
    sm_out[40:48, :] = jnp.full((8, D), loss, F32)
    dn_ref[...] = dot(low, proj[...], TN)

    def post_back(r, carry):
        gain_sum, off_sum, out_sum = carry
        at = chunk(r, 64)
        upstream = dn_ref[at, :]
        down, along = norm_back(final[at, :], gain2, upstream)
        dfin_ref[at, :] = down
        branch = down.astype(BF16)
        dy_ref[at, :] = branch
        return gain_sum + fold(along), off_sum + fold(upstream), out_sum + fold(branch.astype(F32))

    sums = lax.fori_loop(0, LROWS // 64, post_back, (zero, zero, zero))
    for n in range(3):
        sm_out[n : n + 1, :] = col_sum(sums[n]) * SHARE
    dn_ref[...] = jnp.zeros_like(dn_ref)

    def feed(j):
        cols = chunk(j, D)
        act_grad = dot(dy_ref[...], wout[cols, :], NT)
        pre_grad = (act_grad * slope[:, cols]).astype(BF16)
        dpre_ref[:, cols] = pre_grad
        sm_out[pl.ds(8 + j, 1), :] = col_sum(pre_grad.astype(F32)) * SHARE
        dn_ref[...] += dot(pre_grad, win[:, cols], NT)

    loop(FF // D, feed)
    mine = chunk(info[7], D)
    put_pieces(
        info, keep_out, send_out, 0, None, dot(hn[...], dpre_ref[:, mine], TN), 64, 128
    )
    put_pieces(
        info, keep_out, send_out, 64, None, dot(act[:, mine], dy_ref[...], TN), 64, 128
    )

    def mid_back(r, carry):
        gain_sum, off_sum, out_sum = carry
        at = chunk(r, 64)
        upstream = dn_ref[at, :]
        down, along = norm_back(mid[at, :], gain1, upstream)
        total = dfin_ref[at, :] + down
        dmid_out[at, :] = total
        branch = total.astype(BF16)
        dbr_ref[at, :] = branch
        return gain_sum + fold(along), off_sum + fold(upstream), out_sum + fold(branch.astype(F32))

    sums = lax.fori_loop(0, LROWS // 64, mid_back, (zero, zero, zero))
    for n in range(3):
        sm_out[3 + n : 4 + n, :] = col_sum(sums[n]) * SHARE
    sm_out[6:8, :] = jnp.zeros((2, D), F32)
    sm_out[12:16, :] = jnp.zeros((4, D), F32)
    da_out[...] = dot(dbr_ref[...], wo[...], NT).astype(BF16)
    own = attn[:, chunk(info[7], 128)]
    put_pieces(info, keep_out, send_out, 128, None, dot(own, dbr_ref[...], TN), 16, 128)


def enc_back(
    info, da, attn, lse, kv, lqkv, np_in, nl, patches, latents, wqkv, gains, codes, diff,
    sm_mlp, sm_front, sm_dec,
    keep_out, send_out, patch_out, lat_out,
    bias_ref, k_ref, v_ref, kt_ref, dqt_ref, dkv_ref, dlat_ref, w_ref, dn_ref, sm_ref,
):
    zero = jnp.zeros((8, D), F32)
    gain0 = row_of(gains, 0)
    enc_bias(info, bias_ref)
    for image in range(IMGS):
        rows = slice(image * SLOTS, (image + 1) * SLOTS)
        lat_at = slice(image * LAT, (image + 1) * LAT)
        for g in range(2):
            cols = slice(g * GW, (g + 1) * GW)
            enc_keys(kv, lqkv, image, g, k_ref, v_ref, None, kt_ref)
            query_stack = head_stack(lqkv[lat_at, cols] * jnp.asarray(0.125, BF16), LAT)
            out_grad = da[lat_at, cols]
            out_stack = head_stack(out_grad, LAT)
            grad_t = out_grad.astype(F32).T
            out_t = attn[lat_at, cols].astype(F32).T
            inner = jnp.concatenate(
                [
                    col_sum(grad_t[h * HD : (h + 1) * HD, :] * out_t[h * HD : (h + 1) * HD, :])
                    for h in range(GROUP)
                ],
                1,
            )
            log_total = jnp.concatenate(
                [lse[g * GROUP + h : g * GROUP + h + 1, lat_at] for h in range(GROUP)], 1
            )
            scores = dot(k_ref[...], query_stack, NT)
            bias = jnp.concatenate([bias_ref[image]] * GROUP, 1)
            probs = jnp.exp(scores + bias - log_total)
            prob_grad = dot(v_ref[...], out_stack, NT)
            low = (probs * (prob_grad - inner)).astype(BF16)
            value_grad = dot(probs.astype(BF16), out_stack).astype(BF16)
            key_grad = dot(low, query_stack).astype(BF16)
            dkv_ref[rows, cols] = key_grad[:SLOTS, :]
            dkv_ref[rows, D + g * GW : D + (g + 1) * GW] = value_grad[:SLOTS, :]
            dlat_ref[lat_at, D + g * GW : D + (g + 1) * GW] = key_grad[SLOTS:, :]
            dlat_ref[lat_at, 2 * D + g * GW : 2 * D + (g + 1) * GW] = value_grad[SLOTS:, :]
            for h in range(GROUP):
                part = dot(kt_ref[h * HD : (h + 1) * HD, :], low[:, h * LAT : (h + 1) * LAT])
                at = g * GW + h * HD
                dqt_ref[at : at + HD, lat_at] = part * 0.125
    for b in range(D // 128):
        cols = slice(b * 128, (b + 1) * 128)
        dlat_ref[:, cols] = dqt_ref[cols, :].T.astype(BF16)
    dn_ref[...] = dot(dkv_ref[...], wqkv[:, D:], NT)

    def patch_back(r, carry):
        gain_sum, off_sum = carry
        at = chunk(r, 64)
        upstream = dn_ref[at, :]
        down, along = norm_back(patches[at, :].astype(F32), gain0, upstream)
        patch_out[at, :] = down
        return gain_sum + fold(along), off_sum + fold(upstream)

    sums = lax.fori_loop(0, ROWS // 64, patch_back, (zero, zero))
    dn_ref[:LROWS, :] = dot(dlat_ref[...], wqkv[...], NT)

    def lat_back(r, carry):
        gain_sum, off_sum = carry
        at = chunk(r, 64)
        upstream = dn_ref[at, :]
        down, along = norm_back(latents[at, :].astype(F32), gain0, upstream)
        lat_out[at, :] = down.astype(BF16)
        return gain_sum + fold(along), off_sum + fold(upstream)

    sums = lax.fori_loop(0, LROWS // 64, lat_back, sums)
    w_ref[:, :D] = dot(nl[...], dlat_ref[:, :D], TN)
    w_ref[:, D:] = dot(nl[...], dlat_ref[:, D:], TN) + dot(np_in[...], dkv_ref[...], TN)
    for z in range(4):
        put_pieces(
            info, keep_out, send_out, 0, z, w_ref[z * 128 : (z + 1) * 128, :], 16, 384
        )
    sm_ref[0:1, :] = col_sum(sums[0])
    sm_ref[1:2, :] = sm_mlp[3:4, :]
    sm_ref[2:3, :] = sm_mlp[0:1, :]
    sm_ref[3:4, :] = col_sum(sums[1])
    sm_ref[4:5, :] = col_sum(
        fold(dkv_ref[:, D:].astype(F32)) + fold(dlat_ref[:, 2 * D :].astype(F32))
    )
    sm_ref[5:6, :] = sm_mlp[5:6, :]
    sm_ref[6:7, :] = sm_mlp[4:5, :]
    sm_ref[7:8, :] = sm_mlp[2:3, :]
    sm_ref[8:9, :] = sm_mlp[1:2, :]
    sm_ref[9:10, :] = col_sum(fold(dlat_ref[:, :D].astype(F32)))
    sm_ref[10:14, :] = sm_mlp[8:12, :]
    sm_ref[14:26, :] = sm_mlp[16:28, :]
    pick = lax.broadcasted_iota(jnp.int32, (12, D), 0) == lax.broadcasted_iota(
        jnp.int32, (12, D), 1
    )
    sm_ref[26:27, :] = col_sum(jnp.where(pick, sm_mlp[28:40, :], 0.0))
    sm_ref[27:28, :] = sm_mlp[40:41, :]
    sm_ref[28:40, :] = sm_dec[8:20, :]
    sm_ref[40:41, :] = sm_dec[0:1, :]
    sm_ref[41:42, :] = sm_front[0:1, :]
    sm_ref[42:43, :] = sm_dec[1:2, :]
    sm_ref[43:44, :] = sm_dec[4:5, :]
    sm_ref[44:45, :] = sm_dec[5:6, :]
    sm_ref[45:46, :] = sm_dec[3:4, :]
    sm_ref[46:47, :] = sm_front[1:2, :]
    sm_ref[47:48, :] = sm_front[2:3, :]
    sm_ref[48:49, :] = sm_dec[6:7, :]
    sm_ref[49:50, :] = sm_dec[2:3, :]
    sm_ref[50:54, :] = sm_front[4:8, :]
    sm_ref[54:, :] = jnp.zeros((SMALL - 54, D), F32)
    token = lax.broadcasted_iota(jnp.int32, (12, LROWS), 1) % LAT
    mine = jnp.where(token // 32 == info[7], -2.0 * diff[...], 0.0).astype(BF16)
    book = dot(mine, code_onehot(codes, 8 * D), NT)
    for n in range(8):
        at = CODE_ROW + 16 * n
        sm_ref[at : at + 12, :] = book[:, n * D : (n + 1) * D]
    mine_first = info[4] == 0
    for p in range(PIECES):
        z, q = p // 32, p % 32
        if q >= 16:
            continue
        base = turn(z, info[7]) * 16
        own = base + plane_index(info, info[4], q // 4, q % 4)
        away = base + plane_index(info, 1 - info[4], q // 4, q % 4)
        mine = small_piece(sm_ref, p)
        other = small_piece(sm_ref, p + 16)
        keep_out[own, 48:64, :] = jnp.where(mine_first, mine, other)
        send_out[away, 48:64, :] = jnp.where(mine_first, other, mine)


def small_piece(sm_ref, p):
    if p >= SMALL // 4:
        return jnp.zeros((16, 128), BF16)
    row, col = (p // 4) * 16, (p % 4) * 128
    return sm_ref[row : row + 16, col : col + 128].astype(BF16)


def add_all(info, *refs):
    *parts, out = refs

    def one(n):
        values = [part[n].astype(F32) for part in parts]
        if len(values) == 2:
            total = values[0] + values[1]
        else:
            total = (values[0] + values[2]) + (values[1] + values[3])
        out[n] = total.astype(BF16)

    loop(out.shape[0], one)


def join(info, *refs):
    mlp, rest, plane, qkv, out = refs[0], refs[1], refs[2:4], refs[4:8], refs[8]

    def one(n):
        out[n, 0:128, :] = mlp[n]
        out[n, 128:224, :] = rest[n]
        out[n, 224:368, :] = sum(part[n].astype(F32) for part in plane).astype(BF16)
        out[n, 368:432, :] = sum(part[n].astype(F32) for part in qkv).astype(BF16)

    loop(16, one)


def gate(info, *refs):
    pass


def stack(info, *refs):
    *parts, out = refs
    for n, part in enumerate(parts):
        out[4 * n : 4 * n + 4] = part[...]


def unpack(info, *refs):
    src, outs, scratch = refs[:10], refs[10:31], refs[31:]
    (
        dec_in, dec_wout, dec_out, dec_qkv, pos, enc_in, enc_wout, enc_out, enc_qkv,
        gains_out, biases_out, query_out, hidden_out, proj_out, pbias_out, loss_out, embed_out,
        dgains_out, dbiases_out, dhidden_out, book_out,
    ) = outs
    bufs, sm_ref, sems = scratch[:9], scratch[9], scratch[10]
    c0, y0, x0, z0 = coords(info)

    def pieces():
        for s in range(10):
            core = c0 if s < 5 else 1 - c0
            first = core == 0
            step = (0, 1, 3, 2, 2)[s % 5]
            for n in range(16 if s % 5 < 3 else 8):
                high, low = (n + (8 if s % 5 == 4 else 0)) // 4, n % 4
                z = jnp.where(first, (z0 + step) & 3, (z0 + high) & 3)
                y = jnp.where(first, (y0 + high) & 3, low)
                x = jnp.where(first, low, (x0 + step) & 3)
                e = (y & 1) * 4 + x
                f = core * 2 + lax.shift_right_logical(y, 1)
                yield s, n, z, e, f, z * 32 + core * 16 + y * 4 + x

    def take(s, n, offset, dst, row, col, rows, cols):
        for b in range(cols // 128):
            at = offset + b * rows
            lanes = pl.ds(pl.multiple_of(col + b * 128, 128), 128)
            dst[pl.ds(pl.multiple_of(row, 16), rows), lanes] = src[s][n, at : at + rows, :].astype(
                F32
            )

    def z_rows(rows, cols):
        return lambda z, e, f: ((z * 8 + e) * rows, f * cols)

    def z_cols(z, e, f):
        return e * 64, z * D + f * 128

    plan = (
        (0, z_cols, 64, 128), (64, z_rows(64, 128), 64, 128), (128, z_rows(16, 128), 16, 128),
        (144, z_rows(16, 384), 16, 384), (192, z_rows(32, 128), 32, 128),
        (224, z_cols, 64, 128), (288, z_rows(64, 128), 64, 128), (352, z_rows(16, 128), 16, 128),
        (368, z_rows(16, 384), 16, 384),
    )
    copies = []
    for k, (offset, place, rows, cols) in enumerate(plan):
        for s, n, z, e, f, p in pieces():
            row, col = place(z, e, f)
            take(s, n, offset, bufs[k], row, col, rows, cols)
        copy = pltpu.make_async_copy(bufs[k], outs[k], sems.at[k])
        copy.start()
        copies.append(copy)
    for s, n, z, e, f, p in pieces():

        def small(s=s, n=n, p=p):
            row = lax.shift_right_logical(p, 2) * 16
            take(s, n, 416, sm_ref, row, (p & 3) * 128, 16, 128)

        pl.when(p < SMALL // 4)(small)
    gains_out[...] = sm_ref[0:3, :]
    biases_out[...] = sm_ref[3:9, :]
    query_out[...] = sm_ref[9:10, :]
    for n in range(4):
        hidden_out[:, n * D : (n + 1) * D] = sm_ref[10 + n : 11 + n, :]
        dhidden_out[:, n * D : (n + 1) * D] = sm_ref[50 + n : 51 + n, :]
    proj_out[...] = sm_ref[14:26, :]
    pbias_out[...] = sm_ref[26:27, :128]
    loss_out[...] = sm_ref[27:28, :128]
    embed_out[...] = sm_ref[28:40, :]
    dgains_out[...] = sm_ref[40:42, :]
    dbiases_out[...] = sm_ref[42:50, :]
    for n in range(8):
        at = CODE_ROW + 16 * n
        book_out[:, n * D : (n + 1) * D] = sm_ref[at : at + 12, :]
    for copy in copies:
        copy.wait()


def size_of(shape, kind):
    total = jnp.dtype(kind).itemsize
    for n in shape:
        total *= n
    return total


def call(
    kernel, name, outs, scratch, info, *args, flops=0, after=(), forward=(), hbm_outs=0, spare=8
):
    out_shape = [jax.ShapeDtypeStruct(shape, kind) for shape, kind in outs]
    moved = sum(a.size * a.dtype.itemsize for a in args) + sum(
        o.size * o.dtype.itemsize for o in out_shape
    )
    held = sum(a.size * a.dtype.itemsize for a in args)
    held += sum(o.size * o.dtype.itemsize for o in out_shape[hbm_outs:])
    held += sum(size_of(*item) for item in scratch if isinstance(item, tuple))
    vmem = pl.BlockSpec(memory_space=pltpu.VMEM)
    anywhere = pl.BlockSpec(memory_space=pl.ANY)
    count, others_in, own_out = 2 + len(args), len(after) + len(forward), len(outs)

    def body(*refs):
        last = count + others_in + own_out
        kernel(
            Info(*refs[:2]),
            *refs[2:count],
            *refs[count + others_in : last],
            *refs[last + len(forward) :],
        )

    first = count + len(after)
    return pl.pallas_call(
        body,
        out_shape=out_shape + [jax.ShapeDtypeStruct(a.shape, a.dtype) for a in forward],
        in_specs=[pl.BlockSpec(memory_space=pltpu.SMEM)] * 2
        + [vmem] * len(args)
        + [anywhere] * others_in,
        out_specs=[anywhere] * hbm_outs + [vmem] * (own_out - hbm_outs) + [anywhere] * len(forward),
        scratch_shapes=[
            item if not isinstance(item, tuple) else pltpu.VMEM(*item) for item in scratch
        ],
        input_output_aliases={first + n: own_out + n for n in range(len(forward))},
        compiler_params=pltpu.CompilerParams(
            vmem_limit_bytes=min(VMEM_LIMIT, held + spare * 1024 * 1024)
        ),
        cost_estimate=pl.CostEstimate(flops=flops, bytes_accessed=moved, transcendentals=0),
        name=name,
    )(*info, *args, *after, *forward)


def shift(value, axis, by):
    return lax.ppermute(value, axis, [(i, (i + by) % 4) for i in range(4)])


def shift_by_core(value, axes, by):
    sizes = {"y": 4, "x": 4, "core": 2, "z": 4}
    pairs = []
    for start in range(128):
        at = {"z": start % 4, "core": start // 4 % 2, "x": start // 8 % 4, "y": start // 32}
        to = dict(at)
        axis = axes[at["core"]]
        to[axis] = (to[axis] + by) % sizes[axis]
        pairs.append((start, ((to["y"] * 4 + to["x"]) * 2 + to["core"]) * 4 + to["z"]))
    return lax.ppermute(value, ("y", "x", "core", "z"), pairs)


def swap(value):
    return lax.ppermute(value, "core", [(0, 1), (1, 0)])


def scattered(value, move):
    return [value[0]] + [move(value[by], by) for by in (1, 2, 3)]


def others(value, move):
    return [value] + [move(value, -by) for by in (1, 2, 3)]


def around(value, move):
    one, three = move(value, -1), move(value, 1)
    half = value.shape[0] // 2
    return [value, one, three, move(one[:half], -1), move(three[half:], 1)]


def along(axis):
    return lambda value, by: shift(value, axis, by)


def along_by_core(*axes):
    return lambda value, by: shift_by_core(value, axes, by)


def per_device(
    enc_patches, enc_latents, resolution, lengths, codes, enc_qkv, enc_out, enc_mlp_in, enc_mlp_out,
    enc_gains, enc_biases, enc_query_bias, enc_hidden_bias, latent_proj, latent_bias, codebook,
    latent_embed, pos_table, dec_qkv, dec_out, dec_mlp_in, dec_mlp_out, dec_gains, dec_biases,
    dec_hidden_bias, out_cot,
):
    info = (lengths, resolution)
    patches = enc_patches.reshape(ROWS, D)
    latents = enc_latents.reshape(LROWS, D)
    cot = out_cot.reshape(ROWS, D)
    entries = codebook.shape[1]

    enc_norm, lat_norm, kv, lqkv, part, quant = call(
        enc_front, "enc_front",
        [((ROWS, D), BF16), ((LROWS, D), BF16), ((ROWS, 2 * D), BF16), ((LROWS, 3 * D), BF16),
         ((D + 32, LROWS), BF16), ((12, LROWS), BF16)],
        [((IMGS, OWN_KEYS, LAT), F32), ((OWN_KEYS, GW), BF16), ((GW, OWN_KEYS), BF16)],
        info, patches, latents, enc_qkv, enc_gains, enc_biases, enc_query_bias,
        codes, codebook, flops=2_000_000_000, spare=60,
    )
    parts = others(part, along("z"))
    (result, mlp_keep, mlp_send, dmid, attn, tab_norm, own_norm, emb_norm, own_pos, sm_front,
     dq, dkv, dkvl, branch, code_part, sm_back) = call(
        dec_front, "dec_front",
        [((ROWS, D), BF16), ((64, 128, 128), BF16), ((64, 128, 128), BF16), ((ROWS, D), F32),
         ((ROWS, D), BF16), ((TABLE, D), BF16), ((ROWS, D), BF16), ((LROWS, D), BF16),
         ((ROWS, D), BF16), ((8, D), F32),
         ((ROWS, D), BF16), ((TABLE, 2 * D), BF16), ((LROWS, 2 * D), BF16), ((ROWS, D), BF16),
         ((12, LROWS), F32), ((24, D), F32)],
        [((4, KEYS, GROUP * SLOTS), BF16), ((4, GROUP, SLOTS), F32), ((ROWS, D), BF16),
         ((IMGS, KEYS, D), BF16), ((IMGS, KEYS, D), BF16),
         ((IMGS, KEYS, LAT), F32), ((IMGS, D, KEYS), BF16), ((IMGS, D, SLOTS), F32),
         ((ROWS, D), F32), ((ROWS, D), BF16), ((ROWS, D), BF16), ((ROWS, D), F32), ((ROWS, D), F32),
         ((ROWS, D), BF16), ((ROWS, D), BF16),
         ((ROWS, D), BF16), ((IMGS, D, SLOTS), F32), ((TABLE, D), F32), ((TABLE, D), F32),
         ((LROWS, D), F32), ((LROWS, D), F32), ((IMGS, D, KEYS), BF16),
         ((KEYS, GROUP * SLOTS), BF16), ((LROWS, D), F32), ((LROWS, D), F32), ((LROWS, D), BF16)],
        info, pos_table, quant, latent_embed, dec_qkv, dec_out, dec_mlp_in, dec_mlp_out, dec_gains,
        dec_biases, dec_hidden_bias, cot, flops=20_000_000_000, spare=60,
    )
    mlp_send, code_part = call(
        gate, "gate", [], [], info, after=parts + [sm_back], forward=[mlp_send, code_part]
    )
    mlp_other = swap(mlp_send)
    code_parts = others(code_part, along("z"))
    enc_attn, mid, hidden_norm, act, slope, final, post, diff, lse = call(
        enc_mid, "enc_mid",
        [((LROWS, D), BF16), ((LROWS, D), F32), ((LROWS, D), BF16), ((LROWS, FF), BF16),
         ((LROWS, FF), F32), ((LROWS, D), F32), ((LROWS, D), BF16), ((12, LROWS), F32),
         ((HEADS, LROWS), F32)],
        [((D, LROWS), F32), ((LROWS, D), F32)],
        info, *parts, latents, enc_out, enc_mlp_in, enc_mlp_out, enc_gains, enc_biases,
        enc_hidden_bias, latent_proj, latent_bias, quant,
        flops=1_500_000_000, after=[mlp_send], spare=60,
    )
    dec_mlp, *code_parts = call(
        add_all, "sum_mlp_core", [((64, 128, 128), BF16)], [], info, mlp_keep, mlp_other,
        after=[lse], forward=code_parts,
    )
    mlp_parts = scattered(dec_mlp.reshape(4, 16, 128, 128), along("z"))
    rest_keep, rest_send, sm_dec = call(
        dec_weights, "dec_weights",
        [((64, 96, 128), BF16), ((64, 96, 128), BF16), ((24, D), F32)],
        [((D, 3 * D), F32), ((TABLE, D), F32), ((ROWS, D), BF16), ((TABLE, D), F32)],
        info, dq, dkv, dkvl, branch, sm_back, dmid, attn, tab_norm, own_norm, emb_norm, own_pos,
        pos_table, dec_qkv, dec_gains, dec_biases, flops=6_000_000_000, after=[dec_mlp],
    )
    dec_mlp, rest_send = call(
        add_all, "sum_mlp_z", [((16, 128, 128), BF16)], [], info, *mlp_parts, after=[rest_keep],
        forward=[rest_send],
    )
    rest_other = swap(rest_send)
    plane_keep, plane_send, enc_da, enc_dmid, sm_mlp = call(
        enc_mlp_back, "enc_mlp_back",
        [((16, 144, 128), BF16), ((16, 144, 128), BF16), ((LROWS, D), BF16), ((LROWS, D), F32),
         ((48, D), F32)],
        [((LROWS, D), BF16), ((LROWS, D), F32), ((LROWS, D), F32), ((LROWS, FF), BF16),
         ((LROWS, D), BF16)],
        info, *code_parts, diff, post, final, mid, hidden_norm, act, slope, enc_attn, enc_out,
        enc_mlp_in, enc_mlp_out, enc_gains, latent_proj, flops=2_500_000_000, after=[dec_mlp],
    )
    dec_rest, plane_send = call(
        add_all, "sum_rest_core", [((64, 96, 128), BF16)], [], info, rest_keep, rest_other,
        after=[plane_keep], forward=[plane_send],
    )
    rest_parts = scattered(dec_rest.reshape(4, 16, 96, 128), along("z"))
    plane_other = swap(plane_send)
    qkv_keep, qkv_send, grad_patches, lat_part = call(
        enc_back, "enc_back",
        [((64, 64, 128), BF16), ((64, 64, 128), BF16), ((ROWS, D), F32), ((LROWS, D), BF16)],
        [((IMGS, OWN_KEYS, LAT), F32), ((OWN_KEYS, GW), BF16), ((OWN_KEYS, GW), BF16),
         ((GW, OWN_KEYS), BF16), ((D, LROWS), F32), ((ROWS, 2 * D), BF16), ((LROWS, 3 * D), BF16),
         ((D, 3 * D), F32), ((ROWS, D), F32), ((SMALL, D), F32)],
        info, enc_da, enc_attn, lse, kv, lqkv, enc_norm, lat_norm, patches, latents, enc_qkv,
        enc_gains, codes, diff, sm_mlp, sm_front, sm_dec, flops=3_000_000_000, after=[dec_rest],
    )

    dec_rest, qkv_send, plane_other = call(
        add_all, "sum_rest_z", [((16, 96, 128), BF16)], [], info, *rest_parts, after=[qkv_keep],
        forward=[qkv_send, plane_other],
    )
    (enc_qkv_sum,) = call(
        add_all, "sum_qkv_core", [((64, 64, 128), BF16)], [], info, qkv_keep, swap(qkv_send),
    )
    qkv_parts = scattered(enc_qkv_sum.reshape(4, 16, 64, 128), along("z"))
    main, lat_part = call(
        join, "join", [((16, 432, 128), BF16)], [], info, dec_mlp, dec_rest, plane_keep,
        plane_other, *qkv_parts, forward=[lat_part],
    )
    lat_parts = others(lat_part, along("z"))
    main = scattered(main.reshape(4, 4, 432, 128), along_by_core("y", "x"))
    main, *lat_parts = call(
        add_all, "sum_first", [((4, 432, 128), BF16)], [], info, *main, forward=lat_parts
    )
    main = others(main, along_by_core("x", "y"))
    lat_total = sum(part.astype(F32) for part in lat_parts)
    grad_latents = (enc_dmid + lat_total).reshape(IMGS, LAT, D)
    (main,) = call(add_all, "sum_second", [((4, 432, 128), BF16)], [], info, *main)
    main = others(main, along_by_core("y", "z"))
    (main,) = call(stack, "stack", [((16, 432, 128), BF16)], [], info, *main)
    main = around(main, along_by_core("z", "x"))
    main = main + [swap(block) for block in main]

    wide = [(D, FF), (FF, D), (D, D), (D, 3 * D), (TABLE, D), (D, FF), (FF, D), (D, D), (D, 3 * D)]
    small = [(3, D), (6, D), (1, D), (1, FF), (12, D), (1, 128), (1, 128), (12, D), (2, D), (8, D),
             (1, FF), (12, entries)]
    (dec_in_grad, dec_wout_grad, dec_out_grad, dec_qkv_grad, pos_grad,
     enc_in_grad, enc_wout_grad, enc_out_grad, enc_qkv_grad, gains_grad, biases_grad, query_grad,
     hidden_grad, proj_grad, pbias_grad, loss, embed_grad, dec_gains_grad, dec_biases_grad,
     dec_hidden_grad, book_grad) = call(
        unpack, "unpack", [(shape, F32) for shape in wide + small],
        [(shape, F32) for shape in wide] + [((SMALL, D), F32), pltpu.SemaphoreType.DMA((9,))],
        info, *main, hbm_outs=9,
    )
    images = IMGS * lax.axis_size(("y", "x", "core"))
    quant_loss = loss[0, 0] / (images * LAT * 12)
    return (
        result.reshape(IMGS, SLOTS, D),
        grad_patches.reshape(IMGS, SLOTS, D),
        grad_latents,
        quant_loss,
        enc_qkv_grad,
        enc_out_grad,
        enc_in_grad,
        enc_wout_grad,
        gains_grad,
        biases_grad,
        query_grad.reshape(D),
        hidden_grad.reshape(FF),
        proj_grad,
        pbias_grad[0, :12],
        book_grad,
        embed_grad,
        pos_grad,
        dec_qkv_grad,
        dec_out_grad,
        dec_in_grad,
        dec_wout_grad,
        dec_gains_grad,
        dec_biases_grad,
        dec_hidden_grad.reshape(FF),
    )


def solution(mesh):
    devices = mesh.devices.reshape(4, 4, 2, 4)
    fine = Mesh(devices, ("y", "x", "core", "z"))
    dp = ("y", "x", "core")
    whole = P()
    images = P(dp, "z", None)
    placed = (images, P(dp, None, None), P(dp), P(dp), P(dp, None)) + (whole,) * 20 + (images,)
    return jax.shard_map(
        per_device,
        mesh=fine,
        in_specs=placed,
        out_specs=(images, images, P(dp, None, None)) + (whole,) * 21,
        check_vma=False,
    )
```

```python
import functools

import jax
import jax.numpy as jnp
from jax import lax
from jax.experimental import pallas as pl
from jax.experimental.pallas import tpu as pltpu
from jax.sharding import Mesh
from jax.sharding import PartitionSpec as P

F32 = jnp.float32
BF16 = jnp.bfloat16
EPS = 1e-06
COMMIT = 0.25
NEG = -1e30
D = 512
HEADS = 8
HD = 64
FF = 2048
GROUP = 4
GW = GROUP * HD
LAT = 128
IMGS = 2
SLOTS = 256
ROWS = IMGS * SLOTS
LROWS = IMGS * LAT
TABLE = 1024
KEYS = TABLE + LAT
OWN_KEYS = SLOTS + LAT
PIECES = 128
SHARE = 0.25
SMALL = 192
CODE_ROW = 64

NN = (((1,), (0,)), ((), ()))
NT = (((1,), (1,)), ((), ()))
TN = (((0,), (0,)), ((), ()))
VMEM_LIMIT = 60 * 1024 * 1024


def dot(left, right, dims=NN):
    return lax.dot_general(left, right, dims, preferred_element_type=F32)


def row_of(ref, index):
    return ref[index : index + 1, :].astype(F32)


def norm_parts(values):
    centre = values - jnp.mean(values, -1, keepdims=True)
    scale = lax.rsqrt(jnp.mean(centre * centre, -1, keepdims=True) + EPS)
    return centre * scale, scale


def norm_rows(values, gain, offset):
    return norm_parts(values)[0] * gain + offset


def norm_back(values, gain, upstream):
    hat, scale = norm_parts(values)
    inner = upstream * gain
    low = jnp.mean(inner, -1, keepdims=True)
    along = jnp.mean(inner * hat, -1, keepdims=True)
    return scale * (inner - low - hat * along), upstream * hat


def fold(values):
    return jnp.sum(values.reshape(values.shape[0] // 8, 8, values.shape[1]), 0)


def col_sum(values):
    return jnp.sum(values, 0, keepdims=True)


def gelu_parts(point):
    size = jnp.abs(point) * 0.7071067811865476
    t = 1.0 / (1.0 + 0.3275911 * size)
    bell = jnp.exp(-0.5 * point * point)
    poly = t * (
        0.254829592
        + t * (-0.284496736 + t * (1.421413741 + t * (-1.453152027 + t * 1.061405429)))
    )
    tail = 0.5 * poly * bell
    cdf = jnp.where(point >= 0, 1.0 - tail, tail)
    return point * cdf, cdf + point * bell * 0.3989422804014327


def loop(count, body, unroll=1):
    def step(index, carry):
        body(index)
        return carry

    lax.fori_loop(0, count, step, 0, unroll=unroll)


def chunk(index, size):
    return pl.ds(pl.multiple_of(index * size, size), size)


def head_stack(block, rows):
    lane = lax.broadcasted_iota(jnp.int32, (rows, GW), 1) // HD
    parts = [jnp.where(lane == h, block, jnp.zeros_like(block)) for h in range(GROUP)]
    return jnp.concatenate(parts, 0)


class Info:
    def __init__(self, lengths, resolution):
        self.lengths, self.resolution = lengths, resolution

    def __getitem__(self, index):
        if isinstance(index, int) and index >= 4:
            return lax.axis_index(("core", "y", "x", "z")[index - 4])
        return self.lengths[index]

    def side(self, image):
        size = self.resolution[image]
        return 3 + jnp.where(size >= 256, 1, 0) + jnp.where(size >= 512, 1, 0)


def coords(info):
    return info[4], info[5], info[6], info[7]


def turn(at, own):
    return (at - own) & 3


def piece_index(info, core, z, y, x):
    c0, y0, x0, z0 = coords(info)
    if z is None:
        return jnp.where(core == 0, turn(y, y0) * 4 + x, turn(x, x0) * 4 + y)
    first = turn(z, z0) * 16 + turn(y, y0) * 4 + x
    second = turn(x, x0) * 16 + turn(z, z0) * 4 + y
    return jnp.where(core == 0, first, second)


def qkv_index(info, core, z, y, x):
    c0, y0, x0, z0 = coords(info)
    first = turn(x, x0) * 16 + turn(y, y0) * 4 + z
    second = turn(y, y0) * 16 + turn(z, z0) * 4 + x
    return jnp.where(core == 0, first, second)


def put_pieces(info, keep, send, offset, z, block, rows, cols, index=piece_index):
    mine_first = info[4] == 0
    for q in range(16):
        y, x = q // 4, q % 4
        own = index(info, info[4], z, y, x)
        away = index(info, 1 - info[4], z, y, x)
        row = (q % 8) * rows
        for b in range(cols // 128):
            col = (q // 8) * cols + b * 128
            at = offset + b * rows
            mine = block[row : row + rows, col : col + 128].astype(BF16)
            col = col + 2 * cols
            other = block[row : row + rows, col : col + 128].astype(BF16)
            keep[own, at : at + rows, :] = jnp.where(mine_first, mine, other)
            send[away, at : at + rows, :] = jnp.where(mine_first, other, mine)


def own_positions(info, image, iota):
    shift = info.side(image)
    side = lax.shift_left(1, shift)
    slot = info[7] * SLOTS + iota
    row = jnp.minimum(lax.shift_right_logical(slot, shift), side - 1)
    col = slot & (side - 1)
    up = lax.shift_right_logical(row * 32, shift)
    across = lax.shift_right_logical(col * 32, shift)
    return up * 32 + across


def table_bias(info, image, shape):
    shift = info.side(image)
    place = lax.broadcasted_iota(jnp.int32, shape, 0)
    gap = 5 - shift
    mask = lax.shift_left(1, gap) - 1
    row = lax.shift_right_logical(place, 5)
    col = place & 31
    slot = lax.shift_left(lax.shift_right_logical(row, gap), shift) + lax.shift_right_logical(
        col, gap
    )
    keep = jnp.logical_and(((row | col) & mask) == 0, slot < info[image])
    return jnp.where(keep, 0.0, NEG)


def code_onehot(codes_ref, entries):
    ids = jnp.concatenate([codes_ref[image : image + 1, :] for image in range(IMGS)], 1)
    entry = lax.broadcasted_iota(jnp.int32, (entries, LROWS), 0)
    return jnp.where(ids == entry, 1.0, 0.0).astype(BF16)


def enc_front(
    info, patches, latents, wqkv, gains, biases, qbias, codes, codebook,
    np_out, nl_out, kv_out, lqkv_out, part_out, quant_out,
    bias_ref, k_ref, vt_ref,
):
    gain, offset = row_of(gains, 0), row_of(biases, 0)
    vbias = row_of(biases, 1)

    def norm_patch(r):
        at = chunk(r, 64)
        np_out[at, :] = norm_rows(patches[at, :].astype(F32), gain, offset).astype(BF16)

    loop(ROWS // 64, norm_patch, 8)

    def norm_lat(r):
        at = chunk(r, 64)
        nl_out[at, :] = norm_rows(latents[at, :].astype(F32), gain, offset).astype(BF16)

    loop(LROWS // 64, norm_lat, 4)
    kv_out[:, :D] = dot(np_out[...], wqkv[:, D : 2 * D]).astype(BF16)
    kv_out[:, D:] = (dot(np_out[...], wqkv[:, 2 * D :]) + vbias).astype(BF16)
    lqkv_out[:, :D] = (dot(nl_out[...], wqkv[:, :D]) + qbias[...].astype(F32).reshape(1, D)).astype(BF16)
    lqkv_out[:, D : 2 * D] = dot(nl_out[...], wqkv[:, D : 2 * D]).astype(BF16)
    lqkv_out[:, 2 * D :] = (dot(nl_out[...], wqkv[:, 2 * D :]) + vbias).astype(BF16)
    quant_out[...] = dot(codebook[...], code_onehot(codes, codebook.shape[1])).astype(BF16)
    enc_bias(info, bias_ref)
    part_out[D:, :] = jnp.zeros((32, LROWS), BF16)
    for image in range(IMGS):
        lat_at = slice(image * LAT, (image + 1) * LAT)
        lane_at = slice(image * LAT, (image + 1) * LAT)
        for g in range(2):
            cols = slice(g * GW, (g + 1) * GW)
            enc_keys(kv_out, lqkv_out, image, g, k_ref, None, vt_ref, None)
            query = lqkv_out[lat_at, cols] * jnp.asarray(0.125, BF16)
            scores = dot(k_ref[...], head_stack(query, LAT), NT)
            bias = bias_ref[image]
            scores = scores + jnp.concatenate([bias] * GROUP, 1)
            top = jnp.max(scores, 0, keepdims=True)
            expo = jnp.exp(scores - top)
            total = col_sum(expo)
            low = expo.astype(BF16)
            log_total = top + jnp.log(total)
            inverse = 1.0 / total
            for h in range(GROUP):
                head = slice(h * LAT, (h + 1) * LAT)
                mixed = dot(vt_ref[h * HD : (h + 1) * HD, :], low[:, head])
                at = g * GW + h * HD
                part_out[at : at + HD, lane_at] = (mixed * inverse[:, head]).astype(BF16)
            rows = jnp.concatenate(
                [log_total[:, h * LAT : (h + 1) * LAT] for h in range(GROUP)], 0
            )
            high = rows.astype(BF16)
            rest = rows - high.astype(F32)
            mid = rest.astype(BF16)
            last = (rest - mid.astype(F32)).astype(BF16)
            for n, piece in enumerate((high, mid, last)):
                at = D + 8 * n + 4 * g
                part_out[at : at + 4, lane_at] = piece


def enc_bias(info, bias_ref):
    place = lax.broadcasted_iota(jnp.int32, (SLOTS, LAT), 0) + info[7] * SLOTS
    token = lax.broadcasted_iota(jnp.int32, (LAT, LAT), 0) // 32
    lat = jnp.where(token == info[7], 0.0, NEG)
    for image in range(IMGS):
        bias_ref[image, :SLOTS, :] = jnp.where(place < info[image], 0.0, NEG)
        bias_ref[image, SLOTS:, :] = lat


def enc_keys(kv, lqkv, image, g, k_ref, v_ref, vt_ref, kt_ref):
    rows = slice(image * SLOTS, (image + 1) * SLOTS)
    lat_at = slice(image * LAT, (image + 1) * LAT)
    k_ref[:SLOTS, :] = kv[rows, g * GW : (g + 1) * GW]
    k_ref[SLOTS:, :] = lqkv[lat_at, D + g * GW : D + (g + 1) * GW]
    value = jnp.concatenate(
        [kv[rows, D + g * GW : D + (g + 1) * GW], lqkv[lat_at, 2 * D + g * GW : 2 * D + (g + 1) * GW]],
        0,
    )
    if v_ref is not None:
        v_ref[...] = value
    if vt_ref is not None:
        vt_ref[...] = value.T
    if kt_ref is not None:
        kt_ref[...] = k_ref[...].T


def dec_front(
    info, wo_hbm, win_hbm, wout_hbm, pos, quant, lemb, wqkv, gains, biases, hbias, cot,
    res_hbm, keep_hbm, send_hbm, dmid_hbm, attn_hbm, tn_hbm, xn_hbm, x_hbm, dbr_hbm,
    ln_out, sm_out, dq_ref, dkv_ref, dkvl_ref, code_out, sm_back,
    res_out, keep_out, send_out, dmid_out, attn_out, tn_out, xn_out, x_out, dbr_ref,
    wo, win, wout, in_sems, out_sems,
    e_out, inv_out, q_out, k_out, v_out,
    bias_ref, vt_ref, ot_ref, mid_ref, hn_ref, dy_ref, acc_ref, dhn_ref, act_ref, dpre_ref,
    da_ref, dqt_ref, dk_ref, dv_ref, dkl_ref, dvl_ref, ds_ref, dn_ref, emb_ref, din_ref,
):
    loads = [
        pltpu.make_async_copy(src, dst, in_sems.at[n])
        for n, (src, dst) in enumerate(((wo_hbm, wo), (win_hbm, win), (wout_hbm, wout)))
    ]
    for load in loads:
        load.start()
    stores = []

    def store(src, dst):
        copy = pltpu.make_async_copy(src, dst, out_sems.at[len(stores)])
        copy.start()
        stores.append(copy)

    gain0, off0 = row_of(gains, 0), row_of(biases, 0)
    gain1, off1 = row_of(gains, 1), row_of(biases, 4)
    qbias, vbias = row_of(biases, 1), row_of(biases, 2)
    token = row_of(biases, 7)

    def table_norm(r):
        at = chunk(r, 64)
        values = token + pos[at, :].astype(F32)
        tn_out[at, :] = norm_rows(values, gain0, off0).astype(BF16)

    loop(TABLE // 64, table_norm, 8)

    def table_keys(r):
        at = chunk(r, 256)
        key = dot(tn_out[at, :], wqkv[:, D : 2 * D]).astype(BF16)
        value = (dot(tn_out[at, :], wqkv[:, 2 * D :]) + vbias).astype(BF16)
        for image in range(IMGS):
            k_out[image, at, :] = key
            v_out[image, at, :] = value

    loop(TABLE // 256, table_keys)
    embed = dot(quant[...], lemb[...], TN) + row_of(biases, 6)
    ln_out[...] = norm_rows(embed, gain0, off0).astype(BF16)
    lat_k = dot(ln_out[...], wqkv[:, D : 2 * D]).astype(BF16)
    lat_v = (dot(ln_out[...], wqkv[:, 2 * D :]) + vbias).astype(BF16)
    for image in range(IMGS):
        at = slice(image * LAT, (image + 1) * LAT)
        k_out[image, TABLE:, :] = lat_k[at, :]
        v_out[image, TABLE:, :] = lat_v[at, :]
        bias_ref[image, :TABLE, :] = table_bias(info, image, (TABLE, LAT))
        bias_ref[image, TABLE:, :] = jnp.zeros((LAT, LAT), F32)
        place = own_positions(info, image, lax.broadcasted_iota(jnp.int32, (SLOTS, 1), 0))
        lane = lax.broadcasted_iota(jnp.int32, (SLOTS, TABLE), 1)
        hot = jnp.where(place == lane, 1.0, 0.0).astype(BF16)
        x_out[image * SLOTS : (image + 1) * SLOTS, :] = dot(hot, pos[...]).astype(BF16)
        for b in range(D // 128):
            cols = slice(b * 128, (b + 1) * 128)
            if image == 0:
                vt_ref[0, cols, :] = v_out[0, :, cols].T
            else:
                vt_ref[image, cols, :TABLE] = vt_ref[0, cols, :TABLE]
                vt_ref[image, cols, TABLE:] = v_out[image, TABLE:, cols].T

    def own_norm(r):
        at = chunk(r, 64)
        values = token + x_out[at, :].astype(F32)
        xn_out[at, :] = norm_rows(values, gain0, off0).astype(BF16)
        slot = lax.broadcasted_iota(jnp.int32, (64, 1), 0) + (r % 4) * 64 + info[7] * SLOTS
        valid = slot < info[r // 4]
        dy_ref[at, :] = jnp.where(valid, cot[at, :], jnp.zeros((64, D), BF16))

    loop(ROWS // 64, own_norm, 8)
    store(tn_out, tn_hbm)
    store(xn_out, xn_hbm)
    store(x_out, x_hbm)
    q_out[...] = (dot(xn_out[...], wqkv[:, :D]) + qbias).astype(BF16)
    ones = jnp.ones((16, KEYS), BF16)

    def attend(t):
        image, g = t // 2, t % 2
        cols = chunk(g, GW)
        keys = k_out[image, :, cols]
        query = q_out[chunk(image, SLOTS), cols] * jnp.asarray(0.125, BF16)
        bias = bias_ref[image]
        bias = jnp.concatenate([bias, bias], 1)
        lane = lax.broadcasted_iota(jnp.int32, (SLOTS, GW), 1) // HD

        def score(h):
            return dot(keys, jnp.where(lane == h, query, jnp.zeros_like(query)), NT) + bias

        def finish(h, low):
            at = pl.ds(pl.multiple_of(g * GW + h * HD, HD), HD)
            mixed = dot(jnp.concatenate([vt_ref[image, at, :], ones], 0), low)
            inverse = 1.0 / mixed[HD : HD + 1, :]
            ot_ref[image, at, :] = mixed[:HD, :] * inverse
            inv_out[t, h : h + 1, :] = inverse

        ahead, low = score(0), None
        for h in range(GROUP):
            scores = ahead
            if h + 1 < GROUP:
                ahead = score(h + 1)
            if low is not None:
                finish(h - 1, low)
            low = jnp.exp(scores - jnp.max(scores, 0, keepdims=True)).astype(BF16)
            e_out[t, :, h * SLOTS : (h + 1) * SLOTS] = low
        finish(GROUP - 1, low)

    loop(4, attend)
    for image in range(IMGS):
        for b in range(D // 128):
            cols = slice(b * 128, (b + 1) * 128)
            attn_out[image * SLOTS : (image + 1) * SLOTS, cols] = (
                ot_ref[image, cols, :].T.astype(BF16)
            )
    store(attn_out, attn_hbm)
    for load in loads:
        load.wait()
    out_bias = row_of(biases, 3)
    mid_ref[...] = dot(attn_out[...], wo[...]) + out_bias

    def mid_norm(r):
        at = chunk(r, 64)
        values = mid_ref[at, :] + (token + x_out[at, :].astype(F32))
        mid_ref[at, :] = values
        hn_ref[at, :] = norm_rows(values, gain1, off1).astype(BF16)

    loop(ROWS // 64, mid_norm, 8)

    def into(j):
        at = slice(j * D, (j + 1) * D)
        act_grad = dot(dy_ref[...], wout[at, :], NT)
        return act_grad, dot(hn_ref[...], win[:, at]) + hbias[at].astype(F32).reshape(1, D)

    def out_of(j):
        at = slice(j * D, (j + 1) * D)
        more = dot(act_ref[j % 2], wout[at, :])
        back = dot(dpre_ref[j % 2], win[:, at], NT)
        if j == 0:
            acc_ref[...] = more
            dhn_ref[...] = back
        else:
            acc_ref[...] += more
            dhn_ref[...] += back
        put_pieces(info, keep_out, send_out, 0, j, dot(hn_ref[...], dpre_ref[j % 2], TN), 64, 128)
        put_pieces(info, keep_out, send_out, 64, j, dot(act_ref[j % 2], dy_ref[...], TN), 64, 128)

    ahead = into(0)
    for j in range(FF // D):
        act_grad, pre = ahead
        if j + 1 < FF // D:
            ahead = into(j + 1)
        if j > 0:
            out_of(j - 1)
        act, slope = gelu_parts(pre)
        act_ref[j % 2] = act.astype(BF16)
        pre_grad = (act_grad * slope).astype(BF16)
        dpre_ref[j % 2] = pre_grad
        sm_out[4 + j : 5 + j, :] = col_sum(pre_grad.astype(F32))
    out_of(FF // D - 1)
    store(keep_out, keep_hbm)
    store(send_out, send_hbm)
    last_bias = row_of(biases, 5)

    def finish(r, carry):
        gain_sum, off_sum, out_sum = carry
        at = chunk(r, 64)
        values = mid_ref[at, :]
        final = values + acc_ref[at, :] + last_bias
        slot = lax.broadcasted_iota(jnp.int32, (64, 1), 0) + (r % 4) * 64 + info[7] * SLOTS
        valid = slot < info[r // 4]
        res_out[at, :] = jnp.where(valid, final, 0.0).astype(BF16)
        upstream = dhn_ref[at, :]
        down, along = norm_back(values, gain1, upstream)
        top = dy_ref[at, :].astype(F32)
        dmid_out[at, :] = top + down
        return gain_sum + fold(along), off_sum + fold(upstream), out_sum + fold(top)

    zero = jnp.zeros((8, D), F32)
    gain_sum, off_sum, out_sum = lax.fori_loop(0, ROWS // 64, finish, (zero, zero, zero), unroll=8)
    sm_out[0:1, :] = col_sum(gain_sum)
    sm_out[1:2, :] = col_sum(off_sum)
    sm_out[2:3, :] = col_sum(out_sum)
    sm_out[3:4, :] = jnp.zeros((1, D), F32)
    store(res_out, res_hbm)
    store(dmid_out, dmid_hbm)
    dec_back(
        dmid_out, attn_out, e_out, inv_out, q_out, k_out, v_out, quant, lemb, wqkv, wo, gains, biases,
        dq_ref, dkv_ref, dkvl_ref, dbr_ref, code_out, sm_back, lambda: store(dbr_ref, dbr_hbm),
        da_ref, dqt_ref, dk_ref, dv_ref, dkl_ref, dvl_ref, vt_ref, ds_ref, dn_ref, emb_ref, din_ref,
    )
    for copy in stores:
        copy.wait()


def dec_back(
    dmid, attn, e_in, inv, q_in, k_in, v_in, quant, lemb, wqkv, wo, gains, biases,
    dq_ref, dkv_ref, dkvl_ref, dbr_ref, code_out, sm_out, branch_done,
    da_ref, dqt_ref, dk_ref, dv_ref, dkl_ref, dvl_ref, kt_ref, ds_ref, dn_ref, emb_ref, din_ref,
):
    gain0 = row_of(gains, 0)

    def branch(r, carry):
        at = chunk(r, 64)
        low = dmid[at, :].astype(BF16)
        dbr_ref[at, :] = low
        return carry + fold(low.astype(F32))

    zero = jnp.zeros((8, D), F32)
    sm_out[3:4, :] = col_sum(lax.fori_loop(0, ROWS // 64, branch, zero, unroll=8))
    branch_done()
    da_ref[...] = dot(dbr_ref[...], wo[...], NT).astype(BF16)
    for image in range(IMGS):
        for b in range(D // 128):
            cols = slice(b * 128, (b + 1) * 128)
            if image == 0:
                kt_ref[0, cols, :] = k_in[0, :, cols].T
            else:
                kt_ref[image, cols, :TABLE] = kt_ref[0, cols, :TABLE]
                kt_ref[image, cols, TABLE:] = k_in[image, TABLE:, cols].T
    dk_ref[...] = jnp.zeros_like(dk_ref)
    dv_ref[...] = jnp.zeros_like(dv_ref)

    def attend(t):
        image, g = t // 2, t % 2
        cols = chunk(g, GW)
        rows = chunk(image, SLOTS)
        out_grad_t = da_ref[rows, cols].astype(F32).T
        out_t = attn[rows, cols].astype(F32).T
        scaled, inner = [], []
        for h in range(GROUP):
            at = slice(h * HD, (h + 1) * HD)
            inverse = inv[t, h : h + 1, :]
            scaled.append(out_grad_t[at, :] * inverse)
            inner.append(col_sum(out_grad_t[at, :] * out_t[at, :]) * inverse)
        out_grad = jnp.concatenate(scaled, 0).T.astype(BF16)
        out_stack = head_stack(out_grad, SLOTS)
        query = q_in[rows, cols] * jnp.asarray(0.125, BF16)
        values = v_in[image, :, cols]

        def prob_grad(h):
            return dot(values, out_stack[h * SLOTS : (h + 1) * SLOTS, :], NT)

        def query_grad(h, low):
            at = pl.ds(pl.multiple_of(g * GW + h * HD, HD), HD)
            dqt_ref[image, at, :] = dot(kt_ref[image, at, :], low)

        ahead, low = prob_grad(0), None
        for h in range(GROUP):
            lanes = slice(h * SLOTS, (h + 1) * SLOTS)
            grads = ahead
            if h + 1 < GROUP:
                ahead = prob_grad(h + 1)
            if low is not None:
                query_grad(h - 1, low)
            low = (e_in[t, :, lanes].astype(F32) * (grads - inner[h])).astype(BF16)
            ds_ref[:, lanes] = low
        query_grad(GROUP - 1, low)
        value_grad = dot(e_in[t], out_stack)
        dv_ref[:, cols] += value_grad[:TABLE, :]
        lat_rows = chunk(image, LAT)
        dvl_ref[lat_rows, cols] = value_grad[TABLE:, :]
        key_grad = dot(ds_ref[...], head_stack(query, SLOTS))
        dk_ref[:, cols] += key_grad[:TABLE, :]
        dkl_ref[lat_rows, cols] = key_grad[TABLE:, :]

    loop(4, attend)
    dkvl_ref[:, :D] = dkl_ref[...].astype(BF16)
    dkvl_ref[:, D:] = dvl_ref[...].astype(BF16)
    dn_ref[...] = dot(dkvl_ref[...], wqkv[:, D:], NT)
    emb_ref[...] = dot(quant[...], lemb[...], TN) + row_of(biases, 6)

    def latent(r, carry):
        gain_sum, off_sum, embed_sum = carry
        at = chunk(r, 64)
        upstream = dn_ref[at, :]
        down, along = norm_back(emb_ref[at, :], gain0, upstream)
        low = down.astype(BF16)
        din_ref[at, :] = low
        return gain_sum + fold(along), off_sum + fold(upstream), embed_sum + fold(low.astype(F32))

    sums = lax.fori_loop(0, LROWS // 64, latent, (zero, zero, zero), unroll=4)
    embed_grad = din_ref[...]
    code_out[...] = dot(lemb[...], embed_grad, NT)
    sm_out[0:1, :] = col_sum(sums[0])
    sm_out[1:2, :] = col_sum(sums[1])
    sm_out[2:3, :] = jnp.zeros((1, D), F32)
    sm_out[6:7, :] = col_sum(sums[2])
    sm_out[7:8, :] = jnp.zeros((1, D), F32)
    sm_out[8:20, :] = dot(quant[...], embed_grad)
    sm_out[20:, :] = jnp.zeros((4, D), F32)
    for image in range(IMGS):
        for b in range(D // 128):
            cols = slice(b * 128, (b + 1) * 128)
            dq_ref[image * SLOTS : (image + 1) * SLOTS, cols] = (
                (dqt_ref[image, cols, :] * 0.125).T.astype(BF16)
            )
    dkv_ref[:, :D] = dk_ref[...].astype(BF16)
    dkv_ref[:, D:] = dv_ref[...].astype(BF16)
    sm_out[4:5, :] = col_sum(fold(dq_ref[...].astype(F32)))
    sm_out[5:6, :] = col_sum(
        fold(dkv_ref[:, D:].astype(F32)) + fold(dkvl_ref[:, D:].astype(F32))
    )


def dec_weights(
    info, dq_ref, dkv_ref, dkvl_ref, dbr_ref, sm_in, dmid, attn, tn, xn, ln, x_in, pos, wqkv,
    gains, biases,
    keep_out, send_out, sm_out,
    w_ref, dn_ref, din_ref, tab_ref,
):
    gain0 = row_of(gains, 0)
    token = row_of(biases, 7)
    zero = jnp.zeros((8, D), F32)
    w_ref[:, :D] = dot(attn[...], dbr_ref[...], TN)
    for z in range(4):
        put_pieces(
            info, keep_out, send_out, 0, z, w_ref[z * 128 : (z + 1) * 128, :D], 16, 128
        )
    w_ref[:, :D] = dot(xn[...], dq_ref[...], TN)
    w_ref[:, D:] = dot(tn[...], dkv_ref[...], TN) + dot(ln[...], dkvl_ref[...], TN)
    for z in range(4):
        put_pieces(
            info, keep_out, send_out, 16, z, w_ref[z * 128 : (z + 1) * 128, :], 16, 384
        )
    dn_ref[:ROWS, :] = dot(dq_ref[...], wqkv[:, :D], NT)

    def own(r, carry):
        gain_sum, off_sum = carry
        at = chunk(r, 64)
        upstream = dn_ref[at, :]
        down, along = norm_back(token + x_in[at, :].astype(F32), gain0, upstream)
        din_ref[at, :] = (dmid[at, :] + down).astype(BF16)
        return gain_sum + fold(along), off_sum + fold(upstream)

    sums = lax.fori_loop(0, ROWS // 64, own, (zero, zero), unroll=8)
    for r in range(4):
        at = slice(r * 256, (r + 1) * 256)
        dn_ref[at, :] = dot(dkv_ref[at, :], wqkv[:, D:], NT)
    lane = lax.broadcasted_iota(jnp.int32, (1, SLOTS), 1)
    place = [own_positions(info, image, lane) for image in range(IMGS)]

    def scatter(r):
        at = chunk(r, 256)
        index = lax.broadcasted_iota(jnp.int32, (256, SLOTS), 0) + r * 256
        total = jnp.zeros((256, D), F32)
        for image in range(IMGS):
            hot = jnp.where(place[image] == index, 1.0, 0.0).astype(BF16)
            total = total + dot(hot, din_ref[image * SLOTS : (image + 1) * SLOTS, :])
        tab_ref[at, :] = total

    loop(4, scatter)

    def table(r, carry):
        gain_sum, off_sum, mask_sum = carry
        at = chunk(r, 64)
        upstream = dn_ref[at, :]
        down, along = norm_back(token + pos[at, :].astype(F32), gain0, upstream)
        rows = tab_ref[at, :] + down
        tab_ref[at, :] = rows
        return gain_sum + fold(along), off_sum + fold(upstream), mask_sum + fold(rows)

    gain_sum, off_sum, mask_sum = lax.fori_loop(0, TABLE // 64, table, sums + (zero,), unroll=8)
    for z in range(4):
        put_pieces(
            info, keep_out, send_out, 64, z, tab_ref[z * 256 : (z + 1) * 256, :], 32, 128
        )
    sm_out[...] = sm_in[...]
    sm_out[0:1, :] = sm_in[0:1, :] + col_sum(gain_sum)
    sm_out[1:2, :] = sm_in[1:2, :] + col_sum(off_sum)
    sm_out[2:3, :] = col_sum(mask_sum)


def enc_mid(
    info, wo_hbm, win_hbm, wout_hbm, parts0, parts1, parts2, parts3, latents, gains, biases, hbias,
    proj, pbias, quant,
    attn_out, mid_out, hn_out, act_out, slope_out, final_out, post_out, diff_out, lse_out,
    wo, win, wout, sems, ot_ref, acc_ref,
):
    loads = [
        pltpu.make_async_copy(src, dst, sems.at[n])
        for n, (src, dst) in enumerate(((wo_hbm, wo), (win_hbm, win), (wout_hbm, wout)))
    ]
    for load in loads:
        load.start()
    logs = []
    for part in (parts0, parts1, parts2, parts3):
        logs.append(
            part[D : D + 8, :].astype(F32)
            + part[D + 8 : D + 16, :].astype(F32)
            + part[D + 16 : D + 24, :].astype(F32)
        )
    top = functools.reduce(jnp.maximum, logs)
    log_total = top + jnp.log(sum(jnp.exp(rows - top) for rows in logs))
    lse_out[...] = log_total
    weights = [jnp.exp(rows - log_total) for rows in logs]
    for h in range(HEADS):
        at = slice(h * HD, (h + 1) * HD)
        ot_ref[at, :] = sum(
            part[at, :].astype(F32) * weight[h : h + 1, :]
            for part, weight in zip((parts0, parts1, parts2, parts3), weights)
        )
    for b in range(D // 128):
        cols = slice(b * 128, (b + 1) * 128)
        attn_out[:, cols] = ot_ref[cols, :].T.astype(BF16)
    loads[0].wait()
    acc_ref[...] = dot(attn_out[...], wo[...]) + row_of(biases, 2)
    gain1, off1 = row_of(gains, 1), row_of(biases, 3)
    gain2, off2 = row_of(gains, 2), row_of(biases, 5)

    def mid_norm(r):
        at = chunk(r, 64)
        values = acc_ref[at, :] + latents[at, :].astype(F32)
        mid_out[at, :] = values
        hn_out[at, :] = norm_rows(values, gain1, off1).astype(BF16)
        acc_ref[at, :] = values + row_of(biases, 4)

    loop(LROWS // 64, mid_norm, 4)

    def into(j):
        at = slice(j * D, (j + 1) * D)
        return dot(hn_out[...], win[:, at]) + hbias[at].astype(F32).reshape(1, D)

    loads[1].wait()
    loads[2].wait()
    ahead, total = into(0), acc_ref[...]
    for j in range(FF // D):
        at = slice(j * D, (j + 1) * D)
        pre = ahead
        if j + 1 < FF // D:
            ahead = into(j + 1)
        if j > 0:
            total = total + dot(act_out[:, (j - 1) * D : j * D], wout[(j - 1) * D : j * D, :])
        act, slope = gelu_parts(pre)
        act_out[:, at] = act.astype(BF16)
        slope_out[:, at] = slope
    acc_ref[...] = total + dot(act_out[:, FF - D :], wout[FF - D :, :])

    def post_norm(r):
        at = chunk(r, 64)
        values = acc_ref[at, :]
        final_out[at, :] = values
        post_out[at, :] = norm_rows(values, gain2, off2).astype(BF16)

    loop(LROWS // 64, post_norm, 4)
    same = lax.broadcasted_iota(jnp.int32, (12, 12), 0) == lax.broadcasted_iota(
        jnp.int32, (12, 12), 1
    )
    shift_col = jnp.sum(jnp.where(same, pbias[...].astype(F32).reshape(1, 12), 0.0), -1, keepdims=True)
    code = dot(proj[...], post_out[...], NT) + shift_col
    diff_out[...] = code - quant[...].astype(F32)


def enc_mlp_back(
    info, code0, code1, code2, code3, diff, post, final, mid, hn, act, slope, attn, wo, win, wout, gains, proj,
    keep_out, send_out, da_out, dmid_out, sm_out,
    dy_ref, dn_ref, dfin_ref, dpre_ref, dbr_ref,
):
    zero = jnp.zeros((8, D), F32)
    gain1, gain2 = row_of(gains, 1), row_of(gains, 2)
    code_grad = code0[...] + code1[...] + code2[...] + code3[...] + 2.0 * COMMIT * diff[...]
    low = code_grad.astype(BF16)
    sm_out[16:28, :] = dot(low, post[...]) * SHARE
    sm_out[28:40, :] = jnp.broadcast_to(
        jnp.sum(low.astype(F32), -1, keepdims=True) * SHARE, (12, D)
    )
    loss = (1.0 + COMMIT) * jnp.sum(diff[...] * diff[...]) * SHARE
    sm_out[40:48, :] = jnp.full((8, D), loss, F32)
    dn_ref[...] = dot(low, proj[...], TN)

    def post_back(r, carry):
        gain_sum, off_sum, out_sum = carry
        at = chunk(r, 64)
        upstream = dn_ref[at, :]
        down, along = norm_back(final[at, :], gain2, upstream)
        dfin_ref[at, :] = down
        branch = down.astype(BF16)
        dy_ref[at, :] = branch
        return gain_sum + fold(along), off_sum + fold(upstream), out_sum + fold(branch.astype(F32))

    sums = lax.fori_loop(0, LROWS // 64, post_back, (zero, zero, zero), unroll=4)
    for n in range(3):
        sm_out[n : n + 1, :] = col_sum(sums[n]) * SHARE
    def into(j):
        return dot(dy_ref[...], wout[j * D : (j + 1) * D, :], NT)

    ahead, total = into(0), None
    for j in range(FF // D):
        at = slice(j * D, (j + 1) * D)
        act_grad = ahead
        if j + 1 < FF // D:
            ahead = into(j + 1)
        pre_grad = (act_grad * slope[:, at]).astype(BF16)
        dpre_ref[:, at] = pre_grad
        sm_out[8 + j : 9 + j, :] = col_sum(pre_grad.astype(F32)) * SHARE
        back = dot(pre_grad, win[:, at], NT)
        total = back if j == 0 else total + back
    dn_ref[...] = total
    mine = chunk(info[7], D)
    put_pieces(
        info, keep_out, send_out, 0, None, dot(hn[...], dpre_ref[:, mine], TN), 64, 128
    )
    put_pieces(
        info, keep_out, send_out, 64, None, dot(act[:, mine], dy_ref[...], TN), 64, 128
    )

    def mid_back(r, carry):
        gain_sum, off_sum, out_sum = carry
        at = chunk(r, 64)
        upstream = dn_ref[at, :]
        down, along = norm_back(mid[at, :], gain1, upstream)
        total = dfin_ref[at, :] + down
        dmid_out[at, :] = total
        branch = total.astype(BF16)
        dbr_ref[at, :] = branch
        return gain_sum + fold(along), off_sum + fold(upstream), out_sum + fold(branch.astype(F32))

    sums = lax.fori_loop(0, LROWS // 64, mid_back, (zero, zero, zero), unroll=4)
    for n in range(3):
        sm_out[3 + n : 4 + n, :] = col_sum(sums[n]) * SHARE
    sm_out[6:8, :] = jnp.zeros((2, D), F32)
    sm_out[12:16, :] = jnp.zeros((4, D), F32)
    da_out[...] = dot(dbr_ref[...], wo[...], NT).astype(BF16)
    own = attn[:, chunk(info[7], 128)]
    put_pieces(info, keep_out, send_out, 128, None, dot(own, dbr_ref[...], TN), 16, 128)


def enc_back(
    info, da, attn, lse, kv, lqkv, np_in, nl, patches, latents, wqkv, gains, codes, diff,
    sm_mlp, sm_front, sm_dec,
    keep_out, send_out, patch_out, lat_out,
    bias_ref, k_ref, v_ref, kt_ref, dqt_ref, dkv_ref, dlat_ref, w_ref, dn_ref, sm_ref,
):
    zero = jnp.zeros((8, D), F32)
    gain0 = row_of(gains, 0)
    enc_bias(info, bias_ref)
    for image in range(IMGS):
        rows = slice(image * SLOTS, (image + 1) * SLOTS)
        lat_at = slice(image * LAT, (image + 1) * LAT)
        for g in range(2):
            cols = slice(g * GW, (g + 1) * GW)
            enc_keys(kv, lqkv, image, g, k_ref, v_ref, None, kt_ref)
            query_stack = head_stack(lqkv[lat_at, cols] * jnp.asarray(0.125, BF16), LAT)
            out_grad = da[lat_at, cols]
            out_stack = head_stack(out_grad, LAT)
            grad_t = out_grad.astype(F32).T
            out_t = attn[lat_at, cols].astype(F32).T
            inner = jnp.concatenate(
                [
                    col_sum(grad_t[h * HD : (h + 1) * HD, :] * out_t[h * HD : (h + 1) * HD, :])
                    for h in range(GROUP)
                ],
                1,
            )
            log_total = jnp.concatenate(
                [lse[g * GROUP + h : g * GROUP + h + 1, lat_at] for h in range(GROUP)], 1
            )
            scores = dot(k_ref[...], query_stack, NT)
            bias = jnp.concatenate([bias_ref[image]] * GROUP, 1)
            probs = jnp.exp(scores + bias - log_total)
            prob_grad = dot(v_ref[...], out_stack, NT)
            low = (probs * (prob_grad - inner)).astype(BF16)
            value_grad = dot(probs.astype(BF16), out_stack).astype(BF16)
            key_grad = dot(low, query_stack).astype(BF16)
            dkv_ref[rows, cols] = key_grad[:SLOTS, :]
            dkv_ref[rows, D + g * GW : D + (g + 1) * GW] = value_grad[:SLOTS, :]
            dlat_ref[lat_at, D + g * GW : D + (g + 1) * GW] = key_grad[SLOTS:, :]
            dlat_ref[lat_at, 2 * D + g * GW : 2 * D + (g + 1) * GW] = value_grad[SLOTS:, :]
            for h in range(GROUP):
                part = dot(kt_ref[h * HD : (h + 1) * HD, :], low[:, h * LAT : (h + 1) * LAT])
                at = g * GW + h * HD
                dqt_ref[at : at + HD, lat_at] = part * 0.125
    for b in range(D // 128):
        cols = slice(b * 128, (b + 1) * 128)
        dlat_ref[:, cols] = dqt_ref[cols, :].T.astype(BF16)
    dn_ref[...] = dot(dkv_ref[...], wqkv[:, D:], NT)

    def patch_back(r, carry):
        gain_sum, off_sum = carry
        at = chunk(r, 64)
        upstream = dn_ref[at, :]
        down, along = norm_back(patches[at, :].astype(F32), gain0, upstream)
        patch_out[at, :] = down
        return gain_sum + fold(along), off_sum + fold(upstream)

    sums = lax.fori_loop(0, ROWS // 64, patch_back, (zero, zero), unroll=8)
    dn_ref[:LROWS, :] = dot(dlat_ref[...], wqkv[...], NT)

    def lat_back(r, carry):
        gain_sum, off_sum = carry
        at = chunk(r, 64)
        upstream = dn_ref[at, :]
        down, along = norm_back(latents[at, :].astype(F32), gain0, upstream)
        lat_out[at, :] = down.astype(BF16)
        return gain_sum + fold(along), off_sum + fold(upstream)

    sums = lax.fori_loop(0, LROWS // 64, lat_back, sums, unroll=4)
    w_ref[:, :D] = dot(nl[...], dlat_ref[:, :D], TN)
    w_ref[:, D:] = dot(nl[...], dlat_ref[:, D:], TN) + dot(np_in[...], dkv_ref[...], TN)
    for z in range(4):
        put_pieces(
            info, keep_out, send_out, 0, z, w_ref[z * 128 : (z + 1) * 128, :], 16, 384, qkv_index
        )
    sm_ref[0:1, :] = col_sum(sums[0])
    sm_ref[1:2, :] = sm_mlp[3:4, :]
    sm_ref[2:3, :] = sm_mlp[0:1, :]
    sm_ref[3:4, :] = col_sum(sums[1])
    sm_ref[4:5, :] = col_sum(
        fold(dkv_ref[:, D:].astype(F32)) + fold(dlat_ref[:, 2 * D :].astype(F32))
    )
    sm_ref[5:6, :] = sm_mlp[5:6, :]
    sm_ref[6:7, :] = sm_mlp[4:5, :]
    sm_ref[7:8, :] = sm_mlp[2:3, :]
    sm_ref[8:9, :] = sm_mlp[1:2, :]
    sm_ref[9:10, :] = col_sum(fold(dlat_ref[:, :D].astype(F32)))
    sm_ref[10:14, :] = sm_mlp[8:12, :]
    sm_ref[14:26, :] = sm_mlp[16:28, :]
    pick = lax.broadcasted_iota(jnp.int32, (12, D), 0) == lax.broadcasted_iota(
        jnp.int32, (12, D), 1
    )
    sm_ref[26:27, :] = col_sum(jnp.where(pick, sm_mlp[28:40, :], 0.0))
    sm_ref[27:28, :] = sm_mlp[40:41, :]
    sm_ref[28:40, :] = sm_dec[8:20, :]
    sm_ref[40:41, :] = sm_dec[0:1, :]
    sm_ref[41:42, :] = sm_front[0:1, :]
    sm_ref[42:43, :] = sm_dec[1:2, :]
    sm_ref[43:44, :] = sm_dec[4:5, :]
    sm_ref[44:45, :] = sm_dec[5:6, :]
    sm_ref[45:46, :] = sm_dec[3:4, :]
    sm_ref[46:47, :] = sm_front[1:2, :]
    sm_ref[47:48, :] = sm_front[2:3, :]
    sm_ref[48:49, :] = sm_dec[6:7, :]
    sm_ref[49:50, :] = sm_dec[2:3, :]
    sm_ref[50:54, :] = sm_front[4:8, :]
    sm_ref[54:, :] = jnp.zeros((SMALL - 54, D), F32)
    token = lax.broadcasted_iota(jnp.int32, (12, LROWS), 1) % LAT
    mine = jnp.where(token // 32 == info[7], -2.0 * diff[...], 0.0).astype(BF16)
    book = dot(mine, code_onehot(codes, 8 * D), NT)
    for n in range(8):
        at = CODE_ROW + 16 * n
        sm_ref[at : at + 12, :] = book[:, n * D : (n + 1) * D]
    mine_first = info[4] == 0
    for p in range(PIECES):
        z, q = p // 32, p % 32
        if q >= 16:
            continue
        own = qkv_index(info, info[4], z, q // 4, q % 4)
        away = qkv_index(info, 1 - info[4], z, q // 4, q % 4)
        mine = small_piece(sm_ref, p)
        other = small_piece(sm_ref, p + 16)
        keep_out[own, 48:64, :] = jnp.where(mine_first, mine, other)
        send_out[away, 48:64, :] = jnp.where(mine_first, other, mine)


def small_piece(sm_ref, p):
    if p >= SMALL // 4:
        return jnp.zeros((16, 128), BF16)
    row, col = (p // 4) * 16, (p % 4) * 128
    return sm_ref[row : row + 16, col : col + 128].astype(BF16)


def pair_sum(parts, n):
    values = [part[n].astype(F32) for part in parts]
    if len(values) == 2:
        return (values[0] + values[1]).astype(BF16)
    return ((values[0] + values[2]) + (values[1] + values[3])).astype(BF16)


def add_all(info, *refs):
    *parts, out = refs

    def one(n):
        out[n] = pair_sum(parts, n)

    loop(out.shape[0], one)


def join_dec(info, mlp, *refs):
    rest, plane, (dec_out, plane_out) = refs[:4], refs[4:6], refs[6:]

    def one(n):
        dec_out[n, 0:128, :] = mlp[n]
        dec_out[n, 128:224, :] = pair_sum(rest, n)
        plane_out[n] = pair_sum(plane, n)

    loop(16, one)


MAIN = 368
QKV = 64


def join_all(info, *refs):
    dec, plane, qkv = refs[:4], refs[4:8], refs[8:10]
    own_main, own_qkv, *sends = refs[10:]
    fours = 4 * MAIN

    def one(n):
        rows = jnp.concatenate([pair_sum(dec, n), pair_sum(plane, n)], 0)
        at = pl.ds(pl.multiple_of(n * MAIN, 16), MAIN)
        own_main[at, :] = rows
        for send in sends:
            send[at, :] = rows

    loop(4, one)

    def other(n):
        at = pl.ds(pl.multiple_of(n * QKV, 16), QKV)
        own_qkv[at, :] = pair_sum(qkv, n)
        for by in (1, 2, 3):
            after = pl.ds(pl.multiple_of(fours + n * QKV, 16), QKV)
            sends[by - 1][after, :] = pair_sum(qkv, (4 - by) * 16 + n)

    loop(16, other)


def rows_sum(parts, starts, count):
    values = [part[start : start + count, :].astype(F32) for part, start in zip(parts, starts)]
    return ((values[0] + values[2]) + (values[1] + values[3])).astype(BF16)


def join_two(info, own_main, own_qkv, one, two, three, out_main, out_qkv, *sends):
    fours = 4 * MAIN
    got = (one, two, three)
    for n in range(4):
        at = n * MAIN
        rows = rows_sum((own_main,) + got, (at,) * 4, MAIN)
        out_main[at : at + MAIN, :] = rows
        for send in sends:
            send[at : at + MAIN, :] = rows
    for n in range(4):
        at = n * 4 * QKV
        rows = rows_sum((own_qkv,) + got, (at,) + (fours + at,) * 3, 4 * QKV)
        if n == 0:
            out_qkv[...] = rows
        else:
            sends[3 - n][fours:, :] = rows


def join_three(info, own_main, own_qkv, one, two, three, lat, lat_other, out, out_qkv, out_lat):
    fours = 4 * MAIN
    for n, part in enumerate((own_main, one, two, three)):
        out[n * fours : (n + 1) * fours, :] = part[:fours, :]
    rows = rows_sum((own_qkv, one, two, three), (0, fours, fours, fours), 4 * QKV)
    out[4 * fours :, :] = rows
    out_qkv[...] = rows
    out_lat[...] = (lat[...].astype(F32) + lat_other[...].astype(F32)).astype(BF16)


def join_four(info, own, one, two, three, out):
    out[...] = rows_sum((own, one, two, three), (0,) * 4, 4 * QKV)


def gate(info, *refs):
    pass


def stack(info, *refs):
    *parts, out = refs
    rows = parts[0].shape[0]
    for n, part in enumerate(parts):
        out[n * rows : (n + 1) * rows, :] = part[...]


def pieces(info, halves):
    c0, y0, x0, z0 = coords(info)
    steps = (0, 1, 3, 2, 2) if halves else (0, 1, 2, 3)
    count = len(steps)
    for s in range(2 * count):
        core = c0 if s < count else 1 - c0
        first = core == 0
        step = steps[s % count]
        for n in range(8 if s % count >= 3 and halves else 16):
            high, low = (n + (8 if s % count == 4 else 0)) // 4, n % 4
            if halves:
                z = jnp.where(first, z0 + step, z0 + high) & 3
                y = jnp.where(first, (y0 + high) & 3, low)
                x = jnp.where(first, low, (x0 + step) & 3)
            else:
                z = jnp.where(first, low, (z0 + high) & 3)
                y = jnp.where(first, y0 + high, y0 + step) & 3
                x = jnp.where(first, (x0 + step) & 3, low)
            e = (y & 1) * 4 + x
            f = core * 2 + lax.shift_right_logical(y, 1)
            yield s, n, z, e, f, z * 32 + core * 16 + y * 4 + x


def take(src, start, dst, row, col, rows, cols):
    for b in range(cols // 128):
        at = start + b * rows
        lanes = pl.ds(pl.multiple_of(col + b * 128, 128), 128)
        dst[pl.ds(pl.multiple_of(row, 16), rows), lanes] = src[at : at + rows, :].astype(F32)


def z_rows(rows, cols):
    return lambda z, e, f: ((z * 8 + e) * rows, f * cols)


def z_cols(z, e, f):
    return e * 64, z * D + f * 128


def unpack_main(info, *refs):
    src, outs, bufs, sems = refs[:10], refs[10:18], refs[18:26], refs[26]
    plan = (
        (0, z_cols, 64, 128), (64, z_rows(64, 128), 64, 128), (128, z_rows(16, 128), 16, 128),
        (144, z_rows(16, 384), 16, 384), (192, z_rows(32, 128), 32, 128),
        (224, z_cols, 64, 128), (288, z_rows(64, 128), 64, 128), (352, z_rows(16, 128), 16, 128),
    )
    copies = []
    for k, (offset, place, rows, cols) in enumerate(plan):
        for s, n, z, e, f, p in pieces(info, True):
            row, col = place(z, e, f)
            take(src[s], n * MAIN + offset, bufs[k], row, col, rows, cols)
        copy = pltpu.make_async_copy(bufs[k], outs[k], sems.at[k])
        copy.start()
        copies.append(copy)
    for copy in copies:
        copy.wait()


def unpack_qkv(info, *refs):
    src = refs[:8]
    (
        qkv_out, gains_out, biases_out, query_out, hidden_out, proj_out, pbias_out, loss_out,
        embed_out, dgains_out, dbiases_out, dhidden_out, book_out, sm_ref,
    ) = refs[8:]
    place = z_rows(16, 384)
    for s, n, z, e, f, p in pieces(info, False):
        row, col = place(z, e, f)
        take(src[s], n * QKV, qkv_out, row, col, 16, 384)

        def small(s=s, n=n, p=p):
            row = lax.shift_right_logical(p, 2) * 16
            take(src[s], n * QKV + 48, sm_ref, row, (p & 3) * 128, 16, 128)

        pl.when(p < SMALL // 4)(small)
    gains_out[...] = sm_ref[0:3, :]
    biases_out[...] = sm_ref[3:9, :]
    query_out[...] = sm_ref[9:10, :]
    for n in range(4):
        hidden_out[:, n * D : (n + 1) * D] = sm_ref[10 + n : 11 + n, :]
        dhidden_out[:, n * D : (n + 1) * D] = sm_ref[50 + n : 51 + n, :]
    proj_out[...] = sm_ref[14:26, :]
    pbias_out[...] = sm_ref[26:27, :128]
    loss_out[...] = sm_ref[27:28, :128]
    embed_out[...] = sm_ref[28:40, :]
    dgains_out[...] = sm_ref[40:42, :]
    dbiases_out[...] = sm_ref[42:50, :]
    for n in range(8):
        at = CODE_ROW + 16 * n
        book_out[:, n * D : (n + 1) * D] = sm_ref[at : at + 12, :]


def size_of(shape, kind):
    total = jnp.dtype(kind).itemsize
    for n in shape:
        total *= n
    return total


def call(
    kernel, name, outs, scratch, info, *args, flops=0, after=(), forward=(), hbm_outs=0, hbm_args=0,
    spare=8
):
    out_shape = [jax.ShapeDtypeStruct(shape, kind) for shape, kind in outs]
    moved = sum(a.size * a.dtype.itemsize for a in args) + sum(
        o.size * o.dtype.itemsize for o in out_shape
    )
    held = sum(a.size * a.dtype.itemsize for a in args[hbm_args:])
    held += sum(o.size * o.dtype.itemsize for o in out_shape[hbm_outs:])
    held += sum(size_of(*item) for item in scratch if isinstance(item, tuple))
    vmem = pl.BlockSpec(memory_space=pltpu.VMEM)
    anywhere = pl.BlockSpec(memory_space=pl.ANY)
    count, others_in, own_out = 2 + len(args), len(after) + len(forward), len(outs)

    def body(*refs):
        last = count + others_in + own_out
        kernel(
            Info(*refs[:2]),
            *refs[2:count],
            *refs[count + others_in : last],
            *refs[last + len(forward) :],
        )

    first = count + len(after)
    return pl.pallas_call(
        body,
        out_shape=out_shape + [jax.ShapeDtypeStruct(a.shape, a.dtype) for a in forward],
        in_specs=[pl.BlockSpec(memory_space=pltpu.SMEM)] * 2
        + [anywhere] * hbm_args
        + [vmem] * (len(args) - hbm_args)
        + [anywhere] * others_in,
        out_specs=[anywhere] * hbm_outs + [vmem] * (own_out - hbm_outs) + [anywhere] * len(forward),
        scratch_shapes=[
            item if not isinstance(item, tuple) else pltpu.VMEM(*item) for item in scratch
        ],
        input_output_aliases={first + n: own_out + n for n in range(len(forward))},
        compiler_params=pltpu.CompilerParams(
            vmem_limit_bytes=min(VMEM_LIMIT, held + spare * 1024 * 1024)
        ),
        cost_estimate=pl.CostEstimate(flops=flops, bytes_accessed=moved, transcendentals=0),
        name=name,
    )(*info, *args, *after, *forward)


def shift(value, axis, by):
    return lax.ppermute(value, axis, [(i, (i + by) % 4) for i in range(4)])


def shift_by_core(value, axes, by):
    sizes = {"y": 4, "x": 4, "core": 2, "z": 4}
    pairs = []
    for start in range(128):
        at = {"z": start % 4, "core": start // 4 % 2, "x": start // 8 % 4, "y": start // 32}
        to = dict(at)
        axis = axes[at["core"]]
        to[axis] = (to[axis] + by) % sizes[axis]
        pairs.append((start, ((to["y"] * 4 + to["x"]) * 2 + to["core"]) * 4 + to["z"]))
    return lax.ppermute(value, ("y", "x", "core", "z"), pairs)


def swap(value):
    return lax.ppermute(value, "core", [(0, 1), (1, 0)])


def pair(value, bit):
    return lax.ppermute(value, "z", [(i, i ^ bit) for i in range(4)])


def scattered(value, move):
    return [value[0]] + [move(value[by], by) for by in (1, 2, 3)]


def others(value, move):
    return [value] + [move(value, -by) for by in (1, 2, 3)]


def along(axis):
    return lambda value, by: shift(value, axis, by)


def along_by_core(*axes):
    return lambda value, by: shift_by_core(value, axes, by)


def per_device(
    enc_patches, enc_latents, resolution, lengths, codes, enc_qkv, enc_out, enc_mlp_in, enc_mlp_out,
    enc_gains, enc_biases, enc_query_bias, enc_hidden_bias, latent_proj, latent_bias, codebook,
    latent_embed, pos_table, dec_qkv, dec_out, dec_mlp_in, dec_mlp_out, dec_gains, dec_biases,
    dec_hidden_bias, out_cot,
):
    info = (lengths, resolution)
    alpha = along_by_core("z", "x")
    patches = enc_patches.reshape(ROWS, D)
    latents = enc_latents.reshape(LROWS, D)
    cot = out_cot.reshape(ROWS, D)
    entries = codebook.shape[1]

    enc_norm, lat_norm, kv, lqkv, part, quant = call(
        enc_front, "enc_front",
        [((ROWS, D), BF16), ((LROWS, D), BF16), ((ROWS, 2 * D), BF16), ((LROWS, 3 * D), BF16),
         ((D + 32, LROWS), BF16), ((12, LROWS), BF16)],
        [((IMGS, OWN_KEYS, LAT), F32), ((OWN_KEYS, GW), BF16), ((GW, OWN_KEYS), BF16)],
        info, patches, latents, enc_qkv, enc_gains, enc_biases, enc_query_bias,
        codes, codebook, flops=2_000_000_000, spare=60,
    )
    parts = others(part, along("z"))
    early = [((ROWS, D), BF16), ((64, 128, 128), BF16), ((64, 128, 128), BF16), ((ROWS, D), F32),
             ((ROWS, D), BF16), ((TABLE, D), BF16), ((ROWS, D), BF16), ((ROWS, D), BF16),
             ((ROWS, D), BF16)]
    (result, mlp_keep, mlp_send, dmid, attn, tab_norm, own_norm, own_pos, branch, emb_norm,
     sm_front, dq, dkv, dkvl, code_part, sm_back) = call(
        dec_front, "dec_front",
        early + [((LROWS, D), BF16), ((8, D), F32), ((ROWS, D), BF16), ((TABLE, 2 * D), BF16),
                 ((LROWS, 2 * D), BF16), ((12, LROWS), F32), ((24, D), F32)],
        early + [((D, D), BF16), ((D, FF), BF16), ((FF, D), BF16), pltpu.SemaphoreType.DMA((3,)),
                 pltpu.SemaphoreType.DMA((9,)),
         ((4, KEYS, GROUP * SLOTS), BF16), ((4, GROUP, SLOTS), F32), ((ROWS, D), BF16),
         ((IMGS, KEYS, D), BF16), ((IMGS, KEYS, D), BF16),
         ((IMGS, KEYS, LAT), F32), ((IMGS, D, KEYS), BF16), ((IMGS, D, SLOTS), F32),
         ((ROWS, D), F32), ((ROWS, D), BF16), ((ROWS, D), BF16), ((ROWS, D), F32), ((ROWS, D), F32),
         ((2, ROWS, D), BF16), ((2, ROWS, D), BF16),
         ((ROWS, D), BF16), ((IMGS, D, SLOTS), F32), ((TABLE, D), F32), ((TABLE, D), F32),
         ((LROWS, D), F32), ((LROWS, D), F32),
         ((KEYS, GROUP * SLOTS), BF16),
         ((LROWS, D), F32), ((LROWS, D), F32), ((LROWS, D), BF16)],
        info, dec_out, dec_mlp_in, dec_mlp_out, pos_table, quant, latent_embed, dec_qkv, dec_gains,
        dec_biases, dec_hidden_bias, cot, flops=20_000_000_000, spare=60, hbm_args=3, hbm_outs=9,
    )
    mlp_send, code_part = call(
        gate, "gate", [], [], info, after=parts + [sm_back], forward=[mlp_send, code_part]
    )
    mlp_other = swap(mlp_send)
    code_parts = others(code_part, along("z"))
    enc_attn, mid, hidden_norm, act, slope, final, post, diff, lse = call(
        enc_mid, "enc_mid",
        [((LROWS, D), BF16), ((LROWS, D), F32), ((LROWS, D), BF16), ((LROWS, FF), BF16),
         ((LROWS, FF), F32), ((LROWS, D), F32), ((LROWS, D), BF16), ((12, LROWS), F32),
         ((HEADS, LROWS), F32)],
        [((D, D), BF16), ((D, FF), BF16), ((FF, D), BF16), pltpu.SemaphoreType.DMA((3,)),
         ((D, LROWS), F32), ((LROWS, D), F32)],
        info, enc_out, enc_mlp_in, enc_mlp_out, *parts, latents, enc_gains, enc_biases,
        enc_hidden_bias, latent_proj, latent_bias, quant,
        flops=1_500_000_000, after=[mlp_send], spare=60, hbm_args=3,
    )
    dec_mlp, *code_parts = call(
        add_all, "sum_mlp_core", [((64, 128, 128), BF16)], [], info, mlp_keep, mlp_other,
        after=[lse], forward=code_parts,
    )
    mlp_parts = scattered(dec_mlp.reshape(4, 16, 128, 128), alpha)
    rest_keep, rest_send, sm_dec = call(
        dec_weights, "dec_weights",
        [((64, 96, 128), BF16), ((64, 96, 128), BF16), ((24, D), F32)],
        [((D, 3 * D), F32), ((TABLE, D), F32), ((ROWS, D), BF16), ((TABLE, D), F32)],
        info, dq, dkv, dkvl, branch, sm_back, dmid, attn, tab_norm, own_norm, emb_norm, own_pos,
        pos_table, dec_qkv, dec_gains, dec_biases, flops=6_000_000_000, after=[dec_mlp],
    )
    dec_mlp, rest_send = call(
        add_all, "sum_mlp_first", [((16, 128, 128), BF16)], [], info, *mlp_parts, after=[rest_keep],
        forward=[rest_send],
    )
    rest_other = swap(rest_send)
    plane_keep, plane_send, enc_da, enc_dmid, sm_mlp = call(
        enc_mlp_back, "enc_mlp_back",
        [((16, 144, 128), BF16), ((16, 144, 128), BF16), ((LROWS, D), BF16), ((LROWS, D), F32),
         ((48, D), F32)],
        [((LROWS, D), BF16), ((LROWS, D), F32), ((LROWS, D), F32), ((LROWS, FF), BF16),
         ((LROWS, D), BF16)],
        info, *code_parts, diff, post, final, mid, hidden_norm, act, slope, enc_attn, enc_out,
        enc_mlp_in, enc_mlp_out, enc_gains, latent_proj, flops=2_500_000_000, after=[dec_mlp],
    )
    dec_rest, plane_send = call(
        add_all, "sum_rest_core", [((64, 96, 128), BF16)], [], info, rest_keep, rest_other,
        after=[plane_keep], forward=[plane_send],
    )
    rest_parts = scattered(dec_rest.reshape(4, 16, 96, 128), alpha)
    plane_other = swap(plane_send)
    qkv_keep, qkv_send, grad_patches, lat_part = call(
        enc_back, "enc_back",
        [((64, 64, 128), BF16), ((64, 64, 128), BF16), ((ROWS, D), F32), ((LROWS, D), BF16)],
        [((IMGS, OWN_KEYS, LAT), F32), ((OWN_KEYS, GW), BF16), ((OWN_KEYS, GW), BF16),
         ((GW, OWN_KEYS), BF16), ((D, LROWS), F32), ((ROWS, 2 * D), BF16), ((LROWS, 3 * D), BF16),
         ((D, 3 * D), F32), ((ROWS, D), F32), ((SMALL, D), F32)],
        info, enc_da, enc_attn, lse, kv, lqkv, enc_norm, lat_norm, patches, latents, enc_qkv,
        enc_gains, codes, diff, sm_mlp, sm_front, sm_dec, flops=3_000_000_000, after=[dec_rest],
    )

    dec_sum, plane_sum, qkv_send = call(
        join_dec, "join_dec", [((16, 224, 128), BF16), ((16, 144, 128), BF16)], [], info, dec_mlp,
        *rest_parts, plane_keep, plane_other, after=[qkv_keep], forward=[qkv_send],
    )
    dec_parts = scattered(dec_sum.reshape(4, 4, 224, 128), along_by_core("y", "z"))
    plane_parts = scattered(plane_sum.reshape(4, 4, 144, 128), along_by_core("y", "x"))
    both, mains, lasts = 4 * MAIN + 16 * QKV, 4 * MAIN, 16 * MAIN
    main, qkv, *sends = call(
        join_all, "join_all",
        [((mains, 128), BF16), ((16 * QKV, 128), BF16)] + [((both, 128), BF16)] * 3, [], info,
        *dec_parts, *plane_parts, qkv_keep, swap(qkv_send),
    )
    move = along_by_core("x", "y")
    got = [move(send, -by) for by, send in zip((1, 2, 3), sends)]
    both = mains + 4 * QKV
    main, qkv, *sends, lat_part = call(
        join_two, "join_two",
        [((mains, 128), BF16), ((4 * QKV, 128), BF16)] + [((both, 128), BF16)] * 3, [], info,
        main, qkv, *got, forward=[lat_part],
    )
    move = along_by_core("y", "z")
    got = [move(send, -by) for by, send in zip((1, 2, 3), sends)]
    main, qkv, lat_part = call(
        join_three, "join_three",
        [((lasts + 4 * QKV, 128), BF16), ((4 * QKV, 128), BF16), ((LROWS, D), BF16)], [], info,
        main, qkv, *got, lat_part, pair(lat_part, 1),
    )
    last = along_by_core("z", "x")
    one, three, two = last(main, -1), last(main, 1), last(qkv, -2)
    main_far = swap(main)
    qkv, main, one, three, main_far = call(
        join_four, "join_four", [((4 * QKV, 128), BF16)], [], info, qkv, one[lasts:], two,
        three[lasts:], forward=[main, one, three, main_far],
    )
    low, high = last(one[: lasts // 2], -1), last(three[lasts // 2 : lasts], 1)
    near, far = [main, one, three], [main_far, swap(one), swap(three)]
    low, high, qkv, far[1], far[2] = call(
        gate, "gate_halves", [], [], info, forward=[low, high, qkv, far[1], far[2]]
    )
    qkv_parts = others(qkv, move)
    near, far = near + [low, high], far + [swap(low), swap(high)]
    qkv, far[3], far[4], lat_part = call(
        stack, "stack_qkv", [((16 * QKV, 128), BF16)], [], info, *qkv_parts,
        forward=far[3:] + [lat_part],
    )
    lat_other = pair(lat_part, 2)
    qkv_blocks = others(qkv, along_by_core("x", "y"))
    blocks = near + far
    wide = [(D, FF), (FF, D), (D, D), (D, 3 * D), (TABLE, D), (D, FF), (FF, D), (D, D)]
    (dec_in_grad, dec_wout_grad, dec_out_grad, dec_qkv_grad, pos_grad, enc_in_grad, enc_wout_grad,
     enc_out_grad) = call(
        unpack_main, "unpack_main", [(shape, F32) for shape in wide],
        [(shape, F32) for shape in wide] + [pltpu.SemaphoreType.DMA((8,))],
        info, *blocks, hbm_outs=8,
    )
    *qkv_blocks, lat_other = call(
        gate, "gate_qkv", [], [], info, after=[enc_out_grad], forward=qkv_blocks + [lat_other]
    )
    grad_latents = enc_dmid + (lat_part.astype(F32) + lat_other.astype(F32))
    grad_latents = grad_latents.reshape(IMGS, LAT, D)
    qkv_blocks = [*qkv_blocks, *(swap(block) for block in qkv_blocks)]
    small = [(D, 3 * D), (3, D), (6, D), (1, D), (1, FF), (12, D), (1, 128), (1, 128), (12, D),
             (2, D), (8, D), (1, FF), (12, entries)]
    (enc_qkv_grad, gains_grad, biases_grad, query_grad, hidden_grad, proj_grad, pbias_grad, loss,
     embed_grad, dec_gains_grad, dec_biases_grad, dec_hidden_grad, book_grad) = call(
        unpack_qkv, "unpack_qkv", [(shape, F32) for shape in small], [((SMALL, D), F32)],
        info, *qkv_blocks,
    )
    images = IMGS * lax.axis_size(("y", "x", "core"))
    quant_loss = loss[0, 0] / (images * LAT * 12)
    return (
        result.reshape(IMGS, SLOTS, D),
        grad_patches.reshape(IMGS, SLOTS, D),
        grad_latents,
        quant_loss,
        enc_qkv_grad,
        enc_out_grad,
        enc_in_grad,
        enc_wout_grad,
        gains_grad,
        biases_grad,
        query_grad.reshape(D),
        hidden_grad.reshape(FF),
        proj_grad,
        pbias_grad[0, :12],
        book_grad,
        embed_grad,
        pos_grad,
        dec_qkv_grad,
        dec_out_grad,
        dec_in_grad,
        dec_wout_grad,
        dec_gains_grad,
        dec_biases_grad,
        dec_hidden_grad.reshape(FF),
    )


def solution(mesh):
    devices = mesh.devices.reshape(4, 4, 2, 4)
    fine = Mesh(devices, ("y", "x", "core", "z"))
    dp = ("y", "x", "core")
    whole = P()
    images = P(dp, "z", None)
    placed = (images, P(dp, None, None), P(dp), P(dp), P(dp, None)) + (whole,) * 20 + (images,)
    return jax.shard_map(
        per_device,
        mesh=fine,
        in_specs=placed,
        out_specs=(images, images, P(dp, None, None)) + (whole,) * 21,
        check_vma=False,
    )
```

```python
import functools

import jax
import jax.numpy as jnp
from jax import lax
from jax.experimental import pallas as pl
from jax.experimental.pallas import tpu as pltpu
from jax.sharding import Mesh
from jax.sharding import PartitionSpec as P

F32 = jnp.float32
BF16 = jnp.bfloat16
EPS = 1e-06
COMMIT = 0.25
NEG = -1e30
D = 512
HEADS = 8
HD = 64
FF = 2048
GROUP = 4
GW = GROUP * HD
LAT = 128
IMGS = 2
SLOTS = 256
ROWS = IMGS * SLOTS
LROWS = IMGS * LAT
TABLE = 1024
KEYS = TABLE + LAT
OWN_KEYS = SLOTS + LAT
PIECES = 128
SHARE = 0.25
SMALL = 192
CODE_ROW = 64

NN = (((1,), (0,)), ((), ()))
NT = (((1,), (1,)), ((), ()))
TN = (((0,), (0,)), ((), ()))
VMEM_LIMIT = 60 * 1024 * 1024


def dot(left, right, dims=NN):
    return lax.dot_general(left, right, dims, preferred_element_type=F32)


def row_of(ref, index):
    return ref[index : index + 1, :].astype(F32)


def norm_parts(values):
    centre = values - jnp.mean(values, -1, keepdims=True)
    scale = lax.rsqrt(jnp.mean(centre * centre, -1, keepdims=True) + EPS)
    return centre * scale, scale


def norm_rows(values, gain, offset):
    return norm_parts(values)[0] * gain + offset


def norm_back(values, gain, upstream):
    hat, scale = norm_parts(values)
    inner = upstream * gain
    low = jnp.mean(inner, -1, keepdims=True)
    along = jnp.mean(inner * hat, -1, keepdims=True)
    return scale * (inner - low - hat * along), upstream * hat


def fold(values):
    return jnp.sum(values.reshape(values.shape[0] // 8, 8, values.shape[1]), 0)


def col_sum(values):
    return jnp.sum(values, 0, keepdims=True)


def gelu_parts(point):
    size = jnp.abs(point) * 0.7071067811865476
    t = 1.0 / (1.0 + 0.3275911 * size)
    bell = jnp.exp(-0.5 * point * point)
    poly = t * (
        0.254829592
        + t * (-0.284496736 + t * (1.421413741 + t * (-1.453152027 + t * 1.061405429)))
    )
    tail = 0.5 * poly * bell
    cdf = jnp.where(point >= 0, 1.0 - tail, tail)
    return point * cdf, cdf + point * bell * 0.3989422804014327


def loop(count, body, unroll=1):
    def step(index, carry):
        body(index)
        return carry

    lax.fori_loop(0, count, step, 0, unroll=unroll)


def chunk(index, size):
    return pl.ds(pl.multiple_of(index * size, size), size)


def head_stack(block, rows):
    lane = lax.broadcasted_iota(jnp.int32, (rows, GW), 1) // HD
    parts = [jnp.where(lane == h, block, jnp.zeros_like(block)) for h in range(GROUP)]
    return jnp.concatenate(parts, 0)


class Info:
    def __init__(self, lengths, resolution):
        self.lengths, self.resolution = lengths, resolution

    def __getitem__(self, index):
        if isinstance(index, int) and index >= 4:
            return lax.axis_index(("core", "y", "x", "z")[index - 4])
        return self.lengths[index]

    def side(self, image):
        size = self.resolution[image]
        return 3 + jnp.where(size >= 256, 1, 0) + jnp.where(size >= 512, 1, 0)


def coords(info):
    return info[4], info[5], info[6], info[7]


def turn(at, own):
    return (at - own) & 3


def piece_index(info, core, z, y, x):
    c0, y0, x0, z0 = coords(info)
    if z is None:
        return jnp.where(core == 0, turn(y, y0) * 4 + x, turn(x, x0) * 4 + y)
    first = turn(z, z0) * 16 + turn(y, y0) * 4 + x
    second = turn(x, x0) * 16 + turn(z, z0) * 4 + y
    return jnp.where(core == 0, first, second)


def qkv_index(info, core, z, y, x):
    c0, y0, x0, z0 = coords(info)
    first = turn(x, x0) * 16 + turn(y, y0) * 4 + z
    second = turn(y, y0) * 16 + turn(z, z0) * 4 + x
    return jnp.where(core == 0, first, second)


def put_pieces(info, keep, send, offset, z, block, rows, cols, index=piece_index):
    mine_first = info[4] == 0
    for q in range(16):
        y, x = q // 4, q % 4
        own = index(info, info[4], z, y, x)
        away = index(info, 1 - info[4], z, y, x)
        row = (q % 8) * rows
        for b in range(cols // 128):
            col = (q // 8) * cols + b * 128
            at = offset + b * rows
            mine = block[row : row + rows, col : col + 128].astype(BF16)
            col = col + 2 * cols
            other = block[row : row + rows, col : col + 128].astype(BF16)
            keep[own, at : at + rows, :] = jnp.where(mine_first, mine, other)
            send[away, at : at + rows, :] = jnp.where(mine_first, other, mine)


def own_positions(info, image, iota):
    shift = info.side(image)
    side = lax.shift_left(1, shift)
    slot = info[7] * SLOTS + iota
    row = jnp.minimum(lax.shift_right_logical(slot, shift), side - 1)
    col = slot & (side - 1)
    up = lax.shift_right_logical(row * 32, shift)
    across = lax.shift_right_logical(col * 32, shift)
    return up * 32 + across


def table_bias(info, image, shape):
    shift = info.side(image)
    place = lax.broadcasted_iota(jnp.int32, shape, 0)
    gap = 5 - shift
    mask = lax.shift_left(1, gap) - 1
    row = lax.shift_right_logical(place, 5)
    col = place & 31
    slot = lax.shift_left(lax.shift_right_logical(row, gap), shift) + lax.shift_right_logical(
        col, gap
    )
    keep = jnp.logical_and(((row | col) & mask) == 0, slot < info[image])
    return jnp.where(keep, 0.0, NEG)


def code_onehot(codes_ref, entries):
    ids = jnp.concatenate([codes_ref[image : image + 1, :] for image in range(IMGS)], 1)
    entry = lax.broadcasted_iota(jnp.int32, (entries, LROWS), 0)
    return jnp.where(ids == entry, 1.0, 0.0).astype(BF16)


def enc_front(
    info, patches, latents, wqkv, gains, biases, qbias, codes, codebook,
    np_out, nl_out, kv_out, lqkv_out, part_out, quant_out,
    bias_ref, k_ref, vt_ref,
):
    gain, offset = row_of(gains, 0), row_of(biases, 0)
    vbias = row_of(biases, 1)

    def norm_patch(r):
        at = chunk(r, 64)
        np_out[at, :] = norm_rows(patches[at, :].astype(F32), gain, offset).astype(BF16)

    loop(ROWS // 64, norm_patch, 8)

    def norm_lat(r):
        at = chunk(r, 64)
        nl_out[at, :] = norm_rows(latents[at, :].astype(F32), gain, offset).astype(BF16)

    loop(LROWS // 64, norm_lat, 4)
    kv_out[:, :D] = dot(np_out[...], wqkv[:, D : 2 * D]).astype(BF16)
    kv_out[:, D:] = (dot(np_out[...], wqkv[:, 2 * D :]) + vbias).astype(BF16)
    lqkv_out[:, :D] = (dot(nl_out[...], wqkv[:, :D]) + qbias[...].astype(F32).reshape(1, D)).astype(BF16)
    lqkv_out[:, D : 2 * D] = dot(nl_out[...], wqkv[:, D : 2 * D]).astype(BF16)
    lqkv_out[:, 2 * D :] = (dot(nl_out[...], wqkv[:, 2 * D :]) + vbias).astype(BF16)
    quant_out[...] = dot(codebook[...], code_onehot(codes, codebook.shape[1])).astype(BF16)
    enc_bias(info, bias_ref)
    part_out[D:, :] = jnp.zeros((32, LROWS), BF16)
    for image in range(IMGS):
        lat_at = slice(image * LAT, (image + 1) * LAT)
        lane_at = slice(image * LAT, (image + 1) * LAT)
        for g in range(2):
            cols = slice(g * GW, (g + 1) * GW)
            enc_keys(kv_out, lqkv_out, image, g, k_ref, None, vt_ref, None)
            query = lqkv_out[lat_at, cols] * jnp.asarray(0.125, BF16)
            scores = dot(k_ref[...], head_stack(query, LAT), NT)
            bias = bias_ref[image]
            scores = scores + jnp.concatenate([bias] * GROUP, 1)
            top = jnp.max(scores, 0, keepdims=True)
            expo = jnp.exp(scores - top)
            total = col_sum(expo)
            low = expo.astype(BF16)
            log_total = top + jnp.log(total)
            inverse = 1.0 / total
            for h in range(GROUP):
                head = slice(h * LAT, (h + 1) * LAT)
                mixed = dot(vt_ref[h * HD : (h + 1) * HD, :], low[:, head])
                at = g * GW + h * HD
                part_out[at : at + HD, lane_at] = (mixed * inverse[:, head]).astype(BF16)
            rows = jnp.concatenate(
                [log_total[:, h * LAT : (h + 1) * LAT] for h in range(GROUP)], 0
            )
            high = rows.astype(BF16)
            rest = rows - high.astype(F32)
            mid = rest.astype(BF16)
            last = (rest - mid.astype(F32)).astype(BF16)
            for n, piece in enumerate((high, mid, last)):
                at = D + 8 * n + 4 * g
                part_out[at : at + 4, lane_at] = piece


def enc_bias(info, bias_ref):
    place = lax.broadcasted_iota(jnp.int32, (SLOTS, LAT), 0) + info[7] * SLOTS
    token = lax.broadcasted_iota(jnp.int32, (LAT, LAT), 0) // 32
    lat = jnp.where(token == info[7], 0.0, NEG)
    for image in range(IMGS):
        bias_ref[image, :SLOTS, :] = jnp.where(place < info[image], 0.0, NEG)
        bias_ref[image, SLOTS:, :] = lat


def enc_keys(kv, lqkv, image, g, k_ref, v_ref, vt_ref, kt_ref):
    rows = slice(image * SLOTS, (image + 1) * SLOTS)
    lat_at = slice(image * LAT, (image + 1) * LAT)
    k_ref[:SLOTS, :] = kv[rows, g * GW : (g + 1) * GW]
    k_ref[SLOTS:, :] = lqkv[lat_at, D + g * GW : D + (g + 1) * GW]
    value = jnp.concatenate(
        [kv[rows, D + g * GW : D + (g + 1) * GW], lqkv[lat_at, 2 * D + g * GW : 2 * D + (g + 1) * GW]],
        0,
    )
    if v_ref is not None:
        v_ref[...] = value
    if vt_ref is not None:
        vt_ref[...] = value.T
    if kt_ref is not None:
        kt_ref[...] = k_ref[...].T


def dec_front(
    info, wo_hbm, win_hbm, wout_hbm, pos, quant, lemb, wqkv, gains, biases, hbias, cot,
    res_hbm, keep_hbm, send_hbm, dmid_hbm, attn_hbm, tn_hbm, xn_hbm, x_hbm, dbr_hbm,
    ln_out, sm_out, dq_ref, dkv_ref, dkvl_ref, code_out, sm_back,
    res_out, keep_out, send_out, dmid_out, attn_out, tn_out, xn_out, x_out, dbr_ref,
    wo, win, wout, in_sems, out_sems,
    e_out, inv_out, q_out, k_out, v_out,
    bias_ref, vt_ref, ot_ref, mid_ref, hn_ref, dy_ref, acc_ref, dhn_ref, act_ref, dpre_ref,
    da_ref, dqt_ref, dk_ref, dv_ref, dkl_ref, dvl_ref, ds_ref, dn_ref, emb_ref, din_ref,
):
    loads = [
        pltpu.make_async_copy(src, dst, in_sems.at[n])
        for n, (src, dst) in enumerate(((wo_hbm, wo), (win_hbm, win), (wout_hbm, wout)))
    ]
    for load in loads:
        load.start()
    stores = []

    def store(src, dst):
        copy = pltpu.make_async_copy(src, dst, out_sems.at[len(stores)])
        copy.start()
        stores.append(copy)

    gain0, off0 = row_of(gains, 0), row_of(biases, 0)
    gain1, off1 = row_of(gains, 1), row_of(biases, 4)
    qbias, vbias = row_of(biases, 1), row_of(biases, 2)
    token = row_of(biases, 7)

    def table_norm(r):
        at = chunk(r, 64)
        values = token + pos[at, :].astype(F32)
        tn_out[at, :] = norm_rows(values, gain0, off0).astype(BF16)

    loop(TABLE // 64, table_norm, 8)

    def table_keys(r):
        at = chunk(r, 256)
        key = dot(tn_out[at, :], wqkv[:, D : 2 * D]).astype(BF16)
        value = (dot(tn_out[at, :], wqkv[:, 2 * D :]) + vbias).astype(BF16)
        for image in range(IMGS):
            k_out[image, at, :] = key
            v_out[image, at, :] = value

    loop(TABLE // 256, table_keys)
    embed = dot(quant[...], lemb[...], TN) + row_of(biases, 6)
    ln_out[...] = norm_rows(embed, gain0, off0).astype(BF16)
    lat_k = dot(ln_out[...], wqkv[:, D : 2 * D]).astype(BF16)
    lat_v = (dot(ln_out[...], wqkv[:, 2 * D :]) + vbias).astype(BF16)
    for image in range(IMGS):
        at = slice(image * LAT, (image + 1) * LAT)
        k_out[image, TABLE:, :] = lat_k[at, :]
        v_out[image, TABLE:, :] = lat_v[at, :]
        bias_ref[image, :TABLE, :] = table_bias(info, image, (TABLE, LAT))
        bias_ref[image, TABLE:, :] = jnp.zeros((LAT, LAT), F32)
        place = own_positions(info, image, lax.broadcasted_iota(jnp.int32, (SLOTS, 1), 0))
        lane = lax.broadcasted_iota(jnp.int32, (SLOTS, TABLE), 1)
        hot = jnp.where(place == lane, 1.0, 0.0).astype(BF16)
        x_out[image * SLOTS : (image + 1) * SLOTS, :] = dot(hot, pos[...]).astype(BF16)
        for b in range(D // 128):
            cols = slice(b * 128, (b + 1) * 128)
            if image == 0:
                vt_ref[0, cols, :] = v_out[0, :, cols].T
            else:
                vt_ref[image, cols, :TABLE] = vt_ref[0, cols, :TABLE]
                vt_ref[image, cols, TABLE:] = v_out[image, TABLE:, cols].T

    def own_norm(r):
        at = chunk(r, 64)
        values = token + x_out[at, :].astype(F32)
        xn_out[at, :] = norm_rows(values, gain0, off0).astype(BF16)
        slot = lax.broadcasted_iota(jnp.int32, (64, 1), 0) + (r % 4) * 64 + info[7] * SLOTS
        valid = slot < info[r // 4]
        dy_ref[at, :] = jnp.where(valid, cot[at, :], jnp.zeros((64, D), BF16))

    loop(ROWS // 64, own_norm, 8)
    store(tn_out, tn_hbm)
    store(xn_out, xn_hbm)
    store(x_out, x_hbm)
    q_out[...] = (dot(xn_out[...], wqkv[:, :D]) + qbias).astype(BF16)
    ones = jnp.ones((16, KEYS), BF16)

    def attend(t):
        image, g = t // 2, t % 2
        cols = chunk(g, GW)
        keys = k_out[image, :, cols]
        query = q_out[chunk(image, SLOTS), cols] * jnp.asarray(0.125, BF16)
        bias = bias_ref[image]
        bias = jnp.concatenate([bias, bias], 1)
        lane = lax.broadcasted_iota(jnp.int32, (SLOTS, GW), 1) // HD

        def score(h):
            return dot(keys, jnp.where(lane == h, query, jnp.zeros_like(query)), NT) + bias

        def finish(h, low):
            at = pl.ds(pl.multiple_of(g * GW + h * HD, HD), HD)
            mixed = dot(jnp.concatenate([vt_ref[image, at, :], ones], 0), low)
            inverse = 1.0 / mixed[HD : HD + 1, :]
            ot_ref[image, at, :] = mixed[:HD, :] * inverse
            inv_out[t, h : h + 1, :] = inverse

        ahead, low = score(0), None
        for h in range(GROUP):
            scores = ahead
            if h + 1 < GROUP:
                ahead = score(h + 1)
            if low is not None:
                finish(h - 1, low)
            low = jnp.exp(scores - jnp.max(scores, 0, keepdims=True)).astype(BF16)
            e_out[t, :, h * SLOTS : (h + 1) * SLOTS] = low
        finish(GROUP - 1, low)

    loop(4, attend)
    for image in range(IMGS):
        for b in range(D // 128):
            cols = slice(b * 128, (b + 1) * 128)
            attn_out[image * SLOTS : (image + 1) * SLOTS, cols] = (
                ot_ref[image, cols, :].T.astype(BF16)
            )
    store(attn_out, attn_hbm)
    for load in loads:
        load.wait()
    out_bias = row_of(biases, 3)
    mid_ref[...] = dot(attn_out[...], wo[...]) + out_bias

    def mid_norm(r):
        at = chunk(r, 64)
        values = mid_ref[at, :] + (token + x_out[at, :].astype(F32))
        mid_ref[at, :] = values
        hn_ref[at, :] = norm_rows(values, gain1, off1).astype(BF16)

    loop(ROWS // 64, mid_norm, 8)

    def into(j):
        at = slice(j * D, (j + 1) * D)
        act_grad = dot(dy_ref[...], wout[at, :], NT)
        return act_grad, dot(hn_ref[...], win[:, at]) + hbias[at].astype(F32).reshape(1, D)

    def out_of(j):
        at = slice(j * D, (j + 1) * D)
        more = dot(act_ref[j % 2], wout[at, :])
        back = dot(dpre_ref[j % 2], win[:, at], NT)
        if j == 0:
            acc_ref[...] = more
            dhn_ref[...] = back
        else:
            acc_ref[...] += more
            dhn_ref[...] += back
        put_pieces(info, keep_out, send_out, 0, j, dot(hn_ref[...], dpre_ref[j % 2], TN), 64, 128)
        put_pieces(info, keep_out, send_out, 64, j, dot(act_ref[j % 2], dy_ref[...], TN), 64, 128)

    ahead = into(0)
    for j in range(FF // D):
        act_grad, pre = ahead
        if j + 1 < FF // D:
            ahead = into(j + 1)
        if j > 0:
            out_of(j - 1)
        act, slope = gelu_parts(pre)
        act_ref[j % 2] = act.astype(BF16)
        pre_grad = (act_grad * slope).astype(BF16)
        dpre_ref[j % 2] = pre_grad
        sm_out[4 + j : 5 + j, :] = col_sum(pre_grad.astype(F32))
    out_of(FF // D - 1)
    store(keep_out, keep_hbm)
    store(send_out, send_hbm)
    last_bias = row_of(biases, 5)

    def finish(r, carry):
        gain_sum, off_sum, out_sum = carry
        at = chunk(r, 64)
        values = mid_ref[at, :]
        final = values + acc_ref[at, :] + last_bias
        slot = lax.broadcasted_iota(jnp.int32, (64, 1), 0) + (r % 4) * 64 + info[7] * SLOTS
        valid = slot < info[r // 4]
        res_out[at, :] = jnp.where(valid, final, 0.0).astype(BF16)
        upstream = dhn_ref[at, :]
        down, along = norm_back(values, gain1, upstream)
        top = dy_ref[at, :].astype(F32)
        dmid_out[at, :] = top + down
        return gain_sum + fold(along), off_sum + fold(upstream), out_sum + fold(top)

    zero = jnp.zeros((8, D), F32)
    gain_sum, off_sum, out_sum = lax.fori_loop(0, ROWS // 64, finish, (zero, zero, zero), unroll=8)
    sm_out[0:1, :] = col_sum(gain_sum)
    sm_out[1:2, :] = col_sum(off_sum)
    sm_out[2:3, :] = col_sum(out_sum)
    sm_out[3:4, :] = jnp.zeros((1, D), F32)
    store(res_out, res_hbm)
    store(dmid_out, dmid_hbm)
    dec_back(
        dmid_out, attn_out, e_out, inv_out, q_out, k_out, v_out, quant, lemb, wqkv, wo, gains, biases,
        dq_ref, dkv_ref, dkvl_ref, dbr_ref, code_out, sm_back, lambda: store(dbr_ref, dbr_hbm),
        da_ref, dqt_ref, dk_ref, dv_ref, dkl_ref, dvl_ref, vt_ref, ds_ref, dn_ref, emb_ref, din_ref,
    )
    for copy in stores:
        copy.wait()


def dec_back(
    dmid, attn, e_in, inv, q_in, k_in, v_in, quant, lemb, wqkv, wo, gains, biases,
    dq_ref, dkv_ref, dkvl_ref, dbr_ref, code_out, sm_out, branch_done,
    da_ref, dqt_ref, dk_ref, dv_ref, dkl_ref, dvl_ref, kt_ref, ds_ref, dn_ref, emb_ref, din_ref,
):
    gain0 = row_of(gains, 0)

    def branch(r, carry):
        at = chunk(r, 64)
        low = dmid[at, :].astype(BF16)
        dbr_ref[at, :] = low
        return carry + fold(low.astype(F32))

    zero = jnp.zeros((8, D), F32)
    sm_out[3:4, :] = col_sum(lax.fori_loop(0, ROWS // 64, branch, zero, unroll=8))
    branch_done()
    da_ref[...] = dot(dbr_ref[...], wo[...], NT).astype(BF16)
    for image in range(IMGS):
        for b in range(D // 128):
            cols = slice(b * 128, (b + 1) * 128)
            if image == 0:
                kt_ref[0, cols, :] = k_in[0, :, cols].T
            else:
                kt_ref[image, cols, :TABLE] = kt_ref[0, cols, :TABLE]
                kt_ref[image, cols, TABLE:] = k_in[image, TABLE:, cols].T
    dk_ref[...] = jnp.zeros_like(dk_ref)
    dv_ref[...] = jnp.zeros_like(dv_ref)

    def attend(t):
        image, g = t // 2, t % 2
        cols = chunk(g, GW)
        rows = chunk(image, SLOTS)
        out_grad_t = da_ref[rows, cols].astype(F32).T
        out_t = attn[rows, cols].astype(F32).T
        scaled, inner = [], []
        for h in range(GROUP):
            at = slice(h * HD, (h + 1) * HD)
            inverse = inv[t, h : h + 1, :]
            scaled.append(out_grad_t[at, :] * inverse)
            inner.append(col_sum(out_grad_t[at, :] * out_t[at, :]) * inverse)
        out_grad = jnp.concatenate(scaled, 0).T.astype(BF16)
        out_stack = head_stack(out_grad, SLOTS)
        query = q_in[rows, cols] * jnp.asarray(0.125, BF16)
        values = v_in[image, :, cols]

        def prob_grad(h):
            return dot(values, out_stack[h * SLOTS : (h + 1) * SLOTS, :], NT)

        def query_grad(h, low):
            at = pl.ds(pl.multiple_of(g * GW + h * HD, HD), HD)
            dqt_ref[image, at, :] = dot(kt_ref[image, at, :], low)

        ahead, low = prob_grad(0), None
        for h in range(GROUP):
            lanes = slice(h * SLOTS, (h + 1) * SLOTS)
            grads = ahead
            if h + 1 < GROUP:
                ahead = prob_grad(h + 1)
            if low is not None:
                query_grad(h - 1, low)
            low = (e_in[t, :, lanes].astype(F32) * (grads - inner[h])).astype(BF16)
            ds_ref[:, lanes] = low
        query_grad(GROUP - 1, low)
        value_grad = dot(e_in[t], out_stack)
        dv_ref[:, cols] += value_grad[:TABLE, :]
        lat_rows = chunk(image, LAT)
        dvl_ref[lat_rows, cols] = value_grad[TABLE:, :]
        key_grad = dot(ds_ref[...], head_stack(query, SLOTS))
        dk_ref[:, cols] += key_grad[:TABLE, :]
        dkl_ref[lat_rows, cols] = key_grad[TABLE:, :]

    loop(4, attend)
    dkvl_ref[:, :D] = dkl_ref[...].astype(BF16)
    dkvl_ref[:, D:] = dvl_ref[...].astype(BF16)
    dn_ref[...] = dot(dkvl_ref[...], wqkv[:, D:], NT)
    emb_ref[...] = dot(quant[...], lemb[...], TN) + row_of(biases, 6)

    def latent(r, carry):
        gain_sum, off_sum, embed_sum = carry
        at = chunk(r, 64)
        upstream = dn_ref[at, :]
        down, along = norm_back(emb_ref[at, :], gain0, upstream)
        low = down.astype(BF16)
        din_ref[at, :] = low
        return gain_sum + fold(along), off_sum + fold(upstream), embed_sum + fold(low.astype(F32))

    sums = lax.fori_loop(0, LROWS // 64, latent, (zero, zero, zero), unroll=4)
    embed_grad = din_ref[...]
    code_out[...] = dot(lemb[...], embed_grad, NT)
    sm_out[0:1, :] = col_sum(sums[0])
    sm_out[1:2, :] = col_sum(sums[1])
    sm_out[2:3, :] = jnp.zeros((1, D), F32)
    sm_out[6:7, :] = col_sum(sums[2])
    sm_out[7:8, :] = jnp.zeros((1, D), F32)
    sm_out[8:20, :] = dot(quant[...], embed_grad)
    sm_out[20:, :] = jnp.zeros((4, D), F32)
    for image in range(IMGS):
        for b in range(D // 128):
            cols = slice(b * 128, (b + 1) * 128)
            dq_ref[image * SLOTS : (image + 1) * SLOTS, cols] = (
                (dqt_ref[image, cols, :] * 0.125).T.astype(BF16)
            )
    dkv_ref[:, :D] = dk_ref[...].astype(BF16)
    dkv_ref[:, D:] = dv_ref[...].astype(BF16)
    sm_out[4:5, :] = col_sum(fold(dq_ref[...].astype(F32)))
    sm_out[5:6, :] = col_sum(
        fold(dkv_ref[:, D:].astype(F32)) + fold(dkvl_ref[:, D:].astype(F32))
    )


def dec_weights(
    info, dq_ref, dkv_ref, dkvl_ref, dbr_ref, sm_in, dmid, attn, tn, xn, ln, x_in, pos, wqkv,
    gains, biases,
    keep_out, send_out, sm_out,
    w_ref, dn_ref, din_ref, tab_ref,
):
    gain0 = row_of(gains, 0)
    token = row_of(biases, 7)
    zero = jnp.zeros((8, D), F32)
    w_ref[:, :D] = dot(attn[...], dbr_ref[...], TN)
    for z in range(4):
        put_pieces(
            info, keep_out, send_out, 0, z, w_ref[z * 128 : (z + 1) * 128, :D], 16, 128
        )
    w_ref[:, :D] = dot(xn[...], dq_ref[...], TN)
    w_ref[:, D:] = dot(tn[...], dkv_ref[...], TN) + dot(ln[...], dkvl_ref[...], TN)
    for z in range(4):
        put_pieces(
            info, keep_out, send_out, 16, z, w_ref[z * 128 : (z + 1) * 128, :], 16, 384
        )
    dn_ref[:ROWS, :] = dot(dq_ref[...], wqkv[:, :D], NT)

    def own(r, carry):
        gain_sum, off_sum = carry
        at = chunk(r, 64)
        upstream = dn_ref[at, :]
        down, along = norm_back(token + x_in[at, :].astype(F32), gain0, upstream)
        din_ref[at, :] = (dmid[at, :] + down).astype(BF16)
        return gain_sum + fold(along), off_sum + fold(upstream)

    sums = lax.fori_loop(0, ROWS // 64, own, (zero, zero), unroll=8)
    for r in range(4):
        at = slice(r * 256, (r + 1) * 256)
        dn_ref[at, :] = dot(dkv_ref[at, :], wqkv[:, D:], NT)
    lane = lax.broadcasted_iota(jnp.int32, (1, SLOTS), 1)
    place = [own_positions(info, image, lane) for image in range(IMGS)]

    def scatter(r):
        at = chunk(r, 256)
        index = lax.broadcasted_iota(jnp.int32, (256, SLOTS), 0) + r * 256
        total = jnp.zeros((256, D), F32)
        for image in range(IMGS):
            hot = jnp.where(place[image] == index, 1.0, 0.0).astype(BF16)
            total = total + dot(hot, din_ref[image * SLOTS : (image + 1) * SLOTS, :])
        tab_ref[at, :] = total

    loop(4, scatter)

    def table(r, carry):
        gain_sum, off_sum, mask_sum = carry
        at = chunk(r, 64)
        upstream = dn_ref[at, :]
        down, along = norm_back(token + pos[at, :].astype(F32), gain0, upstream)
        rows = tab_ref[at, :] + down
        tab_ref[at, :] = rows
        return gain_sum + fold(along), off_sum + fold(upstream), mask_sum + fold(rows)

    gain_sum, off_sum, mask_sum = lax.fori_loop(0, TABLE // 64, table, sums + (zero,), unroll=8)
    for z in range(4):
        put_pieces(
            info, keep_out, send_out, 64, z, tab_ref[z * 256 : (z + 1) * 256, :], 32, 128
        )
    sm_out[...] = sm_in[...]
    sm_out[0:1, :] = sm_in[0:1, :] + col_sum(gain_sum)
    sm_out[1:2, :] = sm_in[1:2, :] + col_sum(off_sum)
    sm_out[2:3, :] = col_sum(mask_sum)


def enc_mid(
    info, wo_hbm, win_hbm, wout_hbm, parts0, parts1, parts2, parts3, latents, gains, biases, hbias,
    proj, pbias, quant,
    attn_out, mid_out, hn_out, act_out, slope_out, final_out, post_out, diff_out, lse_out,
    wo, win, wout, sems, ot_ref, acc_ref,
):
    loads = [
        pltpu.make_async_copy(src, dst, sems.at[n])
        for n, (src, dst) in enumerate(((wo_hbm, wo), (win_hbm, win), (wout_hbm, wout)))
    ]
    for load in loads:
        load.start()
    logs = []
    for part in (parts0, parts1, parts2, parts3):
        logs.append(
            part[D : D + 8, :].astype(F32)
            + part[D + 8 : D + 16, :].astype(F32)
            + part[D + 16 : D + 24, :].astype(F32)
        )
    top = functools.reduce(jnp.maximum, logs)
    shares = [jnp.exp(rows - top) for rows in logs]
    log_total = top + jnp.log((shares[0] + shares[2]) + (shares[1] + shares[3]))
    lse_out[...] = log_total
    weights = [jnp.exp(rows - log_total) for rows in logs]
    for h in range(HEADS):
        at = slice(h * HD, (h + 1) * HD)
        terms = [
            part[at, :].astype(F32) * weight[h : h + 1, :]
            for part, weight in zip((parts0, parts1, parts2, parts3), weights)
        ]
        ot_ref[at, :] = (terms[0] + terms[2]) + (terms[1] + terms[3])
    for b in range(D // 128):
        cols = slice(b * 128, (b + 1) * 128)
        attn_out[:, cols] = ot_ref[cols, :].T.astype(BF16)
    loads[0].wait()
    acc_ref[...] = dot(attn_out[...], wo[...]) + row_of(biases, 2)
    gain1, off1 = row_of(gains, 1), row_of(biases, 3)
    gain2, off2 = row_of(gains, 2), row_of(biases, 5)

    def mid_norm(r):
        at = chunk(r, 64)
        values = acc_ref[at, :] + latents[at, :].astype(F32)
        mid_out[at, :] = values
        hn_out[at, :] = norm_rows(values, gain1, off1).astype(BF16)
        acc_ref[at, :] = values + row_of(biases, 4)

    loop(LROWS // 64, mid_norm, 4)

    def into(j):
        at = slice(j * D, (j + 1) * D)
        return dot(hn_out[...], win[:, at]) + hbias[at].astype(F32).reshape(1, D)

    loads[1].wait()
    loads[2].wait()
    ahead, total = into(0), acc_ref[...]
    for j in range(FF // D):
        at = slice(j * D, (j + 1) * D)
        pre = ahead
        if j + 1 < FF // D:
            ahead = into(j + 1)
        if j > 0:
            total = total + dot(act_out[:, (j - 1) * D : j * D], wout[(j - 1) * D : j * D, :])
        act, slope = gelu_parts(pre)
        act_out[:, at] = act.astype(BF16)
        slope_out[:, at] = slope
    acc_ref[...] = total + dot(act_out[:, FF - D :], wout[FF - D :, :])

    def post_norm(r):
        at = chunk(r, 64)
        values = acc_ref[at, :]
        final_out[at, :] = values
        post_out[at, :] = norm_rows(values, gain2, off2).astype(BF16)

    loop(LROWS // 64, post_norm, 4)
    same = lax.broadcasted_iota(jnp.int32, (12, 12), 0) == lax.broadcasted_iota(
        jnp.int32, (12, 12), 1
    )
    shift_col = jnp.sum(jnp.where(same, pbias[...].astype(F32).reshape(1, 12), 0.0), -1, keepdims=True)
    code = dot(proj[...], post_out[...], NT) + shift_col
    diff_out[...] = code - quant[...].astype(F32)


def enc_mlp_back(
    info, code0, code1, diff, post, final, mid, hn, act, slope, attn, wo, win, wout, gains, proj,
    keep_out, send_out, da_out, dmid_out, sm_out,
    dy_ref, dn_ref, dfin_ref, dpre_ref, dbr_ref,
):
    zero = jnp.zeros((8, D), F32)
    gain1, gain2 = row_of(gains, 1), row_of(gains, 2)
    code_grad = code0[...] + code1[...] + 2.0 * COMMIT * diff[...]
    low = code_grad.astype(BF16)
    sm_out[16:28, :] = dot(low, post[...]) * SHARE
    sm_out[28:40, :] = jnp.broadcast_to(
        jnp.sum(low.astype(F32), -1, keepdims=True) * SHARE, (12, D)
    )
    loss = (1.0 + COMMIT) * jnp.sum(diff[...] * diff[...]) * SHARE
    sm_out[40:48, :] = jnp.full((8, D), loss, F32)
    dn_ref[...] = dot(low, proj[...], TN)

    def post_back(r, carry):
        gain_sum, off_sum, out_sum = carry
        at = chunk(r, 64)
        upstream = dn_ref[at, :]
        down, along = norm_back(final[at, :], gain2, upstream)
        dfin_ref[at, :] = down
        branch = down.astype(BF16)
        dy_ref[at, :] = branch
        return gain_sum + fold(along), off_sum + fold(upstream), out_sum + fold(branch.astype(F32))

    sums = lax.fori_loop(0, LROWS // 64, post_back, (zero, zero, zero), unroll=4)
    for n in range(3):
        sm_out[n : n + 1, :] = col_sum(sums[n]) * SHARE
    def into(j):
        return dot(dy_ref[...], wout[j * D : (j + 1) * D, :], NT)

    ahead, total = into(0), None
    for j in range(FF // D):
        at = slice(j * D, (j + 1) * D)
        act_grad = ahead
        if j + 1 < FF // D:
            ahead = into(j + 1)
        pre_grad = (act_grad * slope[:, at]).astype(BF16)
        dpre_ref[:, at] = pre_grad
        sm_out[8 + j : 9 + j, :] = col_sum(pre_grad.astype(F32)) * SHARE
        back = dot(pre_grad, win[:, at], NT)
        total = back if j == 0 else total + back
    dn_ref[...] = total
    mine = chunk(info[7], D)
    put_pieces(
        info, keep_out, send_out, 0, None, dot(hn[...], dpre_ref[:, mine], TN), 64, 128
    )
    put_pieces(
        info, keep_out, send_out, 64, None, dot(act[:, mine], dy_ref[...], TN), 64, 128
    )

    def mid_back(r, carry):
        gain_sum, off_sum, out_sum = carry
        at = chunk(r, 64)
        upstream = dn_ref[at, :]
        down, along = norm_back(mid[at, :], gain1, upstream)
        total = dfin_ref[at, :] + down
        dmid_out[at, :] = total
        branch = total.astype(BF16)
        dbr_ref[at, :] = branch
        return gain_sum + fold(along), off_sum + fold(upstream), out_sum + fold(branch.astype(F32))

    sums = lax.fori_loop(0, LROWS // 64, mid_back, (zero, zero, zero), unroll=4)
    for n in range(3):
        sm_out[3 + n : 4 + n, :] = col_sum(sums[n]) * SHARE
    sm_out[6:8, :] = jnp.zeros((2, D), F32)
    sm_out[12:16, :] = jnp.zeros((4, D), F32)
    da_out[...] = dot(dbr_ref[...], wo[...], NT).astype(BF16)
    own = attn[:, chunk(info[7], 128)]
    put_pieces(info, keep_out, send_out, 128, None, dot(own, dbr_ref[...], TN), 16, 128)


def enc_back(
    info, da, attn, lse, kv, lqkv, np_in, nl, patches, latents, wqkv, gains, codes, diff,
    sm_mlp, sm_front, sm_dec,
    keep_out, send_out, patch_out, lat_out,
    bias_ref, k_ref, v_ref, kt_ref, dqt_ref, dkv_ref, dlat_ref, w_ref, dn_ref, sm_ref,
):
    zero = jnp.zeros((8, D), F32)
    gain0 = row_of(gains, 0)
    enc_bias(info, bias_ref)
    for image in range(IMGS):
        rows = slice(image * SLOTS, (image + 1) * SLOTS)
        lat_at = slice(image * LAT, (image + 1) * LAT)
        for g in range(2):
            cols = slice(g * GW, (g + 1) * GW)
            enc_keys(kv, lqkv, image, g, k_ref, v_ref, None, kt_ref)
            query_stack = head_stack(lqkv[lat_at, cols] * jnp.asarray(0.125, BF16), LAT)
            out_grad = da[lat_at, cols]
            out_stack = head_stack(out_grad, LAT)
            grad_t = out_grad.astype(F32).T
            out_t = attn[lat_at, cols].astype(F32).T
            inner = jnp.concatenate(
                [
                    col_sum(grad_t[h * HD : (h + 1) * HD, :] * out_t[h * HD : (h + 1) * HD, :])
                    for h in range(GROUP)
                ],
                1,
            )
            log_total = jnp.concatenate(
                [lse[g * GROUP + h : g * GROUP + h + 1, lat_at] for h in range(GROUP)], 1
            )
            scores = dot(k_ref[...], query_stack, NT)
            bias = jnp.concatenate([bias_ref[image]] * GROUP, 1)
            probs = jnp.exp(scores + bias - log_total)
            prob_grad = dot(v_ref[...], out_stack, NT)
            low = (probs * (prob_grad - inner)).astype(BF16)
            value_grad = dot(probs.astype(BF16), out_stack).astype(BF16)
            key_grad = dot(low, query_stack).astype(BF16)
            dkv_ref[rows, cols] = key_grad[:SLOTS, :]
            dkv_ref[rows, D + g * GW : D + (g + 1) * GW] = value_grad[:SLOTS, :]
            dlat_ref[lat_at, D + g * GW : D + (g + 1) * GW] = key_grad[SLOTS:, :]
            dlat_ref[lat_at, 2 * D + g * GW : 2 * D + (g + 1) * GW] = value_grad[SLOTS:, :]
            for h in range(GROUP):
                part = dot(kt_ref[h * HD : (h + 1) * HD, :], low[:, h * LAT : (h + 1) * LAT])
                at = g * GW + h * HD
                dqt_ref[at : at + HD, lat_at] = part * 0.125
    for b in range(D // 128):
        cols = slice(b * 128, (b + 1) * 128)
        dlat_ref[:, cols] = dqt_ref[cols, :].T.astype(BF16)
    dn_ref[...] = dot(dkv_ref[...], wqkv[:, D:], NT)

    def patch_back(r, carry):
        gain_sum, off_sum = carry
        at = chunk(r, 64)
        upstream = dn_ref[at, :]
        down, along = norm_back(patches[at, :].astype(F32), gain0, upstream)
        patch_out[at, :] = down
        return gain_sum + fold(along), off_sum + fold(upstream)

    sums = lax.fori_loop(0, ROWS // 64, patch_back, (zero, zero), unroll=8)
    dn_ref[:LROWS, :] = dot(dlat_ref[...], wqkv[...], NT)

    def lat_back(r, carry):
        gain_sum, off_sum = carry
        at = chunk(r, 64)
        upstream = dn_ref[at, :]
        down, along = norm_back(latents[at, :].astype(F32), gain0, upstream)
        lat_out[at, :] = down.astype(BF16)
        return gain_sum + fold(along), off_sum + fold(upstream)

    sums = lax.fori_loop(0, LROWS // 64, lat_back, sums, unroll=4)
    w_ref[:, :D] = dot(nl[...], dlat_ref[:, :D], TN)
    w_ref[:, D:] = dot(nl[...], dlat_ref[:, D:], TN) + dot(np_in[...], dkv_ref[...], TN)
    for z in range(4):
        put_pieces(
            info, keep_out, send_out, 0, z, w_ref[z * 128 : (z + 1) * 128, :], 16, 384, qkv_index
        )
    sm_ref[0:1, :] = col_sum(sums[0])
    sm_ref[1:2, :] = sm_mlp[3:4, :]
    sm_ref[2:3, :] = sm_mlp[0:1, :]
    sm_ref[3:4, :] = col_sum(sums[1])
    sm_ref[4:5, :] = col_sum(
        fold(dkv_ref[:, D:].astype(F32)) + fold(dlat_ref[:, 2 * D :].astype(F32))
    )
    sm_ref[5:6, :] = sm_mlp[5:6, :]
    sm_ref[6:7, :] = sm_mlp[4:5, :]
    sm_ref[7:8, :] = sm_mlp[2:3, :]
    sm_ref[8:9, :] = sm_mlp[1:2, :]
    sm_ref[9:10, :] = col_sum(fold(dlat_ref[:, :D].astype(F32)))
    sm_ref[10:14, :] = sm_mlp[8:12, :]
    sm_ref[14:26, :] = sm_mlp[16:28, :]
    pick = lax.broadcasted_iota(jnp.int32, (12, D), 0) == lax.broadcasted_iota(
        jnp.int32, (12, D), 1
    )
    sm_ref[26:27, :] = col_sum(jnp.where(pick, sm_mlp[28:40, :], 0.0))
    sm_ref[27:28, :] = sm_mlp[40:41, :]
    sm_ref[28:40, :] = sm_dec[8:20, :]
    sm_ref[40:41, :] = sm_dec[0:1, :]
    sm_ref[41:42, :] = sm_front[0:1, :]
    sm_ref[42:43, :] = sm_dec[1:2, :]
    sm_ref[43:44, :] = sm_dec[4:5, :]
    sm_ref[44:45, :] = sm_dec[5:6, :]
    sm_ref[45:46, :] = sm_dec[3:4, :]
    sm_ref[46:47, :] = sm_front[1:2, :]
    sm_ref[47:48, :] = sm_front[2:3, :]
    sm_ref[48:49, :] = sm_dec[6:7, :]
    sm_ref[49:50, :] = sm_dec[2:3, :]
    sm_ref[50:54, :] = sm_front[4:8, :]
    sm_ref[54:, :] = jnp.zeros((SMALL - 54, D), F32)
    token = lax.broadcasted_iota(jnp.int32, (12, LROWS), 1) % LAT
    mine = jnp.where(token // 32 == info[7], -2.0 * diff[...], 0.0).astype(BF16)
    book = dot(mine, code_onehot(codes, 8 * D), NT)
    for n in range(8):
        at = CODE_ROW + 16 * n
        sm_ref[at : at + 12, :] = book[:, n * D : (n + 1) * D]
    mine_first = info[4] == 0
    for p in range(PIECES):
        z, q = p // 32, p % 32
        if q >= 16:
            continue
        own = qkv_index(info, info[4], z, q // 4, q % 4)
        away = qkv_index(info, 1 - info[4], z, q // 4, q % 4)
        mine = small_piece(sm_ref, p)
        other = small_piece(sm_ref, p + 16)
        keep_out[own, 48:64, :] = jnp.where(mine_first, mine, other)
        send_out[away, 48:64, :] = jnp.where(mine_first, other, mine)


def small_piece(sm_ref, p):
    if p >= SMALL // 4:
        return jnp.zeros((16, 128), BF16)
    row, col = (p // 4) * 16, (p % 4) * 128
    return sm_ref[row : row + 16, col : col + 128].astype(BF16)


def pair_sum(parts, n):
    values = [part[n].astype(F32) for part in parts]
    if len(values) == 2:
        return (values[0] + values[1]).astype(BF16)
    return ((values[0] + values[2]) + (values[1] + values[3])).astype(BF16)


def add_all(info, *refs):
    *parts, out = refs

    def one(n):
        out[n] = pair_sum(parts, n)

    loop(out.shape[0], one)


def sum_two(info, mlp, mlp_other, code, code_other, out, code_out):
    add_all(info, mlp, mlp_other, out)
    code_out[...] = code[...] + code_other[...]


def join_dec(info, mlp, *refs):
    rest, plane, (dec_out, plane_out) = refs[:4], refs[4:6], refs[6:]

    def one(n):
        dec_out[n, 0:128, :] = mlp[n]
        dec_out[n, 128:224, :] = pair_sum(rest, n)
        plane_out[n] = pair_sum(plane, n)

    loop(16, one)


MAIN = 368
QKV = 64


def join_all(info, *refs):
    dec, plane, qkv = refs[:4], refs[4:8], refs[8:10]
    own_main, own_qkv, *sends = refs[10:]
    fours = 4 * MAIN

    def one(n):
        rows = jnp.concatenate([pair_sum(dec, n), pair_sum(plane, n)], 0)
        at = pl.ds(pl.multiple_of(n * MAIN, 16), MAIN)
        own_main[at, :] = rows
        for send in sends:
            send[at, :] = rows

    loop(4, one)

    def other(n):
        at = pl.ds(pl.multiple_of(n * QKV, 16), QKV)
        own_qkv[at, :] = pair_sum(qkv, n)
        for by in (1, 2, 3):
            after = pl.ds(pl.multiple_of(fours + n * QKV, 16), QKV)
            sends[by - 1][after, :] = pair_sum(qkv, (4 - by) * 16 + n)

    loop(16, other)


def rows_sum(parts, starts, count):
    values = [part[start : start + count, :].astype(F32) for part, start in zip(parts, starts)]
    return ((values[0] + values[2]) + (values[1] + values[3])).astype(BF16)


def join_two(info, own_main, own_qkv, one, two, three, out_main, out_qkv, *sends):
    fours = 4 * MAIN
    got = (one, two, three)
    for n in range(4):
        at = n * MAIN
        rows = rows_sum((own_main,) + got, (at,) * 4, MAIN)
        out_main[at : at + MAIN, :] = rows
        for send in sends:
            send[at : at + MAIN, :] = rows
    for n in range(4):
        at = n * 4 * QKV
        rows = rows_sum((own_qkv,) + got, (at,) + (fours + at,) * 3, 4 * QKV)
        if n == 0:
            out_qkv[...] = rows
        else:
            sends[3 - n][fours:, :] = rows


def join_three(info, own_main, own_qkv, one, two, three, lat, lat_other, out, out_qkv, out_lat):
    fours = 4 * MAIN
    for n, part in enumerate((own_main, one, two, three)):
        out[n * fours : (n + 1) * fours, :] = part[:fours, :]
    rows = rows_sum((own_qkv, one, two, three), (0, fours, fours, fours), 4 * QKV)
    out[4 * fours :, :] = rows
    out_qkv[...] = rows
    out_lat[...] = (lat[...].astype(F32) + lat_other[...].astype(F32)).astype(BF16)


def join_four(info, own, one, two, three, out):
    out[...] = rows_sum((own, one, two, three), (0,) * 4, 4 * QKV)


def gate(info, *refs):
    pass


def stack(info, *refs):
    *parts, out = refs
    rows = parts[0].shape[0]
    for n, part in enumerate(parts):
        out[n * rows : (n + 1) * rows, :] = part[...]


def pieces(info, halves):
    c0, y0, x0, z0 = coords(info)
    steps = (0, 1, 3, 2, 2) if halves else (0, 1, 2, 3)
    count = len(steps)
    for s in range(2 * count):
        core = c0 if s < count else 1 - c0
        first = core == 0
        step = steps[s % count]
        for n in range(8 if s % count >= 3 and halves else 16):
            high, low = (n + (8 if s % count == 4 else 0)) // 4, n % 4
            if halves:
                z = jnp.where(first, z0 + step, z0 + high) & 3
                y = jnp.where(first, (y0 + high) & 3, low)
                x = jnp.where(first, low, (x0 + step) & 3)
            else:
                z = jnp.where(first, low, (z0 + high) & 3)
                y = jnp.where(first, y0 + high, y0 + step) & 3
                x = jnp.where(first, (x0 + step) & 3, low)
            e = (y & 1) * 4 + x
            f = core * 2 + lax.shift_right_logical(y, 1)
            yield s, n, z, e, f, z * 32 + core * 16 + y * 4 + x


def take(src, start, dst, row, col, rows, cols):
    for b in range(cols // 128):
        at = start + b * rows
        lanes = pl.ds(pl.multiple_of(col + b * 128, 128), 128)
        dst[pl.ds(pl.multiple_of(row, 16), rows), lanes] = src[at : at + rows, :].astype(F32)


def z_rows(rows, cols):
    return lambda z, e, f: ((z * 8 + e) * rows, f * cols)


def z_cols(z, e, f):
    return e * 64, z * D + f * 128


def unpack_main(info, *refs):
    src, outs, bufs, sems = refs[:10], refs[10:18], refs[18:26], refs[26]
    plan = (
        (0, z_cols, 64, 128), (64, z_rows(64, 128), 64, 128), (128, z_rows(16, 128), 16, 128),
        (144, z_rows(16, 384), 16, 384), (192, z_rows(32, 128), 32, 128),
        (224, z_cols, 64, 128), (288, z_rows(64, 128), 64, 128), (352, z_rows(16, 128), 16, 128),
    )
    copies = []
    for k, (offset, place, rows, cols) in enumerate(plan):
        for s, n, z, e, f, p in pieces(info, True):
            row, col = place(z, e, f)
            take(src[s], n * MAIN + offset, bufs[k], row, col, rows, cols)
        copy = pltpu.make_async_copy(bufs[k], outs[k], sems.at[k])
        copy.start()
        copies.append(copy)
    for copy in copies:
        copy.wait()


def unpack_qkv(info, *refs):
    src = refs[:8]
    (
        qkv_out, gains_out, biases_out, query_out, hidden_out, proj_out, pbias_out, loss_out,
        embed_out, dgains_out, dbiases_out, dhidden_out, book_out, sm_ref,
    ) = refs[8:]
    place = z_rows(16, 384)
    for s, n, z, e, f, p in pieces(info, False):
        row, col = place(z, e, f)
        take(src[s], n * QKV, qkv_out, row, col, 16, 384)

        def small(s=s, n=n, p=p):
            row = lax.shift_right_logical(p, 2) * 16
            take(src[s], n * QKV + 48, sm_ref, row, (p & 3) * 128, 16, 128)

        pl.when(p < SMALL // 4)(small)
    gains_out[...] = sm_ref[0:3, :]
    biases_out[...] = sm_ref[3:9, :]
    query_out[...] = sm_ref[9:10, :]
    for n in range(4):
        hidden_out[:, n * D : (n + 1) * D] = sm_ref[10 + n : 11 + n, :]
        dhidden_out[:, n * D : (n + 1) * D] = sm_ref[50 + n : 51 + n, :]
    proj_out[...] = sm_ref[14:26, :]
    pbias_out[...] = sm_ref[26:27, :128]
    loss_out[...] = sm_ref[27:28, :128]
    embed_out[...] = sm_ref[28:40, :]
    dgains_out[...] = sm_ref[40:42, :]
    dbiases_out[...] = sm_ref[42:50, :]
    for n in range(8):
        at = CODE_ROW + 16 * n
        book_out[:, n * D : (n + 1) * D] = sm_ref[at : at + 12, :]


def size_of(shape, kind):
    total = jnp.dtype(kind).itemsize
    for n in shape:
        total *= n
    return total


def call(
    kernel, name, outs, scratch, info, *args, flops=0, after=(), forward=(), hbm_outs=0, hbm_args=0,
    spare=8
):
    out_shape = [jax.ShapeDtypeStruct(shape, kind) for shape, kind in outs]
    moved = sum(a.size * a.dtype.itemsize for a in args) + sum(
        o.size * o.dtype.itemsize for o in out_shape
    )
    held = sum(a.size * a.dtype.itemsize for a in args[hbm_args:])
    held += sum(o.size * o.dtype.itemsize for o in out_shape[hbm_outs:])
    held += sum(size_of(*item) for item in scratch if isinstance(item, tuple))
    vmem = pl.BlockSpec(memory_space=pltpu.VMEM)
    anywhere = pl.BlockSpec(memory_space=pl.ANY)
    count, others_in, own_out = 2 + len(args), len(after) + len(forward), len(outs)

    def body(*refs):
        last = count + others_in + own_out
        kernel(
            Info(*refs[:2]),
            *refs[2:count],
            *refs[count + others_in : last],
            *refs[last + len(forward) :],
        )

    first = count + len(after)
    return pl.pallas_call(
        body,
        out_shape=out_shape + [jax.ShapeDtypeStruct(a.shape, a.dtype) for a in forward],
        in_specs=[pl.BlockSpec(memory_space=pltpu.SMEM)] * 2
        + [anywhere] * hbm_args
        + [vmem] * (len(args) - hbm_args)
        + [anywhere] * others_in,
        out_specs=[anywhere] * hbm_outs + [vmem] * (own_out - hbm_outs) + [anywhere] * len(forward),
        scratch_shapes=[
            item if not isinstance(item, tuple) else pltpu.VMEM(*item) for item in scratch
        ],
        input_output_aliases={first + n: own_out + n for n in range(len(forward))},
        compiler_params=pltpu.CompilerParams(
            vmem_limit_bytes=min(VMEM_LIMIT, held + spare * 1024 * 1024)
        ),
        cost_estimate=pl.CostEstimate(flops=flops, bytes_accessed=moved, transcendentals=0),
        name=name,
    )(*info, *args, *after, *forward)


def shift(value, axis, by):
    return lax.ppermute(value, axis, [(i, (i + by) % 4) for i in range(4)])


def shift_by_core(value, axes, by):
    sizes = {"y": 4, "x": 4, "core": 2, "z": 4}
    pairs = []
    for start in range(128):
        at = {"z": start % 4, "core": start // 4 % 2, "x": start // 8 % 4, "y": start // 32}
        to = dict(at)
        axis = axes[at["core"]]
        to[axis] = (to[axis] + by) % sizes[axis]
        pairs.append((start, ((to["y"] * 4 + to["x"]) * 2 + to["core"]) * 4 + to["z"]))
    return lax.ppermute(value, ("y", "x", "core", "z"), pairs)


def swap(value):
    return lax.ppermute(value, "core", [(0, 1), (1, 0)])


def pair(value, bit):
    return lax.ppermute(value, "z", [(i, i ^ bit) for i in range(4)])


def scattered(value, move):
    return [value[0]] + [move(value[by], by) for by in (1, 2, 3)]


def others(value, move):
    return [value] + [move(value, -by) for by in (1, 2, 3)]


def along(axis):
    return lambda value, by: shift(value, axis, by)


def along_by_core(*axes):
    return lambda value, by: shift_by_core(value, axes, by)


def per_device(
    enc_patches, enc_latents, resolution, lengths, codes, enc_qkv, enc_out, enc_mlp_in, enc_mlp_out,
    enc_gains, enc_biases, enc_query_bias, enc_hidden_bias, latent_proj, latent_bias, codebook,
    latent_embed, pos_table, dec_qkv, dec_out, dec_mlp_in, dec_mlp_out, dec_gains, dec_biases,
    dec_hidden_bias, out_cot,
):
    info = (lengths, resolution)
    alpha = along_by_core("z", "x")
    patches = enc_patches.reshape(ROWS, D)
    latents = enc_latents.reshape(LROWS, D)
    cot = out_cot.reshape(ROWS, D)
    entries = codebook.shape[1]

    enc_norm, lat_norm, kv, lqkv, part, quant = call(
        enc_front, "enc_front",
        [((ROWS, D), BF16), ((LROWS, D), BF16), ((ROWS, 2 * D), BF16), ((LROWS, 3 * D), BF16),
         ((D + 32, LROWS), BF16), ((12, LROWS), BF16)],
        [((IMGS, OWN_KEYS, LAT), F32), ((OWN_KEYS, GW), BF16), ((GW, OWN_KEYS), BF16)],
        info, patches, latents, enc_qkv, enc_gains, enc_biases, enc_query_bias,
        codes, codebook, flops=2_000_000_000, spare=60,
    )
    parts = others(part, along("z"))
    early = [((ROWS, D), BF16), ((64, 128, 128), BF16), ((64, 128, 128), BF16), ((ROWS, D), F32),
             ((ROWS, D), BF16), ((TABLE, D), BF16), ((ROWS, D), BF16), ((ROWS, D), BF16),
             ((ROWS, D), BF16)]
    (result, mlp_keep, mlp_send, dmid, attn, tab_norm, own_norm, own_pos, branch, emb_norm,
     sm_front, dq, dkv, dkvl, code_part, sm_back) = call(
        dec_front, "dec_front",
        early + [((LROWS, D), BF16), ((8, D), F32), ((ROWS, D), BF16), ((TABLE, 2 * D), BF16),
                 ((LROWS, 2 * D), BF16), ((12, LROWS), F32), ((24, D), F32)],
        early + [((D, D), BF16), ((D, FF), BF16), ((FF, D), BF16), pltpu.SemaphoreType.DMA((3,)),
                 pltpu.SemaphoreType.DMA((9,)),
         ((4, KEYS, GROUP * SLOTS), BF16), ((4, GROUP, SLOTS), F32), ((ROWS, D), BF16),
         ((IMGS, KEYS, D), BF16), ((IMGS, KEYS, D), BF16),
         ((IMGS, KEYS, LAT), F32), ((IMGS, D, KEYS), BF16), ((IMGS, D, SLOTS), F32),
         ((ROWS, D), F32), ((ROWS, D), BF16), ((ROWS, D), BF16), ((ROWS, D), F32), ((ROWS, D), F32),
         ((2, ROWS, D), BF16), ((2, ROWS, D), BF16),
         ((ROWS, D), BF16), ((IMGS, D, SLOTS), F32), ((TABLE, D), F32), ((TABLE, D), F32),
         ((LROWS, D), F32), ((LROWS, D), F32),
         ((KEYS, GROUP * SLOTS), BF16),
         ((LROWS, D), F32), ((LROWS, D), F32), ((LROWS, D), BF16)],
        info, dec_out, dec_mlp_in, dec_mlp_out, pos_table, quant, latent_embed, dec_qkv, dec_gains,
        dec_biases, dec_hidden_bias, cot, flops=20_000_000_000, spare=60, hbm_args=3, hbm_outs=9,
    )
    mlp_send, code_part = call(
        gate, "gate", [], [], info, after=parts + [sm_back], forward=[mlp_send, code_part]
    )
    mlp_other = swap(mlp_send)
    code_other = pair(code_part, 1)
    enc_attn, mid, hidden_norm, act, slope, final, post, diff, lse = call(
        enc_mid, "enc_mid",
        [((LROWS, D), BF16), ((LROWS, D), F32), ((LROWS, D), BF16), ((LROWS, FF), BF16),
         ((LROWS, FF), F32), ((LROWS, D), F32), ((LROWS, D), BF16), ((12, LROWS), F32),
         ((HEADS, LROWS), F32)],
        [((D, D), BF16), ((D, FF), BF16), ((FF, D), BF16), pltpu.SemaphoreType.DMA((3,)),
         ((D, LROWS), F32), ((LROWS, D), F32)],
        info, enc_out, enc_mlp_in, enc_mlp_out, *parts, latents, enc_gains, enc_biases,
        enc_hidden_bias, latent_proj, latent_bias, quant,
        flops=1_500_000_000, after=[mlp_send], hbm_args=3,
    )
    dec_mlp, code_part = call(
        sum_two, "sum_mlp_core", [((64, 128, 128), BF16), ((12, LROWS), F32)], [], info, mlp_keep,
        mlp_other, code_part, code_other, after=[lse],
    )
    code_other = pair(code_part, 2)
    mlp_parts = scattered(dec_mlp.reshape(4, 16, 128, 128), alpha)
    rest_keep, rest_send, sm_dec = call(
        dec_weights, "dec_weights",
        [((64, 96, 128), BF16), ((64, 96, 128), BF16), ((24, D), F32)],
        [((D, 3 * D), F32), ((TABLE, D), F32), ((ROWS, D), BF16), ((TABLE, D), F32)],
        info, dq, dkv, dkvl, branch, sm_back, dmid, attn, tab_norm, own_norm, emb_norm, own_pos,
        pos_table, dec_qkv, dec_gains, dec_biases, flops=6_000_000_000, after=[dec_mlp],
    )
    dec_mlp, rest_send, code_other = call(
        add_all, "sum_mlp_first", [((16, 128, 128), BF16)], [], info, *mlp_parts, after=[rest_keep],
        forward=[rest_send, code_other],
    )
    rest_other = swap(rest_send)
    plane_keep, plane_send, enc_da, enc_dmid, sm_mlp = call(
        enc_mlp_back, "enc_mlp_back",
        [((16, 144, 128), BF16), ((16, 144, 128), BF16), ((LROWS, D), BF16), ((LROWS, D), F32),
         ((48, D), F32)],
        [((LROWS, D), BF16), ((LROWS, D), F32), ((LROWS, D), F32), ((LROWS, FF), BF16),
         ((LROWS, D), BF16)],
        info, code_part, code_other, diff, post, final, mid, hidden_norm, act, slope, enc_attn, enc_out,
        enc_mlp_in, enc_mlp_out, enc_gains, latent_proj, flops=2_500_000_000, after=[dec_mlp],
    )
    dec_rest, plane_send = call(
        add_all, "sum_rest_core", [((64, 96, 128), BF16)], [], info, rest_keep, rest_other,
        after=[plane_keep], forward=[plane_send],
    )
    rest_parts = scattered(dec_rest.reshape(4, 16, 96, 128), alpha)
    plane_other = swap(plane_send)
    qkv_keep, qkv_send, grad_patches, lat_part = call(
        enc_back, "enc_back",
        [((64, 64, 128), BF16), ((64, 64, 128), BF16), ((ROWS, D), F32), ((LROWS, D), BF16)],
        [((IMGS, OWN_KEYS, LAT), F32), ((OWN_KEYS, GW), BF16), ((OWN_KEYS, GW), BF16),
         ((GW, OWN_KEYS), BF16), ((D, LROWS), F32), ((ROWS, 2 * D), BF16), ((LROWS, 3 * D), BF16),
         ((D, 3 * D), F32), ((ROWS, D), F32), ((SMALL, D), F32)],
        info, enc_da, enc_attn, lse, kv, lqkv, enc_norm, lat_norm, patches, latents, enc_qkv,
        enc_gains, codes, diff, sm_mlp, sm_front, sm_dec, flops=3_000_000_000, after=[dec_rest],
    )

    dec_sum, plane_sum, qkv_send = call(
        join_dec, "join_dec", [((16, 224, 128), BF16), ((16, 144, 128), BF16)], [], info, dec_mlp,
        *rest_parts, plane_keep, plane_other, after=[qkv_keep], forward=[qkv_send],
    )
    dec_parts = scattered(dec_sum.reshape(4, 4, 224, 128), along_by_core("y", "z"))
    plane_parts = scattered(plane_sum.reshape(4, 4, 144, 128), along_by_core("y", "x"))
    both, mains, lasts = 4 * MAIN + 16 * QKV, 4 * MAIN, 16 * MAIN
    main, qkv, *sends = call(
        join_all, "join_all",
        [((mains, 128), BF16), ((16 * QKV, 128), BF16)] + [((both, 128), BF16)] * 3, [], info,
        *dec_parts, *plane_parts, qkv_keep, swap(qkv_send),
    )
    move = along_by_core("x", "y")
    got = [move(send, -by) for by, send in zip((1, 2, 3), sends)]
    both = mains + 4 * QKV
    main, qkv, *sends, lat_part = call(
        join_two, "join_two",
        [((mains, 128), BF16), ((4 * QKV, 128), BF16)] + [((both, 128), BF16)] * 3, [], info,
        main, qkv, *got, forward=[lat_part],
    )
    move = along_by_core("y", "z")
    got = [move(send, -by) for by, send in zip((1, 2, 3), sends)]
    main, qkv, lat_part = call(
        join_three, "join_three",
        [((lasts + 4 * QKV, 128), BF16), ((4 * QKV, 128), BF16), ((LROWS, D), BF16)], [], info,
        main, qkv, *got, lat_part, pair(lat_part, 1),
    )
    last = along_by_core("z", "x")
    one, three, two = last(main, -1), last(main, 1), last(qkv, -2)
    main_far = swap(main)
    qkv, main, one, three, main_far = call(
        join_four, "join_four", [((4 * QKV, 128), BF16)], [], info, qkv, one[lasts:], two,
        three[lasts:], forward=[main, one, three, main_far],
    )
    low, high = last(one[: lasts // 2], -1), last(three[lasts // 2 : lasts], 1)
    near, far = [main, one, three], [main_far, swap(one), swap(three)]
    low, high, qkv, far[1], far[2] = call(
        gate, "gate_halves", [], [], info, forward=[low, high, qkv, far[1], far[2]]
    )
    qkv_parts = others(qkv, move)
    near, far = near + [low, high], far + [swap(low), swap(high)]
    qkv, far[3], far[4], lat_part = call(
        stack, "stack_qkv", [((16 * QKV, 128), BF16)], [], info, *qkv_parts,
        forward=far[3:] + [lat_part],
    )
    lat_other = pair(lat_part, 2)
    qkv_blocks = others(qkv, along_by_core("x", "y"))
    blocks = near + far
    wide = [(D, FF), (FF, D), (D, D), (D, 3 * D), (TABLE, D), (D, FF), (FF, D), (D, D)]
    (dec_in_grad, dec_wout_grad, dec_out_grad, dec_qkv_grad, pos_grad, enc_in_grad, enc_wout_grad,
     enc_out_grad) = call(
        unpack_main, "unpack_main", [(shape, F32) for shape in wide],
        [(shape, F32) for shape in wide] + [pltpu.SemaphoreType.DMA((8,))],
        info, *blocks, hbm_outs=8,
    )
    *qkv_blocks, lat_other = call(
        gate, "gate_qkv", [], [], info, after=[enc_out_grad], forward=qkv_blocks + [lat_other]
    )
    grad_latents = enc_dmid + (lat_part.astype(F32) + lat_other.astype(F32))
    grad_latents = grad_latents.reshape(IMGS, LAT, D)
    qkv_blocks = [*qkv_blocks, *(swap(block) for block in qkv_blocks)]
    small = [(D, 3 * D), (3, D), (6, D), (1, D), (1, FF), (12, D), (1, 128), (1, 128), (12, D),
             (2, D), (8, D), (1, FF), (12, entries)]
    (enc_qkv_grad, gains_grad, biases_grad, query_grad, hidden_grad, proj_grad, pbias_grad, loss,
     embed_grad, dec_gains_grad, dec_biases_grad, dec_hidden_grad, book_grad) = call(
        unpack_qkv, "unpack_qkv", [(shape, F32) for shape in small], [((SMALL, D), F32)],
        info, *qkv_blocks,
    )
    images = IMGS * lax.axis_size(("y", "x", "core"))
    quant_loss = loss[0, 0] / (images * LAT * 12)
    return (
        result.reshape(IMGS, SLOTS, D),
        grad_patches.reshape(IMGS, SLOTS, D),
        grad_latents,
        quant_loss,
        enc_qkv_grad,
        enc_out_grad,
        enc_in_grad,
        enc_wout_grad,
        gains_grad,
        biases_grad,
        query_grad.reshape(D),
        hidden_grad.reshape(FF),
        proj_grad,
        pbias_grad[0, :12],
        book_grad,
        embed_grad,
        pos_grad,
        dec_qkv_grad,
        dec_out_grad,
        dec_in_grad,
        dec_wout_grad,
        dec_gains_grad,
        dec_biases_grad,
        dec_hidden_grad.reshape(FF),
    )


def solution(mesh):
    devices = mesh.devices.reshape(4, 4, 2, 4)
    fine = Mesh(devices, ("y", "x", "core", "z"))
    dp = ("y", "x", "core")
    whole = P()
    images = P(dp, "z", None)
    placed = (images, P(dp, None, None), P(dp), P(dp), P(dp, None)) + (whole,) * 20 + (images,)
    return jax.shard_map(
        per_device,
        mesh=fine,
        in_specs=placed,
        out_specs=(images, images, P(dp, None, None)) + (whole,) * 21,
        check_vma=False,
    )
```
